32 devices in a mesh: batch: 8 (over y, x, core), seq: 4 (over z).
Axes of the slice: x: 2, y: 2, z: 4, core: 2. Of those that a mesh axis runs over, the one named last changes fastest.
Arguments:
- inputs: bfloat16 [16, 1024, 1024], P('batch', 'seq'), may hold values from -6 to 6
- skip_input: bfloat16 [16, 1024, 1024], P('batch', 'seq'), may hold values from -6 to 6
- lengths: int32 [16], P('batch'), may hold values from 128 to 1024, as said below
- skip_weight: bfloat16 [2048, 1024], P('batch', 'seq'), may hold values from -0.125 to 0.125
- query_weight: bfloat16 [1024, 1024], P('batch', 'seq'), may hold values from -0.1875 to 0.1875
- key_weight: bfloat16 [1024, 1024], P('batch', 'seq'), may hold values from -0.1875 to 0.1875
- value_weight: bfloat16 [1024, 1024], P('batch', 'seq'), may hold values from -0.1875 to 0.1875
- out_weight: bfloat16 [1024, 1024], P('seq', 'batch'), may hold values from -0.75 to 0.75
- up_weight: bfloat16 [1024, 4096], P('batch', 'seq'), may hold values from -0.1875 to 0.1875
- down_weight: bfloat16 [4096, 1024], P('seq', 'batch'), may hold values from -0.09375 to 0.09375
- first_gain: bfloat16 [1024], P('seq'), may hold values from 0.25 to 1.75
- first_shift: bfloat16 [1024], P('seq'), may hold values from -3 to 3
- second_gain: bfloat16 [1024], P('seq'), may hold values from 0.25 to 1.75
- second_shift: bfloat16 [1024], P('seq'), may hold values from -3 to 3
- cotangent: bfloat16 [16, 1024, 1024], P('batch', 'seq'), may hold values from -6 to 6
Outputs:
- output: bfloat16 [16, 1024, 1024], P('batch', 'seq')
- input_grad: float32 [16, 1024, 1024], P('batch', 'seq')
- skip_grad: float32 [16, 1024, 1024], P('batch', 'seq')
- skip_weight_grad: float32 [2048, 1024], P('batch', 'seq')
- query_weight_grad: float32 [1024, 1024], P('batch', 'seq')
- key_weight_grad: float32 [1024, 1024], P('batch', 'seq')
- value_weight_grad: float32 [1024, 1024], P('batch', 'seq')
- out_weight_grad: float32 [1024, 1024], P('seq', 'batch')
- up_weight_grad: float32 [1024, 4096], P('batch', 'seq')
- down_weight_grad: float32 [4096, 1024], P('seq', 'batch')
- first_gain_grad: float32 [1024], P('seq')
- first_shift_grad: float32 [1024], P('seq')
- second_gain_grad: float32 [1024], P('seq')
- second_shift_grad: float32 [1024], P('seq')
The draws below stay inside these ranges and needn't reach their ends.
Inputs may be any that keep to these rules, and one draw needn't show every extreme that they name: `lengths`: the utterances of one batch group are 2 consecutive rows; in every group at least one of them, drawn from the seed, has exactly 1024 frames.
All inputs are finite; a program needn't handle non-finite values.
Results may differ from the reference program's by a relative error of at most 0.02.
Values may be sent and summed in bfloat16 or wider, within the bound.
A program may use at most 192 MiB of HBM per device.

```python
import jax
import jax.numpy as jnp
from jax import lax

D = 1024
HEADS = 16
HEAD_DIM = 64
FF = 4096
ITEMS = 2
FRAMES = 1024
UTTERANCES = 16
N_BATCH = 8


def draw_lengths(key, part):
    key = jax.random.fold_in(key, 11)
    length_key, choice_key = jax.random.split(key)
    groups = UTTERANCES // ITEMS
    random_lengths = jax.random.randint(length_key, (groups, ITEMS), FRAMES // 8, FRAMES + 1)
    chosen = jax.random.randint(choice_key, (groups, 1), 0, ITEMS)
    slot_ids = jnp.arange(ITEMS)[None, :]
    return jnp.where(slot_ids == chosen, FRAMES, random_lengths).reshape(UTTERANCES).astype(jnp.int32)


def raised(array, rng, source, target, blocks, factor):
    owner, partner = [(jnp.arange(array.shape[dim]) // (array.shape[dim] // blocks)).reshape([-1 if axis == dim else 1 for axis in range(array.ndim)]) for dim in (source, target)]
    chosen = jax.random.permutation(rng, blocks)[partner]
    strong = (owner == chosen) | (owner == (partner + blocks // 2) % blocks)
    return jnp.where(strong, factor * array, array)


def steps_of(own_key, extent, cuts, least, high):
    def one(position, blocks):
        heights = jax.random.uniform(jax.random.fold_in(jax.random.fold_in(own_key, 6), position), (blocks,), jnp.float32, least / len(cuts), high / len(cuts))
        return jnp.repeat(jnp.exp(heights), extent[position] // blocks).reshape((-1,) + (1,) * (len(extent) - position - 1))

    level = one(*cuts[0])
    for cut in cuts[1:]:
        level = level * one(*cut)
    return level


def bell_draw(stream_key, shape, scale, bound, pieces=(), held_as=jnp.bfloat16):
    level = steps_of(stream_key, shape, pieces, -0.22, 0.18) if pieces else 1.0
    values = jax.random.normal(stream_key, shape, jnp.float32) * scale * level
    return jnp.minimum(jnp.maximum(values, -bound), bound).astype(held_as)


def bell_draw_with(key, extent, width, bound, cuts, heavy, dtype=jnp.bfloat16):
    drawn = width * jax.random.normal(key, extent, jnp.float32)
    if cuts:
        drawn = drawn * steps_of(key, extent, cuts, -0.22, 0.18)
    return jnp.clip(raised(drawn, jax.random.fold_in(key, 3), *heavy), -bound, bound).astype(dtype)


def setup_inputs(seed: int = 0) -> dict:
    arg_keys = jax.random.split(jax.random.key(seed), 16)
    inputs = bell_draw_with(arg_keys[0], (UTTERANCES, FRAMES, D), 1.0, 6.0, ((0, 8), (1, 4)), (0, 2, 8, 2.0))
    skip_input = bell_draw(arg_keys[1], (UTTERANCES, FRAMES, D), 1.0, 6.0, ((0, 8), (1, 4)))
    lengths = draw_lengths(jax.random.fold_in(arg_keys[15], 71), 0)
    skip_weight = bell_draw(arg_keys[3], (2 * D, D), (2 * D) ** -0.5, 0.125, ((0, 8), (1, 4)))
    query_weight = bell_draw(arg_keys[4], (D, D), D ** -0.5, 0.1875, ((0, 8), (1, 4)))
    key_weight = bell_draw(arg_keys[5], (D, D), D ** -0.5, 0.1875, ((0, 8), (1, 4)))
    value_weight = bell_draw(arg_keys[6], (D, D), D ** -0.5, 0.1875, ((0, 8), (1, 4)))
    out_weight = bell_draw(arg_keys[7], (D, D), (D // 16) ** -0.5, 0.75, ((0, 4), (1, 8)))
    up_weight = bell_draw(arg_keys[8], (D, FF), D ** -0.5, 0.1875, ((0, 8), (1, 4)))
    down_weight = bell_draw(arg_keys[9], (FF, D), FF ** -0.5, 0.09375, ((0, 4), (1, 8)))
    first_gain = jnp.clip(1.0 + 0.15 * jax.random.normal(arg_keys[10], (D,), jnp.float32), 0.25, 1.75).astype(jnp.bfloat16)
    first_shift = bell_draw(arg_keys[11], (D,), 0.3, 3.0, ((0, 4),))
    second_gain = jnp.clip(1.0 + 0.15 * jax.random.normal(arg_keys[12], (D,), jnp.float32), 0.25, 1.75).astype(jnp.bfloat16)
    second_shift = bell_draw(arg_keys[13], (D,), 0.3, 3.0, ((0, 4),))
    cotangent = bell_draw(arg_keys[14], (UTTERANCES, FRAMES, D), 1.0, 6.0, ((0, 8), (1, 4)))
    return {"inputs": inputs, "skip_input": skip_input, "lengths": lengths, "skip_weight": skip_weight, "query_weight": query_weight, "key_weight": key_weight, "value_weight": value_weight, "out_weight": out_weight, "up_weight": up_weight, "down_weight": down_weight, "first_gain": first_gain, "first_shift": first_shift, "second_gain": second_gain, "second_shift": second_shift, "cotangent": cotangent}


EPSILON = 1e-05
HIGHEST = lax.Precision.HIGHEST

@jax.custom_vjp
def low(v):
    return lax.optimization_barrier(v.astype(jnp.bfloat16)).astype(jnp.float32)

@jax.custom_vjp
def low_back(v):
    return v

def low_keep(v):
    return (low(v), None)

def low_pass(kept, grad):
    return (grad,)

def back_keep(v):
    return (v, None)

def back_low(kept, grad):
    return (low(grad),)
low.defvjp(low_keep, low_pass)
low_back.defvjp(back_keep, back_low)

def layer_norm(values, norm_gain, norm_shift):
    average = lax.optimization_barrier(jnp.mean(values, -1, keepdims=True))
    centred = values - average
    spread = lax.optimization_barrier(jnp.mean(centred * centred, -1, keepdims=True))
    return centred * lax.rsqrt(spread + EPSILON) * norm_gain + norm_shift

def project(values, weight):
    return jnp.einsum('itd,de->ite', values, weight, precision=HIGHEST)

def attention(queries, key_heads, values, key_valid, slopes):
    frames = queries.shape[1]
    block_rows = min(512, frames)
    score_scale = queries.shape[3] ** (-0.5)
    key_pos = jnp.arange(frames).astype(jnp.float32)

    def one_block(block_index):
        first_row = (block_index * block_rows).astype(jnp.int32)
        query_block = lax.dynamic_slice_in_dim(queries, first_row, block_rows, 1)
        query_pos = (first_row + jnp.arange(block_rows).astype(jnp.int32)).astype(jnp.float32)
        products = jnp.einsum('iqhd,ikhd->ihqk', query_block, key_heads, precision=HIGHEST) * score_scale
        distance = jnp.abs(query_pos[:, None] - key_pos[None, :])
        scores = low_back(products - slopes[None, :, None, None] * distance[None, None])
        scores = jnp.where(key_valid[:, None, None, :], scores, -1e+30)
        highest = lax.optimization_barrier(jnp.max(scores, -1, keepdims=True))
        weights = jnp.exp(scores - highest)
        probabilities = low(weights / lax.optimization_barrier(jnp.sum(weights, -1, keepdims=True)))
        return jnp.einsum('ihqk,ikhd->iqhd', probabilities, values, precision=HIGHEST)
    block_outputs = lax.map(jax.checkpoint(one_block), jnp.arange(frames // block_rows))
    item_count = queries.shape[0]
    return jnp.moveaxis(block_outputs, 0, 1).reshape(queries.shape[0], frames, queries.shape[2], queries.shape[3])

def forward(layer_in, skip_in, weights, key_valid, slopes):
    skip_w, query_w, key_w, value_w, out_w, up_w, down_w, gain_one, shift_one, gain_two, shift_two = weights
    item_count, frames, model_width = layer_in.shape
    head_shape = (item_count, frames, HEADS, HEAD_DIM)
    mixed_stream = low_back(project(jnp.concatenate([layer_in, skip_in], -1), skip_w))
    normed = low(layer_norm(mixed_stream, gain_one, shift_one))
    queries = low_back(low(project(normed, query_w))).reshape(head_shape)
    key_heads = low_back(low(project(normed, key_w))).reshape(head_shape)
    values = low_back(low(project(normed, value_w))).reshape(head_shape)
    attended = attention(queries, key_heads, values, key_valid, slopes).reshape(item_count, frames, model_width)
    attended = low_back(low(attended))
    middle = mixed_stream + low_back(project(attended, out_w))
    ffn_input = low(layer_norm(middle, gain_two, shift_two))
    hidden = low_back(project(ffn_input, up_w))
    active = low(jax.nn.gelu(hidden, approximate=False))
    return middle + low_back(project(active, down_w))

def reference(inputs, skip_input, lengths, skip_weight, query_weight, key_weight, value_weight, out_weight, up_weight, down_weight, first_gain, first_shift, second_gain, second_shift, cotangent):
    params = tuple((weight.astype(jnp.float32) for weight in (skip_weight, query_weight, key_weight, value_weight, out_weight, up_weight, down_weight, first_gain, first_shift, second_gain, second_shift)))
    slopes = 2.0 ** (-8.0 * (jnp.arange(HEADS) + 1).astype(jnp.float32) / HEADS)
    group_shape = (N_BATCH, ITEMS, FRAMES, D)
    grouped = (inputs.astype(jnp.float32).reshape(group_shape), skip_input.astype(jnp.float32).reshape(group_shape), lengths.reshape(N_BATCH, ITEMS), cotangent.astype(jnp.float32).reshape(group_shape))

    def group_step(totals, group_data):
        group_inputs, group_skip, group_lengths, group_cot = group_data
        key_valid = jnp.arange(FRAMES)[None, :] < group_lengths[:, None]

        def layer_run(layer_in, skip_in, weights):
            return forward(layer_in, skip_in, weights, key_valid, slopes)
        result, pullback = jax.vjp(layer_run, group_inputs, group_skip, params)
        group_input_grad, group_skip_grad, weight_grads = pullback(group_cot)
        totals = jax.tree.map(jnp.add, totals, weight_grads)
        return (totals, (result.astype(jnp.bfloat16), group_input_grad, group_skip_grad))
    totals, stacked = lax.scan(group_step, jax.tree.map(jnp.zeros_like, params), grouped)
    full_shape = (UTTERANCES, FRAMES, D)
    return (stacked[0].reshape(full_shape), stacked[1].reshape(full_shape), stacked[2].reshape(full_shape), totals[0], totals[1], totals[2], totals[3], totals[4], totals[5], totals[6], totals[7], totals[8], totals[9], totals[10])
```

```python
import functools
import jax
import jax.numpy as jnp
from jax import lax
from jax.experimental import pallas as pl
from jax.experimental.pallas import tpu as pltpu

from jax.sharding import PartitionSpec as P

MESH = pl.DeviceIdType.MESH
F32 = jnp.float32
BF16 = jnp.bfloat16


def flip(index, mask):
    result = index
    bit = 0
    while mask >> bit:
        if (mask >> bit) & 1:
            on = lax.rem(lax.div(index, 1 << bit), 2)
            result = result + (1 << bit) * (1 - 2 * on)
        bit += 1
    return result


def span(bits):
    masks = [0]
    for bit in bits:
        masks = masks + [m | (1 << bit) for m in masks]
    return masks


class Place:
    def __init__(self, nb, nz):
        self.nb, self.nz = nb, nz
        self.b = lax.axis_index("batch")
        self.z = lax.axis_index("seq")
        count = nb.bit_length() - 1
        rest = list(range(1, count))
        self.rest = rest
        self.orders = (rest, rest[::-1])

    def at(self, mask):
        return (flip(self.b, mask), self.z)

    def greet(self, barrier):
        targets = [self.at(1 << k) for k in [0] + self.rest]
        for t in targets:
            pl.semaphore_signal(barrier, inc=1, device_id=t, device_id_type=MESH)
        for step, ok in ((1, self.z < self.nz - 1), (-1, self.z > 0)):
            @pl.when(ok)
            def _():
                pl.semaphore_signal(
                    barrier, inc=1, device_id=(self.b, self.z + step), device_id_type=MESH
                )
        ends = jnp.where(self.z < self.nz - 1, 1, 0) + jnp.where(self.z > 0, 1, 0)
        pl.semaphore_wait(barrier, len(targets) + ends)


def remote(src, dst, send, recv, device):
    return pltpu.make_async_remote_copy(
        src_ref=src, dst_ref=dst, send_sem=send, recv_sem=recv, device_id=device, device_id_type=MESH
    )


class Gather:
    @staticmethod
    def sems(nb, nz):
        count = nb.bit_length() - 1
        return 2 * (nz - 1) + 2 * (nb // 2 - 1) + nb

    def __init__(self, place, shard, full, local, send, recv):
        self.p, self.shard, self.full = place, shard, full
        self.local, self.send, self.recv = local, send, recv
        self.r, self.c = shard.shape
        nb, nz = place.nb, place.nz
        self.xy0 = 2 * (nz - 1)
        self.core0 = self.xy0 + 2 * (nb // 2 - 1)
        self.stages = nz + len(place.rest) + 1
        self.pending = []

    def zcopy(self, way, step):
        p = self.p
        n = p.nz
        sem = (0 if way > 0 else n - 1) + step - 1
        sent = p.z - way * (step - 1)
        got = p.z - way * step
        inside = lambda v: (v >= 0) & (v < n)
        can_send = inside(sent) & inside(p.z + way)
        can_get = inside(got)
        clip = lambda v: jnp.clip(v, 0, n - 1)
        block = self.full.at[p.b, :, pl.ds(pl.multiple_of(clip(sent) * self.c, self.c), self.c)]
        src = self.shard if step == 1 else block
        out = remote(src, block, self.send.at[sem], self.recv.at[sem], (p.b, clip(p.z + way)))
        land = self.full.at[p.b, :, pl.ds(pl.multiple_of(clip(got) * self.c, self.c), self.c)]
        into = remote(self.shard, land, self.send.at[sem], self.recv.at[sem], (p.b, clip(p.z + way)))
        return out, into, can_send, can_get

    def zstart(self, step):
        for way in (1, -1):
            out, _, can_send, _ = self.zcopy(way, step)
            pl.when(can_send)(out.start)
            self.pending.append((out, can_send))

    def zwait(self, step):
        for way in (1, -1):
            _, into, _, can_get = self.zcopy(way, step)
            pl.when(can_get)(into.wait_recv)

    def rows(self, mask, half):
        return self.full.at[flip(self.p.b, mask), pl.ds(half * (self.r // 2), self.r // 2)]

    def xycopies(self, j):
        p = self.p
        made = []
        for half in (0, 1):
            order = p.orders[half]
            bit = 1 << order[j]
            for i, m in enumerate(span(order[:j])):
                sem = self.xy0 + half * (p.nb // 2 - 1) + (1 << j) - 1 + i
                made.append((half, m | bit, remote(
                    self.rows(m, half), self.rows(m, half), self.send.at[sem], self.recv.at[sem], p.at(bit)
                ), remote(
                    self.rows(m | bit, half), self.rows(m | bit, half), self.send.at[sem], self.recv.at[sem], p.at(bit)
                )))
        return made

    def corecopy(self, mask, half):
        p = self.p
        sem = self.core0 + (mask >> 1) * 2 + half
        out = remote(self.rows(mask, half), self.rows(mask, half), self.send.at[sem], self.recv.at[sem], p.at(1))
        into = remote(self.rows(mask | 1, half), self.rows(mask | 1, half), self.send.at[sem], self.recv.at[sem], p.at(1))
        return out, into

    def corestart(self, mask, half):
        out, _ = self.corecopy(mask, half)
        out.start()
        self.pending.append((out, None))

    def stage(self, t):
        p = self.p
        n = p.nz
        nx = len(p.rest)
        if t == 0:
            mine = self.full.at[p.b, :, pl.ds(pl.multiple_of(p.z * self.c, self.c), self.c)]
            self.own = pltpu.make_async_copy(self.shard, mine, self.local)
            self.own.start()
            if n > 1:
                self.zstart(1)
        if 1 <= t <= n - 1:
            self.zwait(t)
            if t < n - 1:
                self.zstart(t + 1)
        if t == max(n - 1, 0):
            self.own.wait()
        j = t - (n - 1)
        if j >= 1 and j <= nx:
            for half, m, _, into in self.xycopies(j - 1):
                into.wait_recv()
        if 0 <= j < nx:
            for _, _, out, _ in self.xycopies(j):
                out.start()
                self.pending.append((out, None))
        if j == 0:
            for half in (0, 1):
                self.corestart(0, half)
        if 1 <= j <= nx:
            for half, m, _, _ in self.xycopies(j - 1):
                self.corestart(m, half)
        if j == nx + 1:
            for m in span(p.rest):
                for half in (0, 1):
                    self.corecopy(m, half)[1].wait_recv()
            for out, ok in self.pending:
                if ok is None:
                    out.wait_send()
                else:
                    pl.when(ok)(out.wait_send)


def gather_kernel(nb, nz, count, lag, *refs):
    shards, fulls = refs[:count], refs[count:2 * count]
    local, sends, recvs = refs[2 * count], refs[2 * count + 1:3 * count + 1], refs[3 * count + 1:]
    place = Place(nb, nz)
    place.greet(pltpu.get_barrier_semaphore())
    jobs = [Gather(place, shards[i], fulls[i], local.at[i], sends[i], recvs[i]) for i in range(count)]
    total = max(lag[i] + jobs[i].stages for i in range(count))
    for slot in range(total):
        for i, job in enumerate(jobs):
            if 0 <= slot - lag[i] < job.stages:
                job.stage(slot - lag[i])


def gather_all(nb, nz, shards, lag, collective_id):
    count = len(shards)
    sems = Gather.sems(nb, nz)
    return pl.pallas_call(
        functools.partial(gather_kernel, nb, nz, count, lag),
        out_shape=[jax.ShapeDtypeStruct((nb, s.shape[0], nz * s.shape[1]), BF16) for s in shards],
        in_specs=[pl.BlockSpec(memory_space=pl.ANY)] * count,
        out_specs=[pl.BlockSpec(memory_space=pl.ANY)] * count,
        scratch_shapes=[pltpu.SemaphoreType.DMA((count,))]
        + [pltpu.SemaphoreType.DMA((sems,))] * (2 * count),
        compiler_params=pltpu.CompilerParams(collective_id=collective_id, has_side_effects=True),
    )(*shards)


class Scatter:
    @staticmethod
    def sems(nb, nz):
        return nb // 2 + 2 * (nb // 2 - 1) + 2 * (nz - 1)

    @staticmethod
    def scratch(nb, nz, r, wide):
        c = wide // nz
        return [
            pltpu.VMEM((nb // 2, r, wide), BF16),
            pltpu.VMEM((nb // 2, r, wide), BF16),
            pltpu.VMEM((2 * (nb // 2 - 1), r // 2, wide), BF16),
            pltpu.VMEM((2 * (nz - 1), r, c), BF16),
            pltpu.SemaphoreType.DMA((nb // 2,)),
            pltpu.SemaphoreType.DMA((Scatter.sems(nb, nz),)),
            pltpu.SemaphoreType.DMA((Scatter.sems(nb, nz),)),
        ]

    def __init__(self, place, full, share, scratch):
        self.p, self.full, self.share = place, full, share
        self.sums, self.core, self.plane, self.line, self.local, self.send, self.recv = scratch
        _, self.r, self.wide = full.shape
        self.c = self.wide // place.nz
        self.stages = 1 + 1 + len(place.rest) + (place.nz - 1) + 1
        self.pending = []

    def start(self, copy, ok=None):
        if ok is None:
            copy.start()
        else:
            pl.when(ok)(copy.start)
        self.pending.append((copy, ok))

    def add(self, target, *sources):
        rows = target.shape[0]
        step = 16
        def body(i, carry):
            at = pl.ds(pl.multiple_of(i * step, step), step)
            value = target[at].astype(F32)
            for s in sources:
                value = value + s[at].astype(F32)
            target[at] = value.astype(target.dtype)
            return carry
        lax.fori_loop(0, rows // step, body, 0)

    def corecopy(self, i, m):
        p = self.p
        return remote(self.full.at[flip(p.b, m | 1)], self.core.at[i], self.send.at[i], self.recv.at[i], p.at(1))

    def planecopies(self, j):
        p = self.p
        made = []
        for half in (0, 1):
            order = p.orders[half]
            bit = 1 << order[j]
            at = pl.ds(half * (self.r // 2), self.r // 2)
            base = half * (p.nb // 2 - 1)
            for jj in range(j):
                base += len(span(order[jj + 1:]))
            for i, m in enumerate(span(order[j + 1:])):
                slot = base + i
                sem = p.nb // 2 + slot
                made.append((half, m, slot, remote(
                    self.sums.at[(m | bit) >> 1, at], self.plane.at[slot], self.send.at[sem], self.recv.at[sem], p.at(bit)
                )))
        return made

    def linecopy(self, way, step):
        p = self.p
        n = p.nz
        here = p.z if way > 0 else n - 1 - p.z
        goes = n + here - step
        comes = goes - 1
        can_send = (goes > here) & (goes <= n - 1)
        can_get = (comes >= here) & (comes <= n - 1) & (here > 0)
        unfold = lambda d: jnp.clip(d if way > 0 else n - 1 - d, 0, n - 1)
        slot = (0 if way > 0 else n - 1) + step - 1
        sem = p.nb // 2 + 2 * (p.nb // 2 - 1) + slot
        src = self.sums.at[0, :, pl.ds(pl.multiple_of(unfold(goes) * self.c, self.c), self.c)]
        copy = remote(src, self.line.at[slot], self.send.at[sem], self.recv.at[sem], (p.b, jnp.clip(p.z + way, 0, n - 1)))
        return copy, can_send, can_get, unfold(comes), slot

    def stage(self, t):
        p = self.p
        n, nx = p.nz, len(p.rest)
        masks = sorted(span(p.rest))
        if t == 0:
            for i, m in enumerate(masks):
                self.start(self.corecopy(i, m))
            self.loads = [pltpu.make_async_copy(self.full.at[flip(p.b, m)], self.sums.at[i], self.local.at[i]) for i, m in enumerate(masks)]
            for load in self.loads:
                load.start()
        if t == 1:
            for i, m in enumerate(masks):
                self.loads[i].wait()
                self.corecopy(i, m).wait_recv()
                self.add(self.sums.at[i], self.core.at[i])
        j = t - 1
        if 1 <= j <= nx:
            for half, m, slot, copy in self.planecopies(j - 1):
                copy.wait_recv()
                self.add(self.sums.at[m >> 1, pl.ds(half * (self.r // 2), self.r // 2)], self.plane.at[slot])
        if 0 <= j < nx:
            for half, m, slot, copy in self.planecopies(j):
                self.start(copy)
        s = t - 1 - nx
        if 1 <= s <= n - 1:
            for way in (1, -1):
                copy, can_send, can_get, place, slot = self.linecopy(way, s)
                @pl.when(can_get)
                def _():
                    copy.wait_recv()
                    if s < n - 1:
                        self.add(self.sums.at[0, :, pl.ds(pl.multiple_of(place * self.c, self.c), self.c)], self.line.at[slot])
        if 0 <= s < n - 1:
            for way in (1, -1):
                copy, can_send, can_get, place, slot = self.linecopy(way, s + 1)
                self.start(copy, can_send)
        if t == self.stages - 1:
            self.finish()

    def finish(self):
        p = self.p
        n = p.nz
        mine = pl.ds(pl.multiple_of(p.z * self.c, self.c), self.c)
        step = 16
        def body(i, carry):
            at = pl.ds(pl.multiple_of(i * step, step), step)
            self.share[at] = self.sums[0, at, mine].astype(F32)
            return carry
        lax.fori_loop(0, self.r // step, body, 0)
        for way, ok in ((1, p.z > 0), (-1, p.z < n - 1)):
            slot = (0 if way > 0 else n - 1) + n - 2
            @pl.when(ok)
            def _():
                def more(i, carry):
                    at = pl.ds(pl.multiple_of(i * step, step), step)
                    self.share[at] = self.share[at] + self.line[slot, at].astype(F32)
                    return carry
                lax.fori_loop(0, self.r // step, more, 0)
        for copy, ok in self.pending:
            if ok is None:
                copy.wait_send()
            else:
                pl.when(ok)(copy.wait_send)


def scatter_kernel(nb, nz, count, lag, *refs):
    fulls, shares = refs[:count], refs[count:2 * count]
    scratch = refs[2 * count:]
    per = len(scratch) // count
    place = Place(nb, nz)
    place.greet(pltpu.get_barrier_semaphore())
    jobs = [Scatter(place, fulls[i], shares[i], scratch[i * per:(i + 1) * per]) for i in range(count)]
    total = max(lag[i] + jobs[i].stages for i in range(count))
    for slot in range(total):
        for i, job in enumerate(jobs):
            if 0 <= slot - lag[i] < job.stages:
                job.stage(slot - lag[i])


def scatter_all(nb, nz, fulls, lag, collective_id):
    count = len(fulls)
    scratch = []
    for f in fulls:
        scratch += Scatter.scratch(nb, nz, f.shape[1], f.shape[2])
    return pl.pallas_call(
        functools.partial(scatter_kernel, nb, nz, count, lag),
        out_shape=[jax.ShapeDtypeStruct((f.shape[1], f.shape[2] // nz), F32) for f in fulls],
        in_specs=[pl.BlockSpec(memory_space=pl.ANY)] * count,
        out_specs=[pl.BlockSpec(memory_space=pltpu.VMEM)] * count,
        scratch_shapes=scratch,
        compiler_params=pltpu.CompilerParams(
            collective_id=collective_id, has_side_effects=True, vmem_limit_bytes=60 * 2**20
        ),
    )(*fulls)


HEADS = 16
HEAD_DIM = 64


EPSILON = 1e-05


def layer_norm(values, norm_gain, norm_shift):
    average = jnp.mean(values, -1, keepdims=True)
    centred = values - average
    spread = jnp.mean(centred * centred, -1, keepdims=True)
    return centred * lax.rsqrt(spread + EPSILON) * norm_gain + norm_shift


def gelu_exact(values):
    return jax.nn.gelu(values, approximate=False)


def block_scores(queries, key_heads, key_valid, slopes, first_row, block_rows):
    query_block = lax.dynamic_slice_in_dim(queries, first_row, block_rows, 1)
    score_scale = queries.shape[3] ** (-0.5)
    products = (
        jnp.einsum("iqhd,ikhd->ihqk", query_block, key_heads, preferred_element_type=jnp.float32)
        * score_scale
    )
    query_pos = (first_row + jnp.arange(block_rows)).astype(jnp.float32)
    key_pos = jnp.arange(key_heads.shape[1]).astype(jnp.float32)
    distance = jnp.abs(query_pos[:, None] - key_pos[None, :])
    scores = products - slopes[None, :, None, None] * distance[None, None]
    return (jnp.where(key_valid[:, None, None, :], scores, -1e30), query_block)


def shards(
    inputs,
    skip_input,
    lengths,
    skip_weight,
    query_weight,
    key_weight,
    value_weight,
    out_weight,
    up_weight,
    down_weight,
    first_gain,
    first_shift,
    second_gain,
    second_shift,
    cotangent,
):
    gain_one, shift_one, gain_two, shift_two = (
        lax.all_gather(jnp.stack([first_gain, first_shift, second_gain, second_shift]), "seq", axis=1, tiled=True)
    )
    nb, nz = lax.axis_size("batch"), lax.axis_size("seq")
    mix_shard = jnp.concatenate([query_weight, key_weight, value_weight, out_weight.T], 1)
    skip_full, mix_full, up_full, down_t = gather_all(
        nb, nz, [skip_weight, mix_shard, up_weight, down_weight.T], (0, 2, 4, 6), 0
    )
    flat = lambda w: w.reshape(w.shape[0] * w.shape[1], w.shape[2])
    skip_full, up_full, down_t = flat(skip_full), flat(up_full), flat(down_t)
    width = query_weight.shape[1]
    split = flat(mix_full).reshape(-1, nz, 4, width)
    pick = lambda i: split[:, :, i].reshape(-1, nz * width)
    query_full, key_full, value_full, out_t = lax.optimization_barrier((pick(0), pick(1), pick(2), pick(3)))
    gain_first = gain_one.astype(jnp.float32)
    shift_first = shift_one.astype(jnp.float32)
    gain_second = gain_two.astype(jnp.float32)
    shift_second = shift_two.astype(jnp.float32)
    joined = jnp.concatenate([inputs, skip_input], -1)
    mixed_stream = jnp.einsum("ifc,cd->ifd", joined, skip_full, preferred_element_type=jnp.float32)
    normed = layer_norm(mixed_stream, gain_first, shift_first).astype(jnp.bfloat16)
    stacked = jnp.stack([query_full, key_full, value_full])
    projected = jnp.einsum(
        "ifd,cde->ifce", normed, stacked, preferred_element_type=jnp.float32
    ).astype(jnp.bfloat16)
    heads_view = lax.all_to_all(projected, "seq", split_axis=3, concat_axis=1, tiled=True)
    item_count = heads_view.shape[0]
    frames = heads_view.shape[1]
    local_width = heads_view.shape[3]
    local_heads = local_width // HEAD_DIM
    head_shape = (item_count, frames, local_heads, HEAD_DIM)
    queries = heads_view[:, :, 0].reshape(head_shape)
    key_heads = heads_view[:, :, 1].reshape(head_shape)
    values = heads_view[:, :, 2].reshape(head_shape)
    head_numbers = lax.axis_index("seq") * local_heads + jnp.arange(local_heads)
    slopes = 2.0 ** (-8.0 * (head_numbers + 1).astype(jnp.float32) / HEADS)
    key_valid = jnp.arange(frames)[None, :] < lengths[:, None]
    block_rows = min(512, frames)
    block_count = frames // block_rows
    score_scale = HEAD_DIM ** (-0.5)

    def forward_block(block_index):
        scores, query_block = block_scores(
            queries, key_heads, key_valid, slopes, block_index * block_rows, block_rows
        )
        highest = jnp.max(scores, -1, keepdims=True)
        weights = jnp.exp(scores - highest)
        row_total = jnp.sum(weights, -1, keepdims=True)
        weights_low = (weights / row_total).astype(jnp.bfloat16)
        block_out = jnp.einsum(
            "ihqk,ikhd->iqhd", weights_low, values, preferred_element_type=jnp.float32
        ).astype(jnp.bfloat16)
        return (block_out, (highest + jnp.log(row_total))[..., 0])

    block_outputs, logsum = lax.map(forward_block, jnp.arange(block_count))
    attended = jnp.moveaxis(block_outputs, 0, 1).reshape(item_count, frames, local_width)
    attended_frames = lax.optimization_barrier(lax.all_to_all(attended, "seq", split_axis=1, concat_axis=2, tiled=True))
    middle = mixed_stream + jnp.einsum(
        "ifd,ed->ife", attended_frames, out_t, preferred_element_type=jnp.float32
    )
    ffn_input = layer_norm(middle, gain_second, shift_second).astype(jnp.bfloat16)
    hidden = jnp.einsum("ifd,dk->ifk", ffn_input, up_full, preferred_element_type=jnp.float32)
    active = gelu_exact(hidden).astype(jnp.bfloat16)
    output = (
        middle + jnp.einsum("ifk,dk->ifd", active, down_t, preferred_element_type=jnp.float32)
    ).astype(jnp.bfloat16)
    down_grad = jnp.einsum("ifd,ifk->dk", cotangent, active, preferred_element_type=jnp.float32)
    active_grad = jnp.einsum(
        "ifd,dk->ifk", cotangent, down_t, preferred_element_type=jnp.float32
    )
    hidden_grad = jax.vjp(gelu_exact, hidden)[1](active_grad)[0].astype(jnp.bfloat16)
    up_grad = jnp.einsum("ifd,ifk->dk", ffn_input, hidden_grad, preferred_element_type=jnp.float32)
    ffn_input_grad = jnp.einsum(
        "ifk,dk->ifd", hidden_grad, up_full, preferred_element_type=jnp.float32
    )
    second_pull = jax.vjp(layer_norm, middle, gain_second, shift_second)[1]
    middle_part, gain_second_grad, shift_second_grad = second_pull(ffn_input_grad)
    middle_grad = cotangent.astype(jnp.float32) + middle_part
    middle_low = middle_grad.astype(jnp.bfloat16)
    out_grad = jnp.einsum(
        "ifd,ife->ed", attended_frames, middle_low, preferred_element_type=jnp.float32
    )
    attended_grad = lax.optimization_barrier(jnp.einsum(
        "ife,ed->ifd", middle_low, out_t, preferred_element_type=jnp.float32
    ).astype(jnp.bfloat16))
    heads_grad = lax.all_to_all(
        attended_grad, "seq", split_axis=2, concat_axis=1, tiled=True
    ).reshape(head_shape)

    def backward_block(running, block_data):
        key_grad, value_grad = running
        block_index, block_logsum = block_data
        first_row = block_index * block_rows
        scores, query_block = block_scores(
            queries, key_heads, key_valid, slopes, first_row, block_rows
        )
        out_block_grad = lax.dynamic_slice_in_dim(heads_grad, first_row, block_rows, 1)
        probabilities = jnp.exp(scores - block_logsum[..., None])
        weights_low = probabilities.astype(jnp.bfloat16)
        value_grad = value_grad + jnp.einsum(
            "ihqk,iqhd->ikhd", weights_low, out_block_grad, preferred_element_type=jnp.float32
        )
        prob_grad = jnp.einsum(
            "iqhd,ikhd->ihqk", out_block_grad, values, preferred_element_type=jnp.float32
        )
        inner_sum = jnp.sum(prob_grad * probabilities, -1, keepdims=True)
        score_grad = (probabilities * (prob_grad - inner_sum)).astype(jnp.bfloat16)
        query_block_grad = (
            jnp.einsum("ihqk,ikhd->iqhd", score_grad, key_heads, preferred_element_type=jnp.float32)
            * score_scale
        ).astype(jnp.bfloat16)
        key_grad = (
            key_grad
            + jnp.einsum(
                "ihqk,iqhd->ikhd", score_grad, query_block, preferred_element_type=jnp.float32
            )
            * score_scale
        )
        return ((key_grad, value_grad), query_block_grad)

    empty_grad = jnp.zeros(head_shape, jnp.float32)
    (key_grad, value_grad), query_blocks = lax.scan(
        backward_block, (empty_grad, empty_grad), (jnp.arange(block_count), logsum)
    )
    query_grad = jnp.moveaxis(query_blocks, 0, 1).reshape(item_count, frames, local_width)
    key_grad_low = key_grad.reshape(item_count, frames, local_width).astype(jnp.bfloat16)
    value_grad_low = value_grad.reshape(item_count, frames, local_width).astype(jnp.bfloat16)
    grads_heads = jnp.stack([query_grad, key_grad_low, value_grad_low], 2)
    grads_frames = lax.optimization_barrier(lax.all_to_all(grads_heads, "seq", split_axis=1, concat_axis=3, tiled=True))
    qkv_grad = jnp.einsum("ifd,ifce->cde", normed, grads_frames, preferred_element_type=jnp.float32)
    normed_grad = jnp.einsum(
        "ifce,cde->ifd", grads_frames, stacked, preferred_element_type=jnp.float32
    )
    first_pull = jax.vjp(layer_norm, mixed_stream, gain_first, shift_first)[1]
    mixed_part, gain_first_grad, shift_first_grad = first_pull(normed_grad)
    mixed_low = (middle_grad + mixed_part).astype(jnp.bfloat16)
    skip_w_grad = jnp.einsum("ifc,ifd->cd", joined, mixed_low, preferred_element_type=jnp.float32)
    joined_grad = jnp.einsum(
        "ifd,cd->ifc", mixed_low, skip_full, preferred_element_type=jnp.float32
    )
    model_width = mixed_stream.shape[2]
    input_grad = joined_grad[:, :, :model_width]
    skip_grad = joined_grad[:, :, model_width:]
    mix_grad = jnp.concatenate([qkv_grad, out_grad[None]], 0)
    mix_grad = mix_grad.reshape(4, -1, nz, width).transpose(1, 2, 0, 3).reshape(-1, nz * 4 * width)
    blocked = lambda g: g.astype(jnp.bfloat16).reshape(nb, g.shape[0] // nb, g.shape[1])
    down_share, up_share, mix_share, skip_share = scatter_all(
        nb, nz, [blocked(down_grad), blocked(up_grad), blocked(mix_grad), blocked(skip_w_grad)], (0, 1, 2, 3), 1
    )
    down_share = down_share.T
    query_share, key_share, value_share, out_share = [
        mix_share[:, i * width : (i + 1) * width] for i in range(4)
    ]
    out_share = out_share.T
    norm_grads = jnp.stack([gain_first_grad, shift_first_grad, gain_second_grad, shift_second_grad])
    norm_grads = lax.psum(norm_grads, ("batch", "seq"))
    gain_one_grad, shift_one_grad, gain_two_grad, shift_two_grad = lax.dynamic_slice_in_dim(
        norm_grads, lax.axis_index("seq") * width, width, 1
    )
    return (
        output,
        input_grad,
        skip_grad,
        skip_share,
        query_share,
        key_share,
        value_share,
        out_share,
        up_share,
        down_share,
        gain_one_grad,
        shift_one_grad,
        gain_two_grad,
        shift_two_grad,
    )


def solution(mesh):
    in_specs = (
        P("batch", "seq", None),
        P("batch", "seq", None),
        P("batch"),
        P("batch", "seq"),
        P("batch", "seq"),
        P("batch", "seq"),
        P("batch", "seq"),
        P("seq", "batch"),
        P("batch", "seq"),
        P("seq", "batch"),
        P("seq"),
        P("seq"),
        P("seq"),
        P("seq"),
        P("batch", "seq", None),
    )
    out_specs = (
        P("batch", "seq", None),
        P("batch", "seq", None),
        P("batch", "seq", None),
        P("batch", "seq"),
        P("batch", "seq"),
        P("batch", "seq"),
        P("batch", "seq"),
        P("seq", "batch"),
        P("batch", "seq"),
        P("seq", "batch"),
        P("seq"),
        P("seq"),
        P("seq"),
        P("seq"),
    )
    return jax.shard_map(shards, mesh=mesh, in_specs=in_specs, out_specs=out_specs, check_vma=False)
```

```python
import functools

import jax
import jax.numpy as jnp
from jax import lax
from jax.experimental import pallas as pl
from jax.experimental.pallas import tpu as pltpu
from jax.sharding import PartitionSpec as P

HEADS = 16
HEAD_DIM = 64
EPSILON = 1e-05
LOG2E = 1.4426950408889634
QUERIES = 256
F32 = jnp.float32
BF16 = jnp.bfloat16
MESH = pl.DeviceIdType.MESH
VMEM_LIMIT = 60 * 2**20
ANY = pl.BlockSpec(memory_space=pl.ANY)
WHOLE = pl.BlockSpec(memory_space=pltpu.VMEM)


def nt(a, b):
    return lax.dot_general(a, b, (((1,), (1,)), ((), ())), preferred_element_type=F32)


def nn(a, b):
    return jnp.dot(a, b, preferred_element_type=F32)


def part(index, size):
    if isinstance(index, int):
        return pl.ds(index * size, size)
    return pl.ds(pl.multiple_of(index * size, size), size)


def rowwise(rows, step, body):
    def run(i, carry):
        body(part(i, step))
        return carry

    lax.fori_loop(0, rows // step, run, 0)


def flip(index, mask):
    result = index
    bit = 0
    while mask >> bit:
        if (mask >> bit) & 1:
            on = lax.rem(lax.div(index, 1 << bit), 2)
            result = result + (1 << bit) * (1 - 2 * on)
        bit += 1
    return result


def span(bits):
    masks = [0]
    for bit in bits:
        masks = masks + [m | (1 << bit) for m in masks]
    return masks


class Place:
    def __init__(self, nb, nz):
        self.nb, self.nz = nb, nz
        self.b = lax.axis_index("batch")
        self.z = lax.axis_index("seq")
        self.half = nz // 2
        self.group = lax.div(self.z, self.half)
        self.k = lax.rem(self.z, self.half)
        self.partner = lax.rem(self.z + self.half, nz)
        self.rest = list(range(1, nb.bit_length() - 1))
        self.orders = (self.rest, self.rest[::-1])
        self.pending = []

    def at(self, mask):
        return (flip(self.b, mask), self.z)

    def mate(self, r):
        return self.group * self.half + lax.rem(self.k + r, self.half)

    def greet(self):
        barrier = pltpu.get_barrier_semaphore()
        targets = [self.at(1 << k) for k in [0] + self.rest]
        targets += [(self.b, lax.rem(self.z + r, self.nz)) for r in range(1, self.nz)]
        for t in targets:
            pl.semaphore_signal(barrier, inc=1, device_id=t, device_id_type=MESH)
        pl.semaphore_wait(barrier, len(targets))

    def start(self, make, *args):
        copy, ok = self.unpack(make(*args))
        if ok is None:
            copy.start()
        else:
            pl.when(ok)(lambda: copy.start())
        self.pending.append((make, args))

    def drain(self):
        for make, args in self.pending:
            copy, ok = self.unpack(make(*args))
            if ok is None:
                copy.wait_send()
            else:
                pl.when(ok)(lambda copy=copy: copy.wait_send())
        self.pending = []

    @staticmethod
    def unpack(made):
        return made if isinstance(made, tuple) else (made, None)


def remote(src, dst, send, recv, device):
    return pltpu.make_async_remote_copy(
        src_ref=src, dst_ref=dst, send_sem=send, recv_sem=recv, device_id=device, device_id_type=MESH
    )


class Gather:
    @staticmethod
    def sems(nb, nz):
        return 2 * (nz - 1) + 2 * (nb // 2 - 1) + nb

    @staticmethod
    def scratch(nb, nz):
        count = Gather.sems(nb, nz)
        return [pltpu.SemaphoreType.DMA] + [pltpu.SemaphoreType.DMA((count,))] * 2

    def __init__(self, place, shard, full, scratch, paired=False):
        self.p, self.shard, self.full, self.paired = place, shard, full, paired
        self.local, self.send, self.recv = scratch
        self.r, self.c = shard.shape
        nb, nz = place.nb, place.nz
        self.xy0 = 2 * (nz - 1)
        self.core0 = self.xy0 + 2 * (nb // 2 - 1)
        self.zsteps = 1 if paired else nz - 1
        self.stages = self.zsteps + len(place.rest) + 2

    def column(self, index):
        return self.full.at[part(self.p.b, self.r), part(index, self.c)]

    def line(self, way, step):
        p, n = self.p, self.p.nz
        sem = (0 if way > 0 else n - 1) + step - 1
        sent, got = p.z - way * (step - 1), p.z - way * step
        inside = lambda v: (v >= 0) & (v < n)
        clip = lambda v: jnp.clip(v, 0, n - 1)
        to = (p.b, clip(p.z + way))
        block = self.column(clip(sent))
        out = lambda: remote(self.shard if step == 1 else block, block, self.send.at[sem], self.recv.at[sem], to)
        land = self.column(clip(got))
        into = lambda: remote(land, land, self.send.at[sem], self.recv.at[sem], to)
        return out, into, inside(sent) & inside(p.z + way), inside(got)

    def zstart(self, step):
        p = self.p
        if self.paired:
            for t in (0, 1):
                p.start(self.paircopy, t)
            return
        for way in (1, -1):
            p.start(self.lineout, way, step)

    def lineout(self, way, step):
        out, _, can_send, _ = self.line(way, step)
        return out(), can_send

    def paircopy(self, t):
        p = self.p
        target = lax.div(p.z, 2) + t * p.half
        slot = lax.rem(p.z, 2)
        copy = remote(self.shard, self.column(slot), self.send.at[t], self.recv.at[slot], (p.b, target))
        return copy, target != p.z

    def zwait(self, step):
        p = self.p
        if self.paired:
            for s in (0, 1):
                land = self.column(s)
                copy = remote(land, land, self.send.at[s], self.recv.at[s], (p.b, p.partner))
                pl.when(2 * p.k + s != p.z)(lambda copy=copy: copy.wait_recv())
            return
        for way in (1, -1):
            _, into, _, can_get = self.line(way, step)
            pl.when(can_get)(lambda into=into: into().wait_recv())

    def owncopy(self):
        p = self.p
        if self.paired:
            mine = (2 * p.k == p.z) | (2 * p.k + 1 == p.z)
            return pltpu.make_async_copy(self.shard, self.column(lax.rem(p.z, 2)), self.local), mine
        return pltpu.make_async_copy(self.shard, self.column(p.z), self.local), None

    def rows(self, mask, half):
        h = self.r // 2
        return self.full.at[part(flip(self.p.b, mask) * 2 + half, h)]

    def hop(self, sem, mask, half, bit, incoming):
        block = self.rows(mask | bit if incoming else mask, half)
        return remote(block, block, self.send.at[sem], self.recv.at[sem], self.p.at(bit))

    def plane(self, j):
        made = []
        for half in (0, 1):
            order = self.p.orders[half]
            for i, m in enumerate(span(order[:j])):
                sem = self.xy0 + half * (self.p.nb // 2 - 1) + (1 << j) - 1 + i
                made.append((half, m, 1 << order[j], sem))
        return made

    def coresem(self, mask, half):
        return self.core0 + (mask >> 1) * 2 + half

    def corestart(self, mask, half):
        self.p.start(self.hop, self.coresem(mask, half), mask, half, 1, False)

    def stage(self, t):
        p = self.p
        nx = len(p.rest)
        if t == 0:
            own, mine = self.owncopy()
            if mine is None:
                own.start()
            else:
                pl.when(mine)(lambda: own.start())
            self.zstart(1)
        if 1 <= t <= self.zsteps:
            self.zwait(t)
            if t < self.zsteps:
                self.zstart(t + 1)
            else:
                own, mine = self.owncopy()
                if mine is None:
                    own.wait()
                else:
                    pl.when(mine)(lambda: own.wait())
        j = t - self.zsteps
        if 1 <= j <= nx:
            for half, m, bit, sem in self.plane(j - 1):
                self.hop(sem, m, half, bit, True).wait_recv()
        if 0 <= j < nx:
            for half, m, bit, sem in self.plane(j):
                p.start(self.hop, sem, m, half, bit, False)
        if j == 0:
            for half in (0, 1):
                self.corestart(0, half)
        if 1 <= j <= nx:
            for half, m, bit, _ in self.plane(j - 1):
                self.corestart(m | bit, half)
        if j == nx + 1:
            for m in span(p.rest):
                for half in (0, 1):
                    self.hop(self.coresem(m, half), m, half, 1, True).wait_recv()


class Scatter:
    @staticmethod
    def scratch(nb, nz, r, wide, paired=False):
        c = wide // (2 if paired else nz)
        lines = 2 if paired else 2 * (nz - 1)
        count = nb // 2 + 2 * (nb // 2 - 1) + lines
        return [
            pltpu.VMEM((nb // 2, r, wide), BF16),
            pltpu.VMEM((nb // 2, r, wide), BF16),
            pltpu.VMEM((2 * (nb // 2 - 1), r // 2, wide), BF16),
            pltpu.VMEM((lines, r, c), BF16),
            pltpu.SemaphoreType.DMA((nb // 2,)),
            pltpu.SemaphoreType.DMA((count,)),
            pltpu.SemaphoreType.DMA((count,)),
        ]

    def __init__(self, place, full, share, scratch, paired=False):
        self.p, self.full, self.share, self.paired = place, full, share, paired
        self.sums, self.core, self.flat, self.got, self.local, self.send, self.recv = scratch
        _, self.r, self.wide = self.sums.shape
        self.c = self.got.shape[2]
        self.zsteps = 1 if paired else place.nz - 1
        self.stages = 2 + len(place.rest) + self.zsteps
        self.zsem = place.nb // 2 + 2 * (place.nb // 2 - 1)
        self.masks = sorted(span(place.rest))

    def add(self, target, source):
        def body(at):
            target[at] = (target[at].astype(F32) + source[at].astype(F32)).astype(target.dtype)

        rowwise(target.shape[0], 16, body)

    def block(self, mask):
        return self.full.at[part(flip(self.p.b, mask), self.r)]

    def corecopy(self, i, m):
        return remote(self.block(m | 1), self.core.at[i], self.send.at[i], self.recv.at[i], self.p.at(1))

    def load(self, i, m):
        return pltpu.make_async_copy(self.block(m), self.sums.at[i], self.local.at[i])

    def rows(self, m, half):
        return self.sums.at[m >> 1, part(half, self.r // 2)]

    def plane(self, j):
        p = self.p
        made = []
        for half in (0, 1):
            order = p.orders[half]
            base = half * (p.nb // 2 - 1) + sum(len(span(order[q + 1 :])) for q in range(j))
            for i, m in enumerate(span(order[j + 1 :])):
                made.append((half, m, 1 << order[j], base + i))
        return made

    def planecopy(self, half, m, bit, slot):
        sem = self.p.nb // 2 + slot
        return remote(
            self.rows(m | bit, half), self.flat.at[slot], self.send.at[sem], self.recv.at[sem], self.p.at(bit)
        )

    def column(self, index):
        return self.sums.at[0, :, part(index, self.c)]

    def line(self, way, step):
        p, n = self.p, self.p.nz
        here = p.z if way > 0 else n - 1 - p.z
        goes = n + here - step
        comes = goes - 1
        can_send = (goes > here) & (goes <= n - 1)
        can_get = (comes >= here) & (comes <= n - 1) & (here > 0)
        unfold = lambda d: jnp.clip(d if way > 0 else n - 1 - d, 0, n - 1)
        slot = (0 if way > 0 else n - 1) + step - 1
        copy = remote(
            self.column(unfold(goes)),
            self.got.at[slot],
            self.send.at[self.zsem + slot],
            self.recv.at[self.zsem + slot],
            (p.b, jnp.clip(p.z + way, 0, n - 1)),
        )
        return copy, can_send, can_get, unfold(comes), slot

    def paircopy(self, s):
        p = self.p
        copy = remote(
            self.column(s),
            self.got.at[p.group],
            self.send.at[self.zsem + s],
            self.recv.at[self.zsem + p.group],
            (p.b, 2 * p.k + s),
        )
        return copy, 2 * p.k + s != p.z

    def zstart(self, step):
        p = self.p
        if self.paired:
            for s in (0, 1):
                p.start(self.paircopy, s)
            return
        for way in (1, -1):
            p.start(self.lineout, way, step)

    def lineout(self, way, step):
        return self.line(way, step)[:2]

    def zwait(self, step):
        p = self.p
        if self.paired:
            for t in (0, 1):
                copy = remote(
                    self.column(0),
                    self.got.at[t],
                    self.send.at[self.zsem + t],
                    self.recv.at[self.zsem + t],
                    (p.b, p.partner),
                )
                pl.when(lax.div(p.z, 2) + t * p.half != p.z)(lambda copy=copy: copy.wait_recv())
            return
        for way in (1, -1):
            copy, _, can_get, column, slot = self.line(way, step)

            @pl.when(can_get)
            def _(copy=copy, column=column, slot=slot):
                copy.wait_recv()
                if step < self.zsteps:
                    self.add(self.column(column), self.got.at[slot])

    def stage(self, t):
        p = self.p
        nx = len(p.rest)
        if t == 0:
            for i, m in enumerate(self.masks):
                p.start(self.corecopy, i, m)
                self.load(i, m).start()
        if t == 1:
            for i, m in enumerate(self.masks):
                self.load(i, m).wait()
                self.corecopy(i, m).wait_recv()
                self.add(self.sums.at[i], self.core.at[i])
        j = t - 1
        if 1 <= j <= nx:
            for half, m, bit, slot in self.plane(j - 1):
                self.planecopy(half, m, bit, slot).wait_recv()
                self.add(self.rows(m, half), self.flat.at[slot])
        if 0 <= j < nx:
            for half, m, bit, slot in self.plane(j):
                p.start(self.planecopy, half, m, bit, slot)
        s = t - 1 - nx
        if 1 <= s <= self.zsteps:
            self.zwait(s)
        if 0 <= s < self.zsteps:
            self.zstart(s + 1)
        if t == self.stages - 1:
            self.finish()

    def finish(self):
        p = self.p
        if self.paired:
            mine = (2 * p.k == p.z) | (2 * p.k + 1 == p.z)
            own = part(lax.rem(p.z, 2), self.c)
            terms = [(self.got.at[t], lax.div(p.z, 2) + t * p.half != p.z) for t in (0, 1)]
        else:
            mine = None
            own = part(p.z, self.c)
            n = p.nz
            terms = [(self.got.at[n - 2], p.z > 0), (self.got.at[2 * n - 3], p.z < n - 1)]

        def first(at):
            value = self.sums[0, at, own].astype(F32)
            self.share[at] = value if mine is None else jnp.where(mine, value, 0.0)

        rowwise(self.r, 16, first)
        for ref, ok in terms:

            @pl.when(ok)
            def _(ref=ref):
                def more(at):
                    self.share[at] = self.share[at] + ref[at].astype(F32)

                rowwise(self.r, 16, more)


def perform(steps):
    for job, t in steps:
        job.stage(t)


def normalise(v):
    centred = v - jnp.mean(v, 1, keepdims=True)
    scale = lax.rsqrt(jnp.mean(centred * centred, 1, keepdims=True) + EPSILON)
    return centred * scale, scale


def norm_back(g, v, gain, gain_sum, shift_sum):
    n, scale = normalise(v)
    fold = lambda a: sum(a[i * 8 : (i + 1) * 8] for i in range(a.shape[0] // 8))
    gain_sum[...] += fold(g * n)
    shift_sum[...] += fold(g)
    gg = g * gain
    return (gg - jnp.mean(gg, 1, keepdims=True) - n * jnp.mean(gg * n, 1, keepdims=True)) * scale


def own_half(value, i):
    lane = lax.broadcasted_iota(jnp.int32, value.shape, 1)
    return jnp.where((lane >= HEAD_DIM) if i else (lane < HEAD_DIM), value, jnp.zeros_like(value))


def merge_halves(a, b):
    lane = lax.broadcasted_iota(jnp.int32, a.shape, 1)
    return jnp.where(lane < HEAD_DIM, a, b)


def project(normed, weight, qkv, pz):
    c = pz * 128
    rows = normed.shape[0]
    for j in (0, 1):
        for t in range(3):
            for i in range(rows // 512):
                at = pl.ds(i * 512, 512)
                y = nn(normed[at, :], weight[:, pl.ds((j * 3 + t) * c, c)])
                if t == 0:
                    y = y.astype(BF16).astype(F32) * HEAD_DIM**-0.5
                for w in range(pz):
                    qkv[t, j * pz + w, at, :] = y[:, w * 128 : (w + 1) * 128].astype(BF16)


def distances(dist, length):
    rows, cols = dist.shape

    def body(i, carry):
        row = lax.broadcasted_iota(jnp.int32, (64, cols), 0) + i * 64
        col = lax.broadcasted_iota(jnp.int32, (64, cols), 1)
        gap = jnp.abs(row - col).astype(F32)
        dist[part(i, 64), :] = jnp.where(col < length, gap, 1e33)
        return carry

    lax.fori_loop(0, rows // 64, body, 0)


def forward_tile(qkv, dist, pair, first_head, at, store):
    q, k, v = qkv[0, pair, at, :], qkv[1, pair], qkv[2, pair]
    gap = dist[at, :]
    outs = []
    for i in range(2):
        head = (first_head + 2 * pair + i + 1).astype(F32)
        slope = jnp.exp2(jnp.full((1, 1), -8.0 / HEADS, F32) * head) * LOG2E
        x = nt(own_half(q, i), k) * LOG2E - gap * slope
        e = jnp.exp2(x - jnp.max(x, 1, keepdims=True))
        p = (e * (1.0 / jnp.sum(e, 1, keepdims=True))).astype(BF16)
        store(i, p)
        outs.append(nn(p, v))
    return merge_halves(*outs).astype(BF16)


def backward_tile(qkv, do, do_t, q_t, pair, probs, dk, dv):
    k, v = qkv[1, pair], qkv[2, pair]
    dq = []
    for i in range(2):
        p = probs(i)
        rows = pl.ds(i * HEAD_DIM, HEAD_DIM)
        t = p.astype(F32) * nt(own_half(do, i), v)
        ds = (t - p.astype(F32) * jnp.sum(t, 1, keepdims=True)).astype(BF16)
        dq.append(nn(ds, k))
        dv[rows, :] += nn(do_t[rows, :], p)
        dk[rows, :] += nn(q_t[rows, :], ds)
    return (merge_halves(*dq) * HEAD_DIM**-0.5).astype(BF16)


def forward_kernel(
    nb, nz, lengths, x, skip_x, norms, skip_w, qkv_w, out_w, up_w, down_w,
    mixed_out, normed_out, norms_out, skip_out, qkvw_out, out_out, up_out, down_out, qkv_out, probs, attended_out,
    skip, qkvw, joined, mixed, normed, everything, gains, qkv, dist, pbuf, attended,
    load, norm_send, norm_recv, swap_send, swap_recv, flush, psem, att_send, att_recv, *rest,
):
    place = Place(nb, nz)
    z, group, k, half = place.z, place.group, place.k, place.half
    frames = x.shape[0] // 2
    width = x.shape[1]
    keys = nz * frames
    c = norms.shape[1]
    pz = c // 128
    pairs = 2 * pz
    place.greet()

    skip_s, qkvw_s, out_s, up_s, down_s = [rest[3 * i : 3 * i + 3] for i in range(5)]
    skip_job = Gather(place, skip_w, skip, skip_s)
    qkv_job = Gather(place, qkv_w, qkvw, qkvw_s, True)
    out_job = Gather(place, out_w, out_out, out_s)
    up_job = Gather(place, up_w, up_out, up_s)
    down_job = Gather(place, down_w, down_out, down_s)
    last = nz - 1

    skip_job.stage(0)
    loads = [
        pltpu.make_async_copy(x, joined.at[:, pl.ds(0, width)], load.at[0]),
        pltpu.make_async_copy(skip_x, joined.at[:, pl.ds(width, width)], load.at[1]),
        pltpu.make_async_copy(norms, gains.at[:, part(z, c)], load.at[2]),
    ]
    for one in loads:
        one.start()
    norm_copy = lambda r: remote(
        norms, gains.at[:, part(z, c)], norm_send.at[r - 1], norm_recv.at[r - 1], (place.b, lax.rem(z + r, nz))
    )
    for r in range(1, nz):
        place.start(norm_copy, r)
    for t in range(1, last):
        skip_job.stage(t)
    qkv_job.stage(0)
    skip_job.stage(last)
    out_job.stage(0)
    qkv_job.stage(1)
    for t in range(1, last + 1):
        out_job.stage(t)
    skip_job.stage(last + 1)
    up_job.stage(0)
    for t in range(last + 2, skip_job.stages):
        skip_job.stage(t)
    up_job.stage(1)
    qkv_job.stage(2)
    out_job.stage(last + 1)
    flushes = []

    def out_copy(src, dst):
        copy = pltpu.make_async_copy(src, dst, flush.at[len(flushes)])
        flushes.append(copy)
        copy.start()

    out_copy(skip, skip_out)
    for one in loads:
        one.wait()
    for r in range(1, nz):
        norm_copy(r).wait_recv()
    out_copy(gains, norms_out)

    def across():
        return remote(
            normed.at[1 - group], everything.at[part(z, frames)], swap_send.at[0], swap_recv.at[0],
            (place.b, place.partner),
        )

    for turn in (0, 1):
        item = 1 - group if turn == 0 else group
        rows = part(item, frames)
        mixed[rows, :] = nn(joined[rows, :], skip[...])
        gain, shift = gains[0:1, :], gains[1:2, :]

        def body(i, carry):
            at = part(i, 32)
            at2 = pl.ds(pl.multiple_of(item * frames + i * 32, 32), 32)
            n, _ = normalise(mixed[at2, :])
            normed[item, at, :] = (n * gain + shift).astype(BF16)
            return carry

        lax.fori_loop(0, frames // 32, body, 0)
        if turn == 0:
            place.start(across)
        else:
            own = pltpu.make_async_copy(normed.at[item], everything.at[part(z, frames)], load.at[0])
            own.start()

    def mate_copy(src, block, r, sem):
        return remote(
            src, everything.at[part(block, frames)], swap_send.at[sem], swap_recv.at[sem], (place.b, place.mate(r))
        )

    for r in range(1, half):
        place.start(mate_copy, normed.at[group], z, r, r)
    out_copy(mixed, mixed_out)
    across().wait_recv()
    for r in range(1, half):
        block = everything.at[part(place.partner, frames)]
        place.start(mate_copy, block, place.partner, r, half - 1 + r)
    distances(dist, lengths[group])
    up_job.stage(2)
    qkv_job.stage(3)
    for t in range(last + 2, out_job.stages):
        out_job.stage(t)
    for t in range(4, qkv_job.stages):
        qkv_job.stage(t)
    out_copy(qkvw, qkvw_out)
    for t in range(3, last + 1):
        up_job.stage(t)
    down_job.stage(0)
    own.wait()
    for r in range(1, half):
        mate_copy(normed.at[group], z, r, r).wait_recv()
        mate_copy(normed.at[group], z, r, half - 1 + r).wait_recv()
    out_copy(everything, normed_out)

    project(everything, qkvw, qkv, pz)
    out_copy(qkv, qkv_out)
    first_head = k * 2 * pairs
    blocks = keys // QUERIES
    total = pairs * blocks

    def probs_copy(slot, pair, at):
        return pltpu.make_async_copy(pbuf.at[slot], probs.at[pair, :, at], psem.at[slot])

    def att_copy(pair, r):
        owner = lax.rem(z + r, nz)
        slot = pair * (nz - 1) + r - 1
        return remote(
            attended.at[pair, part(owner, frames)],
            attended_out.at[part(group, frames), part(k * pairs + pair, 128)],
            att_send.at[slot], att_recv.at[slot], (place.b, owner),
        )

    def att_own(pair):
        return pltpu.make_async_copy(
            attended.at[pair, part(z, frames)],
            attended_out.at[part(group, frames), part(k * pairs + pair, 128)],
            flush.at[len(flushes)],
        )

    hooks = {}

    def hook(it, *steps):
        hooks.setdefault(min(it, total - 1), []).extend(steps)

    for t in range(1, last):
        hook(t, (down_job, t))
    hook(last, (up_job, last + 1), (down_job, last))
    hook(total * 5 // 8, (up_job, last + 2))
    hook(total * 6 // 8, (down_job, last + 1))

    def body(it, carry):
        pair, q = lax.div(it, blocks), lax.rem(it, blocks)
        at, slot = part(q, QUERIES), lax.rem(it, 2)
        for when, steps in hooks.items():
            pl.when(it == when)(lambda steps=steps: perform(steps))

        @pl.when(it >= 2)
        def _():
            probs_copy(slot, pair, at).wait()

        def store(i, p):
            pbuf[slot, i] = p

        attended[pair, at, :] = forward_tile(qkv, dist, pair, first_head, at, store)
        probs_copy(slot, pair, at).start()

        @pl.when(q == blocks - 1)
        def _():
            for r in range(1, nz):
                att_copy(pair, r).start()

        return carry

    lax.fori_loop(0, total, body, 0)
    for pair in range(pairs):
        att_own(pair).start()
    for t in range(last + 3, up_job.stages):
        up_job.stage(t)
    for t in range(last + 2, down_job.stages):
        down_job.stage(t)
    for pair in range(pairs):
        for r in range(1, nz):
            att_copy(pair, r).wait()
    for pair in range(pairs):
        att_own(pair).wait()
    for slot in range(min(2, total)):
        probs_copy(slot, 0, pl.ds(0, QUERIES)).wait()
    for copy in flushes:
        copy.wait()
    place.drain()


def forward(nb, nz, lengths, x, skip_x, norms, skip_w, qkv_w, out_w, up_w, down_w):
    rows, width = x.shape
    frames = rows // 2
    keys = nz * frames
    pairs = 2 * norms.shape[1] // 128
    S, V, D = jax.ShapeDtypeStruct, pltpu.VMEM, pltpu.SemaphoreType.DMA
    full = lambda w, n: (nb * w.shape[0], n * w.shape[1])
    out_shape = [
        S((rows, width), F32),
        S((keys, width), BF16),
        S((norms.shape[0], width), F32),
        S(full(skip_w, nz), BF16),
        S(full(qkv_w, 2), BF16),
        S(full(out_w, nz), BF16),
        S(full(up_w, nz), BF16),
        S(full(down_w, nz), BF16),
        S((3, pairs, keys, 128), BF16),
        S((pairs, 2, keys, keys), BF16),
        S((rows, width), BF16),
    ]
    scratch = [
        V(full(skip_w, nz), BF16),
        V(full(qkv_w, 2), BF16),
        V((rows, 2 * width), BF16),
        V((rows, width), F32),
        V((2, frames, width), BF16),
        V((keys, width), BF16),
        V((norms.shape[0], width), F32),
        V((3, pairs, keys, 128), BF16),
        V((keys, keys), F32),
        V((2, 2, QUERIES, keys), BF16),
        V((pairs, keys, 128), BF16),
    ]
    scratch += [D((3,)), D((nz - 1,)), D((nz - 1,)), D((nz - 1,)), D((nz - 1,)), D((8,)), D((2,))]
    scratch += [D((pairs * (nz - 1),)), D((pairs * (nz - 1),))]
    for _ in range(5):
        scratch += Gather.scratch(nb, nz)
    return pl.pallas_call(
        functools.partial(forward_kernel, nb, nz),
        out_shape=out_shape,
        in_specs=[pl.BlockSpec(memory_space=pltpu.SMEM)] + [ANY] * 8,
        out_specs=[ANY] * len(out_shape),
        scratch_shapes=scratch,
        compiler_params=pltpu.CompilerParams(
            collective_id=0, has_side_effects=True, vmem_limit_bytes=VMEM_LIMIT
        ),
    )(lengths, x, skip_x, norms, skip_w, qkv_w, out_w, up_w, down_w)


def ffn_kernel(
    steps, mixed, attended, out_t, norms, cot, up, dn,
    output, middle_grad, att_grad, out_grad, up_grad, dn_grad, sums,
    middle, ffn_in, ffn_in_t, cot_t, acc, gacc,
):
    j = pl.program_id(0)
    rows = mixed.shape[0]
    gain, shift = norms[2:3, :], norms[3:4, :]

    @pl.when(j == 0)
    def _():
        middle[...] = nt(attended[...], out_t[...])

        def body(at):
            v = middle[at, :] + mixed[at, :]
            middle[at, :] = v
            n, _ = normalise(v)
            ffn_in[at, :] = (n * gain + shift).astype(BF16)

        rowwise(rows, 32, body)
        ffn_in_t[...] = ffn_in[...].T
        cot_t[...] = cot[...].T
        acc[...] = jnp.zeros_like(acc)
        gacc[...] = jnp.zeros_like(gacc)

    hidden = nn(ffn_in[...], up[...])
    active_grad = nn(cot[...], dn[...])
    cdf = 0.5 * (1.0 + lax.erf(hidden * 0.7071067811865476))
    active = (hidden * cdf).astype(BF16)
    density = jnp.exp2(hidden * hidden * (-0.5 * LOG2E)) * 0.3989422804014327
    hidden_grad = (active_grad * (cdf + hidden * density)).astype(BF16)
    acc[...] += nt(active, dn[...])
    gacc[...] += nt(hidden_grad, up[...])
    dn_grad[...] = nn(cot_t[...], active).astype(BF16)
    up_grad[...] = nn(ffn_in_t[...], hidden_grad).astype(BF16)

    @pl.when(j == steps - 1)
    def _():
        sums[...] = jnp.zeros_like(sums)

        def body(at):
            v = middle[at, :]
            output[at, :] = (v + acc[at, :]).astype(BF16)
            back = norm_back(gacc[at, :], v, gain, sums.at[0], sums.at[1])
            grad = cot[at, :].astype(F32) + back
            middle_grad[at, :] = grad
            ffn_in[at, :] = grad.astype(BF16)

        rowwise(rows, 32, body)
        att_grad[...] = nn(ffn_in[...], out_t[...]).astype(BF16)
        out_grad[...] = nn(ffn_in[...].T, attended[...]).astype(BF16)


def ffn(mixed, attended, out_t, norms, cot, up, dn):
    rows, d = mixed.shape
    ff = up.shape[1]
    block = min(512, ff)
    steps = ff // block
    V, S = pltpu.VMEM, jax.ShapeDtypeStruct
    column = pl.BlockSpec((d, block), lambda j: (0, j))
    return pl.pallas_call(
        functools.partial(ffn_kernel, steps),
        grid=(steps,),
        in_specs=[WHOLE] * 5 + [column, column],
        out_specs=[WHOLE] * 4 + [column, column, WHOLE],
        out_shape=[
            S((rows, d), BF16),
            S((rows, d), F32),
            S((rows, d), BF16),
            S((d, d), BF16),
            S((d, ff), BF16),
            S((d, ff), BF16),
            S((2, 8, d), F32),
        ],
        scratch_shapes=[
            V((rows, d), F32),
            V((rows, d), BF16),
            V((d, rows), BF16),
            V((d, rows), BF16),
            V((rows, d), F32),
            V((rows, d), F32),
        ],
        compiler_params=pltpu.CompilerParams(vmem_limit_bytes=VMEM_LIMIT),
    )(mixed, attended, out_t, norms, cot, up, dn)


def attention_kernel(
    nb, nz, att_grad, qkv_in, probs, up_grad, dn_grad, out_grad,
    dqkv, up_share, dn_share, out_share,
    qkv, dout, pbuf, dk, dv, q_t, do_t, load, psem, att_send, att_recv, *rest,
):
    place = Place(nb, nz)
    z, group, k = place.z, place.group, place.k
    pairs, keys = qkv.shape[1], qkv.shape[2]
    frames = keys // nz
    wide = pairs * 128
    pz = pairs // 2
    per = len(rest) // 3
    place.greet()

    def att_copy(r):
        owner = lax.rem(z + r, nz)
        item, member = lax.div(owner, place.half), lax.rem(owner, place.half)
        return remote(
            att_grad.at[part(item, frames), part(member, wide)], dout.at[part(z, frames)],
            att_send.at[r - 1], att_recv.at[r - 1], (place.b, owner),
        )

    for r in range(1, nz):
        place.start(att_copy, r)
    own = pltpu.make_async_copy(att_grad.at[part(group, frames), part(k, wide)], dout.at[part(z, frames)], load.at[0])
    own.start()
    qkv_load = pltpu.make_async_copy(qkv_in, qkv, load.at[1])
    qkv_load.start()
    dn_job = Scatter(place, dn_grad, dn_share, rest[:per])
    up_job = Scatter(place, up_grad, up_share, rest[per : 2 * per])
    out_job = Scatter(place, out_grad, out_share, rest[2 * per :])
    nx = len(place.rest)
    dn_job.stage(0)
    up_job.stage(0)
    out_job.stage(0)
    dn_job.stage(1)
    up_job.stage(1)
    own.wait()
    qkv_load.wait()

    blocks = keys // QUERIES
    total = pairs * blocks

    def probs_copy(it):
        slot = lax.rem(it, 2)
        pair, q = lax.div(it, blocks), lax.rem(it, blocks)
        return pltpu.make_async_copy(probs.at[pair, :, part(q, QUERIES)], pbuf.at[slot], psem.at[slot])

    probs_copy(0).start()
    for r in range(1, nz):
        att_copy(r).wait_recv()
    hooks = {}

    def hook(it, *steps):
        hooks.setdefault(min(it, total - 1), []).extend(steps)

    hook(total // 8, (dn_job, 2))
    hook(total * 4 // 8, (up_job, 2))
    hook(total * 5 // 8, (out_job, 1))
    hook(total * 6 // 8, (dn_job, 3))

    def body(it, carry):
        pair, q = lax.div(it, blocks), lax.rem(it, blocks)
        at, slot = part(q, QUERIES), lax.rem(it, 2)
        for when, steps in hooks.items():
            pl.when(it == when)(lambda steps=steps: perform(steps))

        @pl.when(it + 1 < total)
        def _():
            probs_copy(it + 1).start()

        probs_copy(it).wait()

        @pl.when(q == 0)
        def _():
            dk[...] = jnp.zeros_like(dk)
            dv[...] = jnp.zeros_like(dv)

        do = dout[at, part(pair, 128)]
        q_t[...] = qkv[0, pair, at, :].T
        do_t[...] = do.T
        block = lax.div(pair, pz)
        column = lambda t: part((block * 3 + t) * pz + lax.rem(pair, pz), 128)
        dqkv[at, column(0)] = backward_tile(qkv, do, do_t, q_t, pair, lambda i: pbuf[slot, i], dk, dv)

        @pl.when(q == blocks - 1)
        def _():
            dqkv[:, column(1)] = dk[...].T.astype(BF16)
            dqkv[:, column(2)] = dv[...].T.astype(BF16)

        return carry

    lax.fori_loop(0, total, body, 0)
    first = {id(dn_job): 4, id(up_job): 3, id(out_job): 2}
    for t in range(2, dn_job.stages + 3):
        for lag, job in enumerate((dn_job, up_job, out_job)):
            if first[id(job)] <= t - lag < job.stages:
                job.stage(t - lag)
    place.drain()


def attention_back(nb, nz, att_grad, qkv, probs, up_grad, dn_grad, out_grad):
    _, pairs, keys, _ = qkv.shape
    S, V, D = jax.ShapeDtypeStruct, pltpu.VMEM, pltpu.SemaphoreType.DMA
    grads = (dn_grad, up_grad, out_grad)
    share = lambda g: S((g.shape[0] // nb, g.shape[1] // nz), F32)
    scratch = [
        V((3, pairs, keys, 128), BF16),
        V((keys, pairs * 128), BF16),
        V((2, 2, QUERIES, keys), BF16),
        V((128, keys), F32),
        V((128, keys), F32),
        V((128, QUERIES), BF16),
        V((128, QUERIES), BF16),
        D((2,)), D((2,)), D((nz - 1,)), D((nz - 1,)),
    ]
    for g in grads:
        scratch += Scatter.scratch(nb, nz, g.shape[0] // nb, g.shape[1])
    return pl.pallas_call(
        functools.partial(attention_kernel, nb, nz),
        out_shape=[S((keys, 3 * pairs * 128), BF16), share(up_grad), share(dn_grad), share(out_grad)],
        in_specs=[ANY] * 6,
        out_specs=[WHOLE] * 4,
        scratch_shapes=scratch,
        compiler_params=pltpu.CompilerParams(
            collective_id=1, has_side_effects=True, vmem_limit_bytes=VMEM_LIMIT
        ),
    )(att_grad, qkv, probs, up_grad, dn_grad, out_grad)


def first_kernel(
    nb, nz, dqkv, everything, qkvw, x, skip_x, skip_w, mixed, middle_grad, norms, second_sums,
    input_grad, skip_grad, qkv_share, skip_share, norm_share,
    qkv_grad, skip_w_grad, weight, joined, mixed_low, ahead, mine, from_mate, to_partner, from_partner,
    sums, packed, norm_in, norm_line, load, swap_send, swap_recv, norm_send, norm_recv, *rest,
):
    place = Place(nb, nz)
    z, group, k, half = place.z, place.group, place.k, place.half
    frames = x.shape[0] // 2
    width = x.shape[1]
    per = len(rest) // 2
    place.greet()
    qkv_job = Scatter(place, qkv_grad, qkv_share, rest[:per], True)
    skip_job = Scatter(place, skip_w_grad, skip_share, rest[per:])
    loads = [
        pltpu.make_async_copy(x, joined.at[:, pl.ds(0, width)], load.at[0]),
        pltpu.make_async_copy(skip_x, joined.at[:, pl.ds(width, width)], load.at[1]),
        pltpu.make_async_copy(skip_w, weight, load.at[2]),
    ]
    for one in loads:
        one.start()

    def mate_copy(r, t):
        slot = (r - 1) * 2 + t
        return remote(
            ahead.at[slot], from_mate.at[slot], swap_send.at[slot], swap_recv.at[slot], (place.b, place.mate(r))
        )

    for r in range(1, half):
        for t in (0, 1):
            block = lax.rem(k + r, half) + t * half
            ahead[(r - 1) * 2 + t] = nt(dqkv[part(block, frames), :], qkvw[...]).astype(BF16)
            place.start(mate_copy, r, t)
    for t in (0, 1):
        mine[t] = nt(dqkv[part(k + t * half, frames), :], qkvw[...])
    qkv_grad[...] = nn(everything[...].T, dqkv[...]).astype(BF16)
    qkv_job.stage(0)
    for r in range(1, half):
        for t in (0, 1):
            mate_copy(r, t).wait_recv()
            slot = (r - 1) * 2 + t

            def body(at):
                mine[t, at] = mine[t, at] + from_mate[slot, at].astype(F32)

            rowwise(frames, 16, body)
    sem = 2 * (half - 1)
    across = lambda: remote(to_partner, from_partner, swap_send.at[sem], swap_recv.at[sem], (place.b, place.partner))

    def narrow(at):
        to_partner[at] = mine[1 - group, at].astype(BF16)

    rowwise(frames, 16, narrow)
    place.start(across)
    qkv_job.stage(1)

    sums[...] = jnp.zeros_like(sums)
    gain = norms[0:1, :]

    def back(item, grad):
        def body(i, carry):
            at = part(i, 32)
            to = pl.ds(pl.multiple_of(item * frames + i * 32, 32), 32)
            part_grad = norm_back(grad(at), mixed[to, :], gain, sums.at[0], sums.at[1])
            mixed_low[to, :] = (middle_grad[to, :] + part_grad).astype(BF16)
            return carry

        lax.fori_loop(0, frames // 32, body, 0)

    back(group, lambda at: mine[group, at])
    across().wait_recv()
    back(1 - group, lambda at: from_partner[at].astype(F32))
    for one in loads:
        one.wait()
    skip_w_grad[...] = nn(joined[...].T, mixed_low[...]).astype(BF16)
    skip_job.stage(0)

    total = lambda a: jnp.sum(a, 0, keepdims=True)
    for i, v in enumerate((sums[0], sums[1], second_sums[0], second_sums[1])):
        packed[i : i + 1, :] = total(v)
    packed[4:8, :] = jnp.zeros_like(packed[4:8, :])
    bits = [0] + place.rest
    norm_copy = lambda i: remote(
        packed, norm_in.at[i], norm_send.at[i], norm_recv.at[i], place.at(1 << bits[i])
    )
    c = norm_share.shape[1]
    line_copy = lambda r: remote(
        packed.at[:, part(lax.rem(z + r, nz), c)], norm_line.at[r - 1],
        norm_send.at[len(bits) + r - 1], norm_recv.at[len(bits) + r - 1], (place.b, lax.rem(z + r, nz)),
    )

    def norm_step(i):
        if i > 0:
            norm_copy(i - 1).wait()
            packed[...] = packed[...] + norm_in[i - 1]
        if i < len(bits):
            norm_copy(i).start()
        else:
            for r in range(1, nz):
                line_copy(r).start()

    norm_step(0)
    skip_job.stage(1)
    norm_step(1)
    qkv_job.stage(2)
    for t in range(2):
        (input_grad, skip_grad)[t][...] = nt(mixed_low[...], weight[pl.ds(t * width, width), :])
        norm_step(2 + t)
    for i in range(4, len(bits) + 1):
        norm_step(i)
    skip_job.stage(2)
    qkv_job.stage(3)
    for t in range(3, max(skip_job.stages, qkv_job.stages - 1)):
        if t < skip_job.stages:
            skip_job.stage(t)
        if t + 1 < qkv_job.stages:
            qkv_job.stage(t + 1)
    value = packed[:, part(z, c)]
    for r in range(1, nz):
        line_copy(r).wait()
        value = value + norm_line[r - 1]
    norm_share[...] = value
    place.drain()


def first_back(nb, nz, dqkv, everything, qkvw, x, skip_x, skip_w, mixed, middle_grad, norms, second_sums):
    rows, width = x.shape
    frames = rows // 2
    half = nz // 2
    c = width // nz
    S, V, D = jax.ShapeDtypeStruct, pltpu.VMEM, pltpu.SemaphoreType.DMA
    qkv_wide = qkvw.shape[1]
    bits = nb.bit_length() - 1
    swaps = 2 * (half - 1)
    scratch = [
        V(qkvw.shape, BF16),
        V(skip_w.shape, BF16),
        V(skip_w.shape, BF16),
        V((rows, 2 * width), BF16),
        V((rows, width), BF16),
        V((max(swaps, 1), frames, width), BF16),
        V((2, frames, width), F32),
        V((max(swaps, 1), frames, width), BF16),
        V((frames, width), BF16),
        V((frames, width), BF16),
        V((2, 8, width), F32),
        V((8, width), F32),
        V((bits, 8, width), F32),
        V((nz - 1, 8, c), F32),
        D((3,)), D((swaps + 1,)), D((swaps + 1,)), D((bits + nz - 1,)), D((bits + nz - 1,)),
    ]
    scratch += Scatter.scratch(nb, nz, qkvw.shape[0] // nb, qkv_wide, True)
    scratch += Scatter.scratch(nb, nz, skip_w.shape[0] // nb, width)
    return pl.pallas_call(
        functools.partial(first_kernel, nb, nz),
        out_shape=[
            S((rows, width), F32),
            S((rows, width), F32),
            S((qkvw.shape[0] // nb, qkv_wide // 2), F32),
            S((skip_w.shape[0] // nb, c), F32),
            S((8, c), F32),
        ],
        in_specs=[WHOLE] * 3 + [ANY] * 3 + [WHOLE] * 4,
        out_specs=[WHOLE] * 5,
        scratch_shapes=scratch,
        compiler_params=pltpu.CompilerParams(
            collective_id=2, has_side_effects=True, vmem_limit_bytes=VMEM_LIMIT
        ),
    )(dqkv, everything, qkvw, x, skip_x, skip_w, mixed, middle_grad, norms, second_sums)


def shards(
    inputs,
    skip_input,
    lengths,
    skip_weight,
    query_weight,
    key_weight,
    value_weight,
    out_weight,
    up_weight,
    down_weight,
    first_gain,
    first_shift,
    second_gain,
    second_shift,
    cotangent,
):
    nb, nz = lax.axis_size("batch"), lax.axis_size("seq")
    shape = inputs.shape
    flat = lambda a: a.reshape(shape[0] * shape[1], shape[2])
    x, skip_x, cot = flat(inputs), flat(skip_input), flat(cotangent)
    norms = jnp.stack([first_gain, first_shift, second_gain, second_shift]).astype(F32)
    norms = jnp.pad(norms, ((0, 4), (0, 0)))
    qkv_shard = jnp.concatenate([query_weight, key_weight, value_weight], 1)
    (mixed, everything, gains, skip_w, qkvw, out_t, up, down_t, qkv, probs, attended) = forward(
        nb, nz, lengths, x, skip_x, norms, skip_weight, qkv_shard, out_weight.T, up_weight, down_weight.T
    )
    output, middle_grad, att_grad, out_grad, up_grad, dn_grad, second_sums = ffn(
        mixed, attended, out_t, gains, cot, up, down_t
    )
    dqkv, up_share, dn_share, out_share = attention_back(
        nb, nz, att_grad, qkv, probs, up_grad, dn_grad, out_grad
    )
    input_grad, skip_grad, qkv_share, skip_share, norm_share = first_back(
        nb, nz, dqkv, everything, qkvw, x, skip_x, skip_w, mixed, middle_grad, gains, second_sums
    )
    c = query_weight.shape[1]
    return (
        output.reshape(shape),
        input_grad.reshape(shape),
        skip_grad.reshape(shape),
        skip_share,
        qkv_share[:, :c],
        qkv_share[:, c : 2 * c],
        qkv_share[:, 2 * c :],
        out_share.T,
        up_share,
        dn_share.T,
        norm_share[0],
        norm_share[1],
        norm_share[2],
        norm_share[3],
    )


def solution(mesh):
    rows = P("batch", "seq", None)
    weight, turned, norm = P("batch", "seq"), P("seq", "batch"), P("seq")
    return jax.shard_map(
        shards,
        mesh=mesh,
        in_specs=(rows, rows, P("batch"), *[weight] * 4, turned, weight, turned, *[norm] * 4, rows),
        out_specs=(rows, rows, rows, *[weight] * 4, turned, weight, turned, *[norm] * 4),
        check_vma=False,
    )
```

```python
import functools

import jax
import jax.numpy as jnp
from jax import lax
from jax.experimental import pallas as pl
from jax.experimental.pallas import tpu as pltpu
from jax.sharding import PartitionSpec as P

HEADS = 16
HEAD_DIM = 64
EPSILON = 1e-05
LOG2E = 1.4426950408889634
QUERIES = 256
F32 = jnp.float32
BF16 = jnp.bfloat16
MESH = pl.DeviceIdType.MESH
VMEM_LIMIT = 60 * 2**20
ANY = pl.BlockSpec(memory_space=pl.ANY)
WHOLE = pl.BlockSpec(memory_space=pltpu.VMEM)


def nt(a, b):
    return lax.dot_general(a, b, (((1,), (1,)), ((), ())), preferred_element_type=F32)


def nn(a, b):
    return jnp.dot(a, b, preferred_element_type=F32)


def part(index, size):
    if isinstance(index, int):
        return pl.ds(index * size, size)
    return pl.ds(pl.multiple_of(index * size, size), size)


def rowwise(rows, step, body):
    def run(i, carry):
        body(part(i, step))
        return carry

    lax.fori_loop(0, rows // step, run, 0)


def flip(index, mask):
    result = index
    bit = 0
    while mask >> bit:
        if (mask >> bit) & 1:
            on = lax.rem(lax.div(index, 1 << bit), 2)
            result = result + (1 << bit) * (1 - 2 * on)
        bit += 1
    return result


def span(bits):
    masks = [0]
    for bit in bits:
        masks = masks + [m | (1 << bit) for m in masks]
    return masks


class Place:
    def __init__(self, nb, nz):
        self.nb, self.nz = nb, nz
        self.b = lax.axis_index("batch")
        self.z = lax.axis_index("seq")
        self.half = nz // 2
        self.group = lax.div(self.z, self.half)
        self.k = lax.rem(self.z, self.half)
        self.partner = lax.rem(self.z + self.half, nz)
        self.rest = list(range(1, nb.bit_length() - 1))
        self.orders = (self.rest, self.rest[::-1])
        self.pending = []

    def at(self, mask):
        return (flip(self.b, mask), self.z)

    def mate(self, r):
        return self.group * self.half + lax.rem(self.k + r, self.half)

    def greet(self):
        barrier = pltpu.get_barrier_semaphore()
        targets = [self.at(1 << k) for k in [0] + self.rest]
        targets += [(self.b, lax.rem(self.z + r, self.nz)) for r in range(1, self.nz)]
        for t in targets:
            pl.semaphore_signal(barrier, inc=1, device_id=t, device_id_type=MESH)
        pl.semaphore_wait(barrier, len(targets))

    def start(self, make, *args):
        copy, ok = self.unpack(make(*args))
        if ok is None:
            copy.start()
        else:
            pl.when(ok)(lambda: copy.start())
        self.pending.append((make, args))

    def drain(self):
        for make, args in self.pending:
            copy, ok = self.unpack(make(*args))
            if ok is None:
                copy.wait_send()
            else:
                pl.when(ok)(lambda copy=copy: copy.wait_send())
        self.pending = []

    @staticmethod
    def unpack(made):
        return made if isinstance(made, tuple) else (made, None)


def remote(src, dst, send, recv, device):
    return pltpu.make_async_remote_copy(
        src_ref=src, dst_ref=dst, send_sem=send, recv_sem=recv, device_id=device, device_id_type=MESH
    )


class Gather:
    @staticmethod
    def sems(nb, nz):
        return 2 * (nz - 1) + 2 * (nb // 2 - 1) + nb

    @staticmethod
    def scratch(nb, nz):
        count = Gather.sems(nb, nz)
        return [pltpu.SemaphoreType.DMA] + [pltpu.SemaphoreType.DMA((count,))] * 2

    def __init__(self, place, shard, full, scratch, paired=False):
        self.p, self.shard, self.full, self.paired = place, shard, full, paired
        self.local, self.send, self.recv = scratch
        self.r, self.c = shard.shape
        nb, nz = place.nb, place.nz
        self.xy0 = 2 * (nz - 1)
        self.core0 = self.xy0 + 2 * (nb // 2 - 1)
        self.zsteps = 1 if paired else nz - 1
        self.stages = self.zsteps + len(place.rest) + 2

    def column(self, index):
        return self.full.at[part(self.p.b, self.r), part(index, self.c)]

    def line(self, way, step):
        p, n = self.p, self.p.nz
        sem = (0 if way > 0 else n - 1) + step - 1
        sent, got = p.z - way * (step - 1), p.z - way * step
        inside = lambda v: (v >= 0) & (v < n)
        clip = lambda v: jnp.clip(v, 0, n - 1)
        to = (p.b, clip(p.z + way))
        block = self.column(clip(sent))
        out = lambda: remote(self.shard if step == 1 else block, block, self.send.at[sem], self.recv.at[sem], to)
        land = self.column(clip(got))
        into = lambda: remote(land, land, self.send.at[sem], self.recv.at[sem], to)
        return out, into, inside(sent) & inside(p.z + way), inside(got)

    def zstart(self, step):
        p = self.p
        if self.paired:
            for t in (0, 1):
                p.start(self.paircopy, t)
            return
        for way in (1, -1):
            p.start(self.lineout, way, step)

    def lineout(self, way, step):
        out, _, can_send, _ = self.line(way, step)
        return out(), can_send

    def paircopy(self, t):
        p = self.p
        target = lax.div(p.z, 2) + t * p.half
        slot = lax.rem(p.z, 2)
        copy = remote(self.shard, self.column(slot), self.send.at[t], self.recv.at[slot], (p.b, target))
        return copy, target != p.z

    def zwait(self, step):
        p = self.p
        if self.paired:
            for s in (0, 1):
                land = self.column(s)
                copy = remote(land, land, self.send.at[s], self.recv.at[s], (p.b, p.partner))
                pl.when(2 * p.k + s != p.z)(lambda copy=copy: copy.wait_recv())
            return
        for way in (1, -1):
            _, into, _, can_get = self.line(way, step)
            pl.when(can_get)(lambda into=into: into().wait_recv())

    def owncopy(self):
        p = self.p
        if self.paired:
            mine = (2 * p.k == p.z) | (2 * p.k + 1 == p.z)
            return pltpu.make_async_copy(self.shard, self.column(lax.rem(p.z, 2)), self.local), mine
        return pltpu.make_async_copy(self.shard, self.column(p.z), self.local), None

    def rows(self, mask, half):
        h = self.r // 2
        return self.full.at[part(flip(self.p.b, mask) * 2 + half, h)]

    def hop(self, sem, mask, half, bit, incoming):
        block = self.rows(mask | bit if incoming else mask, half)
        return remote(block, block, self.send.at[sem], self.recv.at[sem], self.p.at(bit))

    def plane(self, j):
        made = []
        for half in (0, 1):
            order = self.p.orders[half]
            for i, m in enumerate(span(order[:j])):
                sem = self.xy0 + half * (self.p.nb // 2 - 1) + (1 << j) - 1 + i
                made.append((half, m, 1 << order[j], sem))
        return made

    def coresem(self, mask, half):
        return self.core0 + (mask >> 1) * 2 + half

    def corestart(self, mask, half):
        self.p.start(self.hop, self.coresem(mask, half), mask, half, 1, False)

    def stage(self, t):
        p = self.p
        nx = len(p.rest)
        if t == 0:
            own, mine = self.owncopy()
            if mine is None:
                own.start()
            else:
                pl.when(mine)(lambda: own.start())
            self.zstart(1)
        if 1 <= t <= self.zsteps:
            self.zwait(t)
            if t < self.zsteps:
                self.zstart(t + 1)
            else:
                own, mine = self.owncopy()
                if mine is None:
                    own.wait()
                else:
                    pl.when(mine)(lambda: own.wait())
        j = t - self.zsteps
        if 1 <= j <= nx:
            for half, m, bit, sem in self.plane(j - 1):
                self.hop(sem, m, half, bit, True).wait_recv()
        if 0 <= j < nx:
            for half, m, bit, sem in self.plane(j):
                p.start(self.hop, sem, m, half, bit, False)
        if j == 0:
            for half in (0, 1):
                self.corestart(0, half)
        if 1 <= j <= nx:
            for half, m, bit, _ in self.plane(j - 1):
                self.corestart(m | bit, half)
        if j == nx + 1:
            for m in span(p.rest):
                for half in (0, 1):
                    self.hop(self.coresem(m, half), m, half, 1, True).wait_recv()


class Scatter:
    @staticmethod
    def scratch(nb, nz, r, wide, paired=False, sums=True, plane=True, line=True):
        c = wide // (2 if paired else nz)
        lines = 2 if paired else 2 * (nz - 1)
        count = nb // 2 + 2 * (nb // 2 - 1) + lines
        made = [pltpu.VMEM((nb // 2 if plane else 1, r, wide), BF16)] if sums else []
        if plane:
            made += [
                pltpu.VMEM((nb // 2, r, wide), BF16),
                pltpu.VMEM((2 * (nb // 2 - 1), r // 2, wide), BF16),
            ]
        if line:
            made += [pltpu.VMEM((lines, r, c), BF16)]
        return made + [
            pltpu.SemaphoreType.DMA((nb // 2,)),
            pltpu.SemaphoreType.DMA((count,)),
            pltpu.SemaphoreType.DMA((count,)),
        ]

    def __init__(self, place, full, share, scratch, paired=False, sums=True, plane=True, line=True):
        self.p, self.full, self.share, self.paired = place, full, share, paired
        scratch = list(scratch)
        self.sums = scratch.pop(0) if sums else None
        self.core, self.flat = (scratch.pop(0), scratch.pop(0)) if plane else (None, None)
        self.got = scratch.pop(0) if line else None
        self.local, self.send, self.recv = scratch
        self.has_plane, self.has_line = plane, line
        _, self.r, self.wide = (full if plane else self.sums).shape
        self.c = self.wide // (2 if paired else place.nz)
        self.zsteps = 1 if paired else place.nz - 1
        self.nx = len(place.rest)
        self.plane_stages = 2 + self.nx
        self.stages = (self.plane_stages if plane else 1) + (self.zsteps if line else 0)
        self.zsem = place.nb // 2 + 2 * (place.nb // 2 - 1)
        self.masks = sorted(span(place.rest))

    def sum(self, m):
        return self.full.at[m] if self.sums is None else self.sums.at[m >> 1]

    def add(self, target, source):
        def body(at):
            target[at] = (target[at].astype(F32) + source[at].astype(F32)).astype(target.dtype)

        rowwise(target.shape[0], 16, body)

    def corecopy(self, i, m):
        return remote(self.full.at[m | 1], self.core.at[i], self.send.at[i], self.recv.at[i], self.p.at(1))

    def load(self, i, m):
        return pltpu.make_async_copy(self.full.at[m], self.sum(m), self.local.at[i])

    def rows(self, m, half):
        return self.sum(m).at[part(half, self.r // 2)]

    def plane(self, j):
        p = self.p
        made = []
        for half in (0, 1):
            order = p.orders[half]
            base = half * (p.nb // 2 - 1) + sum(len(span(order[q + 1 :])) for q in range(j))
            for i, m in enumerate(span(order[j + 1 :])):
                made.append((half, m, 1 << order[j], base + i))
        return made

    def planecopy(self, half, m, bit, slot):
        sem = self.p.nb // 2 + slot
        return remote(
            self.rows(m | bit, half), self.flat.at[slot], self.send.at[sem], self.recv.at[sem], self.p.at(bit)
        )

    def column(self, index):
        return self.sum(0).at[:, part(index, self.c)]

    def line(self, way, step):
        p, n = self.p, self.p.nz
        here = p.z if way > 0 else n - 1 - p.z
        goes = n + here - step
        comes = goes - 1
        can_send = (goes > here) & (goes <= n - 1)
        can_get = (comes >= here) & (comes <= n - 1) & (here > 0)
        unfold = lambda d: jnp.clip(d if way > 0 else n - 1 - d, 0, n - 1)
        slot = (0 if way > 0 else n - 1) + step - 1
        copy = remote(
            self.column(unfold(goes)),
            self.got.at[slot],
            self.send.at[self.zsem + slot],
            self.recv.at[self.zsem + slot],
            (p.b, jnp.clip(p.z + way, 0, n - 1)),
        )
        return copy, can_send, can_get, unfold(comes), slot

    def paircopy(self, s):
        p = self.p
        copy = remote(
            self.column(s),
            self.got.at[p.group],
            self.send.at[self.zsem + s],
            self.recv.at[self.zsem + p.group],
            (p.b, 2 * p.k + s),
        )
        return copy, 2 * p.k + s != p.z

    def lineout(self, way, step):
        return self.line(way, step)[:2]

    def zstart(self, step):
        p = self.p
        if self.paired:
            for s in (0, 1):
                p.start(self.paircopy, s)
            return
        for way in (1, -1):
            p.start(self.lineout, way, step)

    def zwait(self, step):
        p = self.p
        if self.paired:
            for t in (0, 1):
                copy = remote(
                    self.column(0),
                    self.got.at[t],
                    self.send.at[self.zsem + t],
                    self.recv.at[self.zsem + t],
                    (p.b, p.partner),
                )
                pl.when(lax.div(p.z, 2) + t * p.half != p.z)(lambda copy=copy: copy.wait_recv())
            return
        for way in (1, -1):
            copy, _, can_get, column, slot = self.line(way, step)

            @pl.when(can_get)
            def _(copy=copy, column=column, slot=slot):
                copy.wait_recv()
                if step < self.zsteps:
                    self.add(self.column(column), self.got.at[slot])

    def stage(self, t):
        p, nx = self.p, self.nx
        s = t - (self.plane_stages - 1 if self.has_plane else 0)
        if self.has_plane:
            if t == 0:
                for i, m in enumerate(self.masks):
                    p.start(self.corecopy, i, m)
                    if self.sums is not None:
                        self.load(i, m).start()
            if t == 1:
                for i, m in enumerate(self.masks):
                    if self.sums is not None:
                        self.load(i, m).wait()
                    self.corecopy(i, m).wait_recv()
                    self.add(self.sum(m), self.core.at[i])
            j = t - 1
            if 1 <= j <= nx:
                for half, m, bit, slot in self.plane(j - 1):
                    self.planecopy(half, m, bit, slot).wait_recv()
                    self.add(self.rows(m, half), self.flat.at[slot])
            if 0 <= j < nx:
                for half, m, bit, slot in self.plane(j):
                    p.start(self.planecopy, half, m, bit, slot)
        if self.has_line:
            if 1 <= s <= self.zsteps:
                self.zwait(s)
            if 0 <= s < self.zsteps:
                self.zstart(s + 1)
            if t == self.stages - 1:
                self.finish()

    def finish(self):
        p = self.p
        if self.paired:
            mine = (2 * p.k == p.z) | (2 * p.k + 1 == p.z)
            own = lax.rem(p.z, 2)
            terms = [(self.got.at[t], lax.div(p.z, 2) + t * p.half != p.z) for t in (0, 1)]
        else:
            mine = None
            own = p.z
            n = p.nz
            terms = [(self.got.at[n - 2], p.z > 0), (self.got.at[2 * n - 3], p.z < n - 1)]
        source = self.column(own)

        def first(at):
            value = source[at].astype(F32)
            self.share[at] = value if mine is None else jnp.where(mine, value, 0.0)

        rowwise(self.r, 16, first)
        for ref, ok in terms:

            @pl.when(ok)
            def _(ref=ref):
                def more(at):
                    self.share[at] = self.share[at] + ref[at].astype(F32)

                rowwise(self.r, 16, more)


def perform(steps):
    for step in steps:
        if callable(step):
            step()
        else:
            step[0].stage(step[1])


def normalise(v):
    centred = v - jnp.mean(v, 1, keepdims=True)
    scale = lax.rsqrt(jnp.mean(centred * centred, 1, keepdims=True) + EPSILON)
    return centred * scale, scale


def norm_back(g, v, gain, gain_sum, shift_sum):
    n, scale = normalise(v)
    fold = lambda a: sum(a[i * 8 : (i + 1) * 8] for i in range(a.shape[0] // 8))
    gain_sum[...] += fold(g * n)
    shift_sum[...] += fold(g)
    gg = g * gain
    return (gg - jnp.mean(gg, 1, keepdims=True) - n * jnp.mean(gg * n, 1, keepdims=True)) * scale


def own_half(value, i):
    lane = lax.broadcasted_iota(jnp.int32, value.shape, 1)
    return jnp.where((lane >= HEAD_DIM) if i else (lane < HEAD_DIM), value, jnp.zeros_like(value))


def merge_halves(a, b):
    lane = lax.broadcasted_iota(jnp.int32, a.shape, 1)
    return jnp.where(lane < HEAD_DIM, a, b)


def project(normed, weight, qkv, pz):
    c = pz * 128
    rows = normed.shape[0]
    for j in (0, 1):
        for t in range(3):
            for i in range(rows // 512):
                at = pl.ds(i * 512, 512)
                y = nn(normed[at, :], weight[:, pl.ds((j * 3 + t) * c, c)])
                if t == 0:
                    y = y.astype(BF16).astype(F32) * HEAD_DIM**-0.5
                for w in range(pz):
                    qkv[t, j * pz + w, at, :] = y[:, w * 128 : (w + 1) * 128].astype(BF16)


def distances(dist, length):
    rows, cols = dist.shape

    def body(i, carry):
        row = lax.broadcasted_iota(jnp.int32, (64, cols), 0) + i * 64
        col = lax.broadcasted_iota(jnp.int32, (64, cols), 1)
        gap = jnp.abs(row - col).astype(F32)
        dist[part(i, 64), :] = jnp.where(col < length, gap, 1e33)
        return carry

    lax.fori_loop(0, rows // 64, body, 0)


def forward_tile(qkv, dist, pair, first_head, at, store):
    q, k, v = qkv[0, pair, at, :], qkv[1, pair], qkv[2, pair]
    gap = dist[at, :]
    outs = []
    for i in range(2):
        head = (first_head + 2 * pair + i + 1).astype(F32)
        slope = jnp.exp2(jnp.full((1, 1), -8.0 / HEADS, F32) * head) * LOG2E
        x = nt(own_half(q, i), k) * LOG2E - gap * slope
        e = jnp.exp2(x - jnp.max(x, 1, keepdims=True))
        p = (e * (1.0 / jnp.sum(e, 1, keepdims=True))).astype(BF16)
        store(i, p)
        outs.append(nn(p, v))
    return merge_halves(*outs).astype(BF16)


def backward_tile(qkv, do, do_t, q_t, pair, probs, dk, dv):
    k, v = qkv[1, pair], qkv[2, pair]
    dq = []
    for i in range(2):
        p = probs(i)
        rows = pl.ds(i * HEAD_DIM, HEAD_DIM)
        t = p.astype(F32) * nt(own_half(do, i), v)
        ds = (t - p.astype(F32) * jnp.sum(t, 1, keepdims=True)).astype(BF16)
        dq.append(nn(ds, k))
        dv[rows, :] += nn(do_t[rows, :], p)
        dk[rows, :] += nn(q_t[rows, :], ds)
    return (merge_halves(*dq) * HEAD_DIM**-0.5).astype(BF16)


def forward_kernel(
    nb, nz, lengths, x, skip_x, norms, skip_w, qkv_w, out_w, ff_w,
    mixed_out, normed_out, norms_out, skip_out, qkvw_out, out_out, ff0_out, ff1_out, ff2_out, qkv_out, probs, attended_out,
    skip, qkvw, joined, mixed, normed, everything, gains, qkv, dist, pbuf, attended,
    load, norm_send, norm_recv, swap_send, swap_recv, flush, psem, att_send, att_recv, *rest,
):
    place = Place(nb, nz)
    z, group, k, half = place.z, place.group, place.k, place.half
    frames = x.shape[0] // 2
    width = x.shape[1]
    keys = nz * frames
    c = norms.shape[1]
    pz = c // 128
    pairs = 2 * pz
    place.greet()

    jobs = [rest[3 * i : 3 * i + 3] for i in range(6)]
    skip_job = Gather(place, skip_w, skip, jobs[0])
    qkv_job = Gather(place, qkv_w, qkvw, jobs[1], True)
    out_job = Gather(place, out_w, out_out, jobs[2])
    ff = [Gather(place, ff_w.at[i], o, jobs[3 + i]) for i, o in enumerate((ff0_out, ff1_out, ff2_out))]
    last = nz - 1
    go = lambda job, *stages: [job.stage(t) for t in stages if t < job.stages]

    go(skip_job, 0)
    loads = [
        pltpu.make_async_copy(x, joined.at[:, pl.ds(0, width)], load.at[0]),
        pltpu.make_async_copy(skip_x, joined.at[:, pl.ds(width, width)], load.at[1]),
        pltpu.make_async_copy(norms, gains.at[:, part(z, c)], load.at[2]),
    ]
    for one in loads:
        one.start()
    norm_copy = lambda r: remote(
        norms, gains.at[:, part(z, c)], norm_send.at[r - 1], norm_recv.at[r - 1], (place.b, lax.rem(z + r, nz))
    )
    for r in range(1, nz):
        place.start(norm_copy, r)
    go(skip_job, *range(1, last))
    go(qkv_job, 0)
    distances(dist, lengths[group])
    go(skip_job, last)
    go(out_job, 0)
    go(skip_job, last + 1)
    go(out_job, *range(1, last))
    go(ff[0], 0, 1)
    go(skip_job, last + 2)
    go(qkv_job, 1)
    go(out_job, last)
    go(ff[0], 2)
    for t in range(last + 3, skip_job.stages):
        go(skip_job, t)
    flushes = []

    def out_copy(src, dst):
        copy = pltpu.make_async_copy(src, dst, flush.at[len(flushes)])
        flushes.append(copy)
        copy.start()

    out_copy(skip, skip_out)
    for one in loads:
        one.wait()
    for r in range(1, nz):
        norm_copy(r).wait_recv()
    out_copy(gains, norms_out)

    def across():
        return remote(
            normed.at[1 - group], everything.at[part(z, frames)], swap_send.at[0], swap_recv.at[0],
            (place.b, place.partner),
        )

    for turn in (0, 1):
        item = 1 - group if turn == 0 else group
        rows = part(item, frames)
        mixed[rows, :] = nn(joined[rows, :], skip[...])
        gain, shift = gains[0:1, :], gains[1:2, :]

        def body(i, carry):
            at = part(i, 32)
            at2 = pl.ds(pl.multiple_of(item * frames + i * 32, 32), 32)
            n, _ = normalise(mixed[at2, :])
            normed[item, at, :] = (n * gain + shift).astype(BF16)
            return carry

        lax.fori_loop(0, frames // 32, body, 0)
        if turn == 0:
            place.start(across)
            go(qkv_job, 2)
            go(out_job, last + 1)
            for t in range(3, last + 1):
                go(ff[0], t)
        else:
            own = pltpu.make_async_copy(normed.at[item], everything.at[part(z, frames)], load.at[0])
            own.start()

    def mate_copy(src, block, r, sem):
        return remote(
            src, everything.at[part(block, frames)], swap_send.at[sem], swap_recv.at[sem], (place.b, place.mate(r))
        )

    for r in range(1, half):
        place.start(mate_copy, normed.at[group], z, r, r)
    out_copy(mixed, mixed_out)
    go(ff[1], 0, 1)
    go(qkv_job, 3)
    go(out_job, last + 2)
    across().wait_recv()
    for r in range(1, half):
        block = everything.at[part(place.partner, frames)]
        place.start(mate_copy, block, place.partner, r, half - 1 + r)
    go(ff[1], 2)
    go(ff[0], last + 1)
    for t in range(3, last + 1):
        go(ff[1], t)
    go(qkv_job, *range(4, qkv_job.stages))
    go(out_job, *range(last + 3, out_job.stages))
    out_copy(qkvw, qkvw_out)
    go(ff[2], 0)
    go(ff[0], last + 2)
    own.wait()
    for r in range(1, half):
        mate_copy(normed.at[group], z, r, r).wait_recv()
        mate_copy(normed.at[group], z, r, half - 1 + r).wait_recv()
    out_copy(everything, normed_out)
    go(ff[2], 1)

    project(everything, qkvw, qkv, pz)
    out_copy(qkv, qkv_out)
    first_head = k * 2 * pairs
    blocks = keys // QUERIES
    total = pairs * blocks

    def probs_copy(slot, pair, at):
        return pltpu.make_async_copy(pbuf.at[slot], probs.at[pair, :, at], psem.at[slot])

    def att_copy(pair, r):
        owner = lax.rem(z + r, nz)
        slot = pair * (nz - 1) + r - 1
        return remote(
            attended.at[pair, part(owner, frames)],
            attended_out.at[part(group, frames), part(k * pairs + pair, 128)],
            att_send.at[slot], att_recv.at[slot], (place.b, owner),
        )

    def att_own(pair):
        return pltpu.make_async_copy(
            attended.at[pair, part(z, frames)],
            attended_out.at[part(group, frames), part(k * pairs + pair, 128)],
            flush.at[len(flushes)],
        )

    hooks = {}

    def hook(it, *steps):
        hooks.setdefault(min(it, total - 1), []).extend(steps)

    rest_of = lambda job, t: [(job, s) for s in range(t, job.stages)]
    hook(0, *[(ff[2], t) for t in range(2, last)], (ff[1], last + 1))
    hook(total // 8, (ff[2], last), *rest_of(ff[0], last + 3))
    hook(total * 3 // 8, (ff[1], last + 2), (ff[2], last + 1))
    hook(total * 6 // 8, *rest_of(ff[1], last + 3))
    hook(total * 7 // 8, (ff[2], last + 2))

    def body(it, carry):
        pair, q = lax.div(it, blocks), lax.rem(it, blocks)
        at, slot = part(q, QUERIES), lax.rem(it, 2)
        for when, steps in hooks.items():
            pl.when(it == when)(lambda steps=steps: perform(steps))

        @pl.when(it >= 2)
        def _():
            probs_copy(slot, pair, at).wait()

        def store(i, p):
            pbuf[slot, i] = p

        attended[pair, at, :] = forward_tile(qkv, dist, pair, first_head, at, store)
        probs_copy(slot, pair, at).start()

        @pl.when(q == blocks - 1)
        def _():
            for r in range(1, nz):
                att_copy(pair, r).start()

        return carry

    lax.fori_loop(0, total, body, 0)
    for pair in range(pairs):
        att_own(pair).start()
    go(ff[2], *range(last + 3, ff[2].stages))
    for pair in range(pairs):
        for r in range(1, nz):
            att_copy(pair, r).wait()
    for pair in range(pairs):
        att_own(pair).wait()
    for slot in range(min(2, total)):
        probs_copy(slot, 0, pl.ds(0, QUERIES)).wait()
    for copy in flushes:
        copy.wait()
    place.drain()


def forward(nb, nz, lengths, x, skip_x, norms, skip_w, qkv_w, out_w, ff_w):
    rows, width = x.shape
    frames = rows // 2
    keys = nz * frames
    pairs = 2 * norms.shape[1] // 128
    S, V, D = jax.ShapeDtypeStruct, pltpu.VMEM, pltpu.SemaphoreType.DMA
    full = lambda w, n: (nb * w.shape[0], n * w.shape[1])
    out_shape = [
        S((rows, width), F32),
        S((keys, width), BF16),
        S((norms.shape[0], width), F32),
        S(full(skip_w, nz), BF16),
        S(full(qkv_w, 2), BF16),
        S(full(out_w, nz), BF16),
        *[S((nb * ff_w.shape[1], nz * ff_w.shape[2]), BF16)] * 3,
        S((3, pairs, keys, 128), BF16),
        S((pairs, 2, keys, keys), BF16),
        S((rows, width), BF16),
    ]
    scratch = [
        V(full(skip_w, nz), BF16),
        V(full(qkv_w, 2), BF16),
        V((rows, 2 * width), BF16),
        V((rows, width), F32),
        V((2, frames, width), BF16),
        V((keys, width), BF16),
        V((norms.shape[0], width), F32),
        V((3, pairs, keys, 128), BF16),
        V((keys, keys), F32),
        V((2, 2, QUERIES, keys), BF16),
        V((pairs, keys, 128), BF16),
    ]
    scratch += [D((3,)), D((nz - 1,)), D((nz - 1,)), D((nz - 1,)), D((nz - 1,)), D((8,)), D((2,))]
    scratch += [D((pairs * (nz - 1),)), D((pairs * (nz - 1),))]
    for _ in range(6):
        scratch += Gather.scratch(nb, nz)
    return pl.pallas_call(
        functools.partial(forward_kernel, nb, nz),
        out_shape=out_shape,
        in_specs=[pl.BlockSpec(memory_space=pltpu.SMEM)] + [ANY] * 7,
        out_specs=[ANY] * len(out_shape),
        scratch_shapes=scratch,
        compiler_params=pltpu.CompilerParams(
            collective_id=0, has_side_effects=True, vmem_limit_bytes=VMEM_LIMIT
        ),
    )(lengths, x, skip_x, norms, skip_w, qkv_w, out_w, ff_w)


def ffn_kernel(
    nb, nz, mixed_in, attended_in, out_in, norms, cot_in, ff0, ff1, ff2, ff_w,
    output_out, middle_out, att_out, out_grad, part0, part1, grad2, grad3, sums, ff3,
    middle, attended, out_t, cot, weights, grads, ffn_in, ffn_in_t, cot_t, acc, gacc, low,
    load, wload, flush, *rest,
):
    place = Place(nb, nz)
    rows, d = mixed_in.shape
    r = grads.shape[2]
    cw = ff_w.shape[2] // 2
    subs = nz // 2
    total = 4 * subs
    place.greet()
    gather = Gather(place, ff_w.at[3], ff3, rest[:3])
    per = (len(rest) - 3) // 2
    jobs = [
        Scatter(place, grads.at[i], None, rest[3 + i * per : 3 + (i + 1) * per], sums=False, line=False) for i in (0, 1)
    ]
    go = lambda job, *stages: [job.stage(t) for t in stages if t < job.stages]
    last = nz - 1
    go(gather, 0)
    loads = [
        pltpu.make_async_copy(src, dst, load.at[i])
        for i, (src, dst) in enumerate(
            ((attended_in, attended), (out_in, out_t), (mixed_in, middle), (cot_in, cot))
        )
    ]
    weight_load = lambda i: pltpu.make_async_copy((ff0, ff1, ff2, ff3)[i], weights.at[i % 2], wload.at[i % 2])
    for one in loads:
        one.start()
    weight_load(0).start()
    weight_load(1).start()
    gain, shift = norms[2:3, :], norms[3:4, :]
    for one in loads[:3]:
        one.wait()
    acc[...] = nt(attended[...], out_t[...])
    go(gather, 1)

    def enter(at):
        v = middle[at, :] + acc[at, :]
        middle[at, :] = v
        n, _ = normalise(v)
        ffn_in[at, :] = (n * gain + shift).astype(BF16)
        acc[at, :] = v
        gacc[at, :] = jnp.zeros_like(v)

    rowwise(rows, 32, enter)
    ffn_in_t[...] = ffn_in[...].T
    loads[3].wait()
    cot_t[...] = cot[...].T
    go(gather, *range(2, last))
    weight_load(0).wait()

    hooks = {}

    def hook(it, *steps):
        hooks.setdefault(min(it, total - 1), []).extend(steps)

    rest_of = lambda job, t: [(job, s) for s in range(t, job.stages)]
    hook(total // 8, (gather, last))
    hook(total * 2 // 8, lambda: weight_load(1).wait(), lambda: weight_load(2).start(), (gather, last + 1), (jobs[0], 0))
    hook(total * 3 // 8, (jobs[0], 1))
    hook(total * 4 // 8, lambda: weight_load(2).wait(), (gather, last + 2), (jobs[1], 0))
    hook(total * 5 // 8, *rest_of(gather, last + 3), lambda: weight_load(3).start(), (jobs[1], 1))
    hook(total * 6 // 8, lambda: weight_load(3).wait(), (jobs[0], 2), lambda: flush_copy(0).start())
    hook(total * 7 // 8, *rest_of(jobs[0], 3), (jobs[1], 2))

    def flush_copy(i):
        pairs = (
            (grads.at[2], grad2), (grads.at[3], grad3), (grads.at[0, 0], part0), (grads.at[1, 0], part1),
            (low, output_out), (gacc, middle_out), (attended, att_out),
        )
        return pltpu.make_async_copy(*pairs[i], flush.at[i])

    def body(it, carry):
        for when, steps in hooks.items():
            pl.when(it == when)(lambda steps=steps: perform(steps))
        chunk, sub = lax.div(it, subs), lax.rem(it, subs)
        slot = lax.rem(chunk, 2)
        first = [(2 * sub + i) * 2 for i in (0, 1)]
        up = jnp.concatenate([weights[slot, :, part(f, cw)] for f in first], 1)
        dn = jnp.concatenate([weights[slot, :, part(f + 1, cw)] for f in first], 1)
        hidden = nn(ffn_in[...], up)
        active_grad = nn(cot[...], dn)
        cdf = 0.5 * (1.0 + lax.erf(hidden * 0.7071067811865476))
        active = (hidden * cdf).astype(BF16)
        density = jnp.exp2(hidden * hidden * (-0.5 * LOG2E)) * 0.3989422804014327
        hidden_grad = (active_grad * (cdf + hidden * density)).astype(BF16)
        acc[...] += nt(active, dn)
        gacc[...] += nt(hidden_grad, up)
        up_grad = nn(ffn_in_t[...], hidden_grad).astype(BF16)
        dn_grad = nn(cot_t[...], active).astype(BF16)
        for j in range(nb):
            m = flip(place.b, j)
            block = slice(j * r, (j + 1) * r)
            for i in (0, 1):
                cols = slice(i * cw, (i + 1) * cw)
                grads[chunk, m, :, part(first[i], cw)] = up_grad[block, cols]
                grads[chunk, m, :, part(first[i] + 1, cw)] = dn_grad[block, cols]
        return carry

    lax.fori_loop(0, total, body, 0)
    flush_copy(1).start()
    flush_copy(2).start()
    sums[...] = jnp.zeros_like(sums)

    def leave(at):
        low[at, :] = acc[at, :].astype(BF16)
        back = norm_back(gacc[at, :], middle[at, :], gain, sums.at[0], sums.at[1])
        grad = cot[at, :].astype(F32) + back
        gacc[at, :] = grad
        ffn_in[at, :] = grad.astype(BF16)

    rowwise(rows, 32, leave)
    flush_copy(4).start()
    flush_copy(5).start()
    grad_t = ffn_in[...].T
    for j in range(nb):
        out_grad[flip(place.b, j)] = nn(grad_t[j * r : (j + 1) * r, :], attended[...]).astype(BF16)
    attended[...] = nn(ffn_in[...], out_t[...]).astype(BF16)
    flush_copy(6).start()
    go(jobs[1], *range(3, jobs[1].stages))
    flush_copy(3).start()
    for i in range(7):
        flush_copy(i).wait()
    place.drain()


def ffn(nb, nz, mixed, attended, out_t, norms, cot, ff0, ff1, ff2, ff_w):
    rows, d = mixed.shape
    _, r, width = ff_w.shape
    wide = nz * width
    V, S, D = pltpu.VMEM, jax.ShapeDtypeStruct, pltpu.SemaphoreType.DMA
    scratch = [
        V((rows, d), F32),
        V((rows, d), BF16),
        V((d, d), BF16),
        V((rows, d), BF16),
        V((2, d, wide), BF16),
        V((4, nb, r, wide), BF16),
        V((rows, d), BF16),
        V((d, rows), BF16),
        V((d, rows), BF16),
        V((rows, d), F32),
        V((rows, d), F32),
        V((rows, d), BF16),
        D((4,)), D((2,)), D((7,)),
    ]
    scratch += Gather.scratch(nb, nz)
    for _ in range(2):
        scratch += Scatter.scratch(nb, nz, r, wide, sums=False, line=False)
    return pl.pallas_call(
        functools.partial(ffn_kernel, nb, nz),
        out_shape=[
            S((rows, d), BF16),
            S((rows, d), F32),
            S((rows, d), BF16),
            S((nb, r, d), BF16),
            *[S((r, wide), BF16)] * 2,
            *[S((nb, r, wide), BF16)] * 2,
            S((2, 8, d), F32),
            S((d, wide), BF16),
        ],
        in_specs=[ANY] * 3 + [WHOLE] + [ANY] * 5,
        out_specs=[ANY] * 3 + [WHOLE] + [ANY] * 4 + [WHOLE, ANY],
        scratch_shapes=scratch,
        compiler_params=pltpu.CompilerParams(
            collective_id=3, has_side_effects=True, vmem_limit_bytes=VMEM_LIMIT
        ),
    )(mixed, attended, out_t, norms, cot, ff0, ff1, ff2, ff_w)


def attention_kernel(
    nb, nz, att_grad, qkv_in, probs, part0, part1, grad2, grad3, out_grad,
    dqkv, ff_share, out_share,
    qkv, dout, pbuf, dk, dv, q_t, do_t, load, psem, att_send, att_recv, *rest,
):
    place = Place(nb, nz)
    z, group, k = place.z, place.group, place.k
    pairs, keys = qkv.shape[1], qkv.shape[2]
    frames = keys // nz
    wide = pairs * 128
    pz = pairs // 2
    place.greet()

    def att_copy(r):
        owner = lax.rem(z + r, nz)
        item, member = lax.div(owner, place.half), lax.rem(owner, place.half)
        return remote(
            att_grad.at[part(item, frames), part(member, wide)], dout.at[part(z, frames)],
            att_send.at[r - 1], att_recv.at[r - 1], (place.b, owner),
        )

    for r in range(1, nz):
        place.start(att_copy, r)
    own = pltpu.make_async_copy(att_grad.at[part(group, frames), part(k, wide)], dout.at[part(z, frames)], load.at[0])
    own.start()
    qkv_load = pltpu.make_async_copy(qkv_in, qkv, load.at[1])
    qkv_load.start()
    rest = list(rest)

    def job(full, share, **kind):
        count = 3 + sum(kind.get(key, True) and size for key, size in (("sums", 1), ("plane", 2), ("line", 1)))
        mine = [rest.pop(0) for _ in range(count)]
        return Scatter(place, full, share, mine, **kind)

    early = [job(None, ff_share.at[i], plane=False) for i in (0, 1)]
    late = [job(g, ff_share.at[2 + i]) for i, g in enumerate((grad2, grad3))]
    out_job = job(out_grad, out_share)
    go = lambda job, *stages: [job.stage(t) for t in stages if t < job.stages]
    early_loads = [
        pltpu.make_async_copy(p, e.sums.at[0], load.at[2 + i]) for i, (p, e) in enumerate(zip((part0, part1), early))
    ]
    for one in early_loads:
        one.start()
    go(late[0], 0)
    go(late[1], 0)
    go(out_job, 0)
    go(late[0], 1)
    own.wait()
    qkv_load.wait()

    blocks = keys // QUERIES
    total = pairs * blocks

    def probs_copy(it):
        slot = lax.rem(it, 2)
        pair, q = lax.div(it, blocks), lax.rem(it, blocks)
        return pltpu.make_async_copy(probs.at[pair, :, part(q, QUERIES)], pbuf.at[slot], psem.at[slot])

    probs_copy(0).start()
    for r in range(1, nz):
        att_copy(r).wait_recv()
    hooks = {}

    def hook(it, *steps):
        hooks.setdefault(min(it, total - 1), []).extend(steps)

    zs = place.nz - 1
    rest_of = lambda job, t: [(job, s) for s in range(t, job.stages)]
    hook(0, (late[1], 1), *[lambda one=one: one.wait() for one in early_loads], (early[0], 0), (early[1], 0))
    hook(total // 8, (late[0], 2), (early[0], 1), (early[1], 1))
    hook(total * 2 // 8, (out_job, 1), *[(early[0], t) for t in range(2, zs)], *[(early[1], t) for t in range(2, zs)])
    hook(total * 3 // 8, (late[1], 2), (early[0], zs), (early[1], zs))
    hook(total * 4 // 8, (late[0], 3))
    hook(total * 5 // 8, (out_job, 2), (late[0], 4))
    hook(total * 6 // 8, (late[1], 3), (late[0], 5))
    hook(total * 7 // 8, (late[1], 4), (out_job, 3))

    def body(it, carry):
        pair, q = lax.div(it, blocks), lax.rem(it, blocks)
        at, slot = part(q, QUERIES), lax.rem(it, 2)
        for when, steps in hooks.items():
            pl.when(it == when)(lambda steps=steps: perform(steps))

        @pl.when(it + 1 < total)
        def _():
            probs_copy(it + 1).start()

        probs_copy(it).wait()

        @pl.when(q == 0)
        def _():
            dk[...] = jnp.zeros_like(dk)
            dv[...] = jnp.zeros_like(dv)

        do = dout[at, part(pair, 128)]
        q_t[...] = qkv[0, pair, at, :].T
        do_t[...] = do.T
        block = lax.div(pair, pz)
        column = lambda t: part((block * 3 + t) * pz + lax.rem(pair, pz), 128)
        dqkv[at, column(0)] = backward_tile(qkv, do, do_t, q_t, pair, lambda i: pbuf[slot, i], dk, dv)

        @pl.when(q == blocks - 1)
        def _():
            dqkv[:, column(1)] = dk[...].T.astype(BF16)
            dqkv[:, column(2)] = dv[...].T.astype(BF16)

        return carry

    lax.fori_loop(0, total, body, 0)
    for t in range(4, out_job.stages + 1):
        go(out_job, t)
        go(late[1], t + 1)
        go(late[0], t + 2)
    place.drain()


def attention_back(nb, nz, att_grad, qkv, probs, part0, part1, grad2, grad3, out_grad):
    _, pairs, keys, _ = qkv.shape
    S, V, D = jax.ShapeDtypeStruct, pltpu.VMEM, pltpu.SemaphoreType.DMA
    _, r, wide = grad2.shape
    scratch = [
        V((3, pairs, keys, 128), BF16),
        V((keys, pairs * 128), BF16),
        V((2, 2, QUERIES, keys), BF16),
        V((128, keys), F32),
        V((128, keys), F32),
        V((128, QUERIES), BF16),
        V((128, QUERIES), BF16),
        D((4,)), D((2,)), D((nz - 1,)), D((nz - 1,)),
    ]
    for _ in range(2):
        scratch += Scatter.scratch(nb, nz, r, wide, plane=False)
    for g in (grad2, grad3, out_grad):
        scratch += Scatter.scratch(nb, nz, r, g.shape[2])
    return pl.pallas_call(
        functools.partial(attention_kernel, nb, nz),
        out_shape=[
            S((keys, 3 * pairs * 128), BF16),
            S((4, r, wide // nz), F32),
            S((r, out_grad.shape[2] // nz), F32),
        ],
        in_specs=[ANY] * 8,
        out_specs=[WHOLE] * 3,
        scratch_shapes=scratch,
        compiler_params=pltpu.CompilerParams(
            collective_id=1, has_side_effects=True, vmem_limit_bytes=VMEM_LIMIT
        ),
    )(att_grad, qkv, probs, part0, part1, grad2, grad3, out_grad)


def first_kernel(
    nb, nz, dqkv, everything, qkvw, x, skip_x, skip_w, mixed, middle_grad, norms, second_sums,
    input_grad, skip_grad, qkv_share, skip_share, norm_share,
    qkv_grad, skip_w_grad, weight, joined, joined_t, mixed_low, ahead, mine, from_mate, to_partner, from_partner,
    sums, packed, norm_in, norm_line, load, swap_send, swap_recv, norm_send, norm_recv, *rest,
):
    place = Place(nb, nz)
    z, group, k, half = place.z, place.group, place.k, place.half
    frames = x.shape[0] // 2
    width = x.shape[1]
    per = len(rest) // 2
    place.greet()
    qkv_job = Scatter(place, qkv_grad, qkv_share, rest[:per], True, sums=False)
    skip_job = Scatter(place, skip_w_grad, skip_share, rest[per:], sums=False)
    loads = [
        pltpu.make_async_copy(x, joined.at[:, pl.ds(0, width)], load.at[0]),
        pltpu.make_async_copy(skip_x, joined.at[:, pl.ds(width, width)], load.at[1]),
        pltpu.make_async_copy(skip_w, weight, load.at[2]),
    ]
    for one in loads:
        one.start()

    def mate_copy(r, t):
        slot = (r - 1) * 2 + t
        return remote(
            ahead.at[slot], from_mate.at[slot], swap_send.at[slot], swap_recv.at[slot], (place.b, place.mate(r))
        )

    for r in range(1, half):
        for s in (0, 1):
            block = lax.rem(k + r, half) + (1 - group if s == 0 else group) * half
            ahead[(r - 1) * 2 + s] = nt(dqkv[part(block, frames), :], qkvw[...]).astype(BF16)
        place.start(mate_copy, r, 0)
    for s in (0, 1):
        block = k + (1 - group if s == 0 else group) * half
        mine[s] = nt(dqkv[part(block, frames), :], qkvw[...])
    turned = everything[...].T
    rq = qkv_grad.shape[1]
    for j in range(nb):
        qkv_grad[flip(place.b, j)] = nn(turned[j * rq : (j + 1) * rq, :], dqkv[...]).astype(BF16)
    qkv_job.stage(0)

    def add_mates(s):
        for r in range(1, half):
            mate_copy(r, s).wait_recv()
            slot = (r - 1) * 2 + s

            def body(at):
                mine[s, at] = mine[s, at] + from_mate[slot, at].astype(F32)

            rowwise(frames, 16, body)

    add_mates(0)
    sem = 2 * (half - 1)
    across = lambda: remote(to_partner, from_partner, swap_send.at[sem], swap_recv.at[sem], (place.b, place.partner))

    def narrow(at):
        to_partner[at] = mine[0, at].astype(BF16)

    rowwise(frames, 16, narrow)
    place.start(across)
    for r in range(1, half):
        place.start(mate_copy, r, 1)
    for one in loads:
        one.wait()
    joined_t[...] = joined[...].T
    qkv_job.stage(1)

    sums[...] = jnp.zeros_like(sums)
    gain = norms[0:1, :]

    def back(item, grad):
        def body(i, carry):
            at = part(i, 32)
            to = pl.ds(pl.multiple_of(item * frames + i * 32, 32), 32)
            part_grad = norm_back(grad(at), mixed[to, :], gain, sums.at[0], sums.at[1])
            mixed_low[to, :] = (middle_grad[to, :] + part_grad).astype(BF16)
            return carry

        lax.fori_loop(0, frames // 32, body, 0)

    add_mates(1)
    back(group, lambda at: mine[1, at])
    across().wait_recv()
    back(1 - group, lambda at: from_partner[at].astype(F32))
    rs = skip_w_grad.shape[1]
    for j in range(nb):
        skip_w_grad[flip(place.b, j)] = nn(joined_t[j * rs : (j + 1) * rs, :], mixed_low[...]).astype(BF16)
    skip_job.stage(0)

    total = lambda a: jnp.sum(a, 0, keepdims=True)
    for i, v in enumerate((sums[0], sums[1], second_sums[0], second_sums[1])):
        packed[i : i + 1, :] = total(v)
    packed[4:8, :] = jnp.zeros_like(packed[4:8, :])
    bits = [0] + place.rest
    norm_copy = lambda i: remote(
        packed, norm_in.at[i], norm_send.at[i], norm_recv.at[i], place.at(1 << bits[i])
    )
    c = norm_share.shape[1]
    line_copy = lambda r: remote(
        packed.at[:, part(lax.rem(z + r, nz), c)], norm_line.at[r - 1],
        norm_send.at[len(bits) + r - 1], norm_recv.at[len(bits) + r - 1], (place.b, lax.rem(z + r, nz)),
    )

    def norm_step(i):
        if i > 0:
            norm_copy(i - 1).wait()
            packed[...] = packed[...] + norm_in[i - 1]
        if i < len(bits):
            norm_copy(i).start()
        else:
            for r in range(1, nz):
                line_copy(r).start()

    norm_step(0)
    skip_job.stage(1)
    norm_step(1)
    qkv_job.stage(2)
    for t in range(2):
        (input_grad, skip_grad)[t][...] = nt(mixed_low[...], weight[pl.ds(t * width, width), :])
        norm_step(2 + t)
    for i in range(4, len(bits) + 1):
        norm_step(i)
    skip_job.stage(2)
    qkv_job.stage(3)
    for t in range(3, max(skip_job.stages, qkv_job.stages - 1)):
        if t < skip_job.stages:
            skip_job.stage(t)
        if t + 1 < qkv_job.stages:
            qkv_job.stage(t + 1)
    value = packed[:, part(z, c)]
    for r in range(1, nz):
        line_copy(r).wait()
        value = value + norm_line[r - 1]
    norm_share[...] = value
    place.drain()


def first_back(nb, nz, dqkv, everything, qkvw, x, skip_x, skip_w, mixed, middle_grad, norms, second_sums):
    rows, width = x.shape
    frames = rows // 2
    half = nz // 2
    c = width // nz
    S, V, D = jax.ShapeDtypeStruct, pltpu.VMEM, pltpu.SemaphoreType.DMA
    qkv_wide = qkvw.shape[1]
    bits = nb.bit_length() - 1
    swaps = 2 * (half - 1)
    scratch = [
        V((nb, qkvw.shape[0] // nb, qkv_wide), BF16),
        V((nb, skip_w.shape[0] // nb, width), BF16),
        V(skip_w.shape, BF16),
        V((rows, 2 * width), BF16),
        V((2 * width, rows), BF16),
        V((rows, width), BF16),
        V((max(swaps, 1), frames, width), BF16),
        V((2, frames, width), F32),
        V((max(swaps, 1), frames, width), BF16),
        V((frames, width), BF16),
        V((frames, width), BF16),
        V((2, 8, width), F32),
        V((8, width), F32),
        V((bits, 8, width), F32),
        V((nz - 1, 8, c), F32),
        D((3,)), D((swaps + 1,)), D((swaps + 1,)), D((bits + nz - 1,)), D((bits + nz - 1,)),
    ]
    scratch += Scatter.scratch(nb, nz, qkvw.shape[0] // nb, qkv_wide, True, sums=False)
    scratch += Scatter.scratch(nb, nz, skip_w.shape[0] // nb, width, sums=False)
    return pl.pallas_call(
        functools.partial(first_kernel, nb, nz),
        out_shape=[
            S((rows, width), F32),
            S((rows, width), F32),
            S((qkvw.shape[0] // nb, qkv_wide // 2), F32),
            S((skip_w.shape[0] // nb, c), F32),
            S((8, c), F32),
        ],
        in_specs=[WHOLE] * 3 + [ANY] * 3 + [WHOLE] * 4,
        out_specs=[WHOLE] * 5,
        scratch_shapes=scratch,
        compiler_params=pltpu.CompilerParams(
            collective_id=2, has_side_effects=True, vmem_limit_bytes=VMEM_LIMIT
        ),
    )(dqkv, everything, qkvw, x, skip_x, skip_w, mixed, middle_grad, norms, second_sums)


def shards(
    inputs,
    skip_input,
    lengths,
    skip_weight,
    query_weight,
    key_weight,
    value_weight,
    out_weight,
    up_weight,
    down_weight,
    first_gain,
    first_shift,
    second_gain,
    second_shift,
    cotangent,
):
    nb, nz = lax.axis_size("batch"), lax.axis_size("seq")
    shape = inputs.shape
    flat = lambda a: a.reshape(shape[0] * shape[1], shape[2])
    x, skip_x, cot = flat(inputs), flat(skip_input), flat(cotangent)
    norms = jnp.stack([first_gain, first_shift, second_gain, second_shift]).astype(F32)
    norms = jnp.pad(norms, ((0, 4), (0, 0)))
    qkv_shard = jnp.concatenate([query_weight, key_weight, value_weight], 1)
    cw = up_weight.shape[1] // 4
    chunks = lambda w: w.reshape(w.shape[0], 4, cw)
    ff_w = jnp.concatenate([chunks(up_weight), chunks(down_weight.T)], 2).transpose(1, 0, 2)
    (mixed, everything, gains, skip_w, qkvw, out_t, ff0, ff1, ff2, qkv, probs, attended) = forward(
        nb, nz, lengths, x, skip_x, norms, skip_weight, qkv_shard, out_weight.T, ff_w
    )
    output, middle_grad, att_grad, out_grad, part0, part1, grad2, grad3, second_sums, _ = ffn(
        nb, nz, mixed, attended, out_t, gains, cot, ff0, ff1, ff2, ff_w
    )
    dqkv, ff_share, out_share = attention_back(
        nb, nz, att_grad, qkv, probs, part0, part1, grad2, grad3, out_grad
    )
    up_share, dn_share = [
        ff_share[:, :, i * cw : (i + 1) * cw].transpose(1, 0, 2).reshape(up_weight.shape) for i in (0, 1)
    ]
    input_grad, skip_grad, qkv_share, skip_share, norm_share = first_back(
        nb, nz, dqkv, everything, qkvw, x, skip_x, skip_w, mixed, middle_grad, gains, second_sums
    )
    c = query_weight.shape[1]
    return (
        output.reshape(shape),
        input_grad.reshape(shape),
        skip_grad.reshape(shape),
        skip_share,
        qkv_share[:, :c],
        qkv_share[:, c : 2 * c],
        qkv_share[:, 2 * c :],
        out_share.T,
        up_share,
        dn_share.T,
        norm_share[0],
        norm_share[1],
        norm_share[2],
        norm_share[3],
    )


def solution(mesh):
    rows = P("batch", "seq", None)
    weight, turned, norm = P("batch", "seq"), P("seq", "batch"), P("seq")
    return jax.shard_map(
        shards,
        mesh=mesh,
        in_specs=(rows, rows, P("batch"), *[weight] * 4, turned, weight, turned, *[norm] * 4, rows),
        out_specs=(rows, rows, rows, *[weight] * 4, turned, weight, turned, *[norm] * 4),
        check_vma=False,
    )
```

```python
import functools

import jax
import jax.numpy as jnp
from jax import lax
from jax.experimental import pallas as pl
from jax.experimental.pallas import tpu as pltpu
from jax.sharding import PartitionSpec as P

HEADS = 16
HEAD_DIM = 64
EPSILON = 1e-05
LOG2E = 1.4426950408889634
QUERIES = 256
F32 = jnp.float32
BF16 = jnp.bfloat16
MESH = pl.DeviceIdType.MESH
VMEM_LIMIT = 60 * 2**20
ANY = pl.BlockSpec(memory_space=pl.ANY)
WHOLE = pl.BlockSpec(memory_space=pltpu.VMEM)


def nt(a, b):
    return lax.dot_general(a, b, (((1,), (1,)), ((), ())), preferred_element_type=F32)


def nn(a, b):
    return jnp.dot(a, b, preferred_element_type=F32)


def part(index, size):
    if isinstance(index, int):
        return pl.ds(index * size, size)
    return pl.ds(pl.multiple_of(index * size, size), size)


def rowwise(rows, step, body):
    def run(i, carry):
        body(part(i, step))
        return carry

    lax.fori_loop(0, rows // step, run, 0)


def flip(index, mask):
    result = index
    bit = 0
    while mask >> bit:
        if (mask >> bit) & 1:
            on = lax.rem(lax.div(index, 1 << bit), 2)
            result = result + (1 << bit) * (1 - 2 * on)
        bit += 1
    return result


def span(bits):
    masks = [0]
    for bit in bits:
        masks = masks + [m | (1 << bit) for m in masks]
    return masks


class Place:
    def __init__(self, nb, nz):
        self.nb, self.nz = nb, nz
        self.b = lax.axis_index("batch")
        self.z = lax.axis_index("seq")
        self.half = nz // 2
        self.group = lax.div(self.z, self.half)
        self.k = lax.rem(self.z, self.half)
        self.partner = lax.rem(self.z + self.half, nz)
        self.rest = list(range(1, nb.bit_length() - 1))
        self.orders = (self.rest, self.rest[::-1])
        self.pending = []

    def at(self, mask):
        return (flip(self.b, mask), self.z)

    def mate(self, r):
        return self.group * self.half + lax.rem(self.k + r, self.half)

    def greet(self):
        barrier = pltpu.get_barrier_semaphore()
        targets = [self.at(1 << k) for k in [0] + self.rest]
        targets += [(self.b, lax.rem(self.z + r, self.nz)) for r in range(1, self.nz)]
        for t in targets:
            pl.semaphore_signal(barrier, inc=1, device_id=t, device_id_type=MESH)
        pl.semaphore_wait(barrier, len(targets))

    def start(self, make, *args):
        copy, ok = self.unpack(make(*args))
        if ok is None:
            copy.start()
        else:
            pl.when(ok)(lambda: copy.start())
        self.pending.append((make, args))

    def drain(self):
        for make, args in self.pending:
            copy, ok = self.unpack(make(*args))
            if ok is None:
                copy.wait_send()
            else:
                pl.when(ok)(lambda copy=copy: copy.wait_send())
        self.pending = []

    @staticmethod
    def unpack(made):
        return made if isinstance(made, tuple) else (made, None)


def remote(src, dst, send, recv, device):
    return pltpu.make_async_remote_copy(
        src_ref=src, dst_ref=dst, send_sem=send, recv_sem=recv, device_id=device, device_id_type=MESH
    )


class Gather:
    @staticmethod
    def sems(nb, nz):
        return max(2 * (nz - 1), 6) + 2 * (nb // 2 - 1) + nb

    @staticmethod
    def scratch(nb, nz):
        count = Gather.sems(nb, nz)
        return [pltpu.SemaphoreType.DMA((3,))] + [pltpu.SemaphoreType.DMA((count,))] * 2

    def __init__(self, place, shard, full, scratch, paired=False, h=0, of=1):
        self.p, self.full, self.paired, self.h, self.of = place, full, paired, h, of
        self.shards = shard if paired else [shard]
        self.shard = self.shards[0]
        self.local, self.send, self.recv = scratch
        self.r, self.c = self.shard.shape
        nb, nz = place.nb, place.nz
        self.xy0 = max(2 * (nz - 1), 6)
        self.core0 = self.xy0 + 2 * (nb // 2 - 1)
        self.zsteps = 1 if paired else nz - 1
        self.stages = self.zsteps + len(place.rest) + 2

    def column(self, index):
        return self.full.at[part(self.p.b * self.of + self.h, self.r), part(index, self.c)]

    def line(self, way, step):
        p, n = self.p, self.p.nz
        sem = (0 if way > 0 else n - 1) + step - 1
        sent, got = p.z - way * (step - 1), p.z - way * step
        inside = lambda v: (v >= 0) & (v < n)
        clip = lambda v: jnp.clip(v, 0, n - 1)
        to = (p.b, clip(p.z + way))
        block = self.column(clip(sent))
        out = lambda: remote(self.shard if step == 1 else block, block, self.send.at[sem], self.recv.at[sem], to)
        land = self.column(clip(got))
        into = lambda: remote(land, land, self.send.at[sem], self.recv.at[sem], to)
        return out, into, inside(sent) & inside(p.z + way), inside(got)

    def zstart(self, step):
        p = self.p
        if self.paired:
            for t in (0, 1):
                for i in range(len(self.shards)):
                    p.start(self.paircopy, t, i)
            return
        for way in (1, -1):
            p.start(self.lineout, way, step)

    def lineout(self, way, step):
        out, _, can_send, _ = self.line(way, step)
        return out(), can_send

    def paircopy(self, t, i):
        p, count = self.p, len(self.shards)
        target = lax.div(p.z, 2) + t * p.half
        slot = lax.rem(p.z, 2) * count + i
        copy = remote(
            self.shards[i], self.column(slot), self.send.at[t * count + i], self.recv.at[slot], (p.b, target)
        )
        return copy, target != p.z

    def zwait(self, step):
        p = self.p
        if self.paired:
            for s in (0, 1):

                @pl.when(2 * p.k + s != p.z)
                def _(s=s):
                    for i in range(len(self.shards)):
                        slot = s * len(self.shards) + i
                        land = self.column(slot)
                        remote(land, land, self.send.at[slot], self.recv.at[slot], (p.b, p.partner)).wait_recv()

            return
        for way in (1, -1):
            _, into, _, can_get = self.line(way, step)
            pl.when(can_get)(lambda into=into: into().wait_recv())

    def owncopy(self, act):
        p, count = self.p, len(self.shards)
        place = lax.rem(p.z, 2) if self.paired else p.z
        copies = lambda: [
            pltpu.make_async_copy(shard, self.column(place * count + i), self.local.at[i])
            for i, shard in enumerate(self.shards)
        ]
        if self.paired:
            pl.when((2 * p.k == p.z) | (2 * p.k + 1 == p.z))(lambda: [act(copy) for copy in copies()][:0] or None)
        else:
            act(copies()[0])

    def rows(self, mask, half):
        h = self.r // 2
        return self.full.at[part((flip(self.p.b, mask) * self.of + self.h) * 2 + half, h)]

    def hop(self, sem, mask, half, bit, incoming):
        block = self.rows(mask | bit if incoming else mask, half)
        return remote(block, block, self.send.at[sem], self.recv.at[sem], self.p.at(bit))

    def plane(self, j):
        made = []
        for half in (0, 1):
            order = self.p.orders[half]
            for i, m in enumerate(span(order[:j])):
                sem = self.xy0 + half * (self.p.nb // 2 - 1) + (1 << j) - 1 + i
                made.append((half, m, 1 << order[j], sem))
        return made

    def coresem(self, mask, half):
        return self.core0 + (mask >> 1) * 2 + half

    def corestart(self, mask, half):
        self.p.start(self.hop, self.coresem(mask, half), mask, half, 1, False)

    def stage(self, t):
        p = self.p
        nx = len(p.rest)
        if t == 0:
            self.owncopy(lambda copy: copy.start())
            self.zstart(1)
        if 1 <= t <= self.zsteps:
            self.zwait(t)
            if t < self.zsteps:
                self.zstart(t + 1)
            else:
                self.owncopy(lambda copy: copy.wait())
        j = t - self.zsteps
        if 1 <= j <= nx:
            for half, m, bit, sem in self.plane(j - 1):
                self.hop(sem, m, half, bit, True).wait_recv()
        if 0 <= j < nx:
            for half, m, bit, sem in self.plane(j):
                p.start(self.hop, sem, m, half, bit, False)
        if j == 0:
            for half in (0, 1):
                self.corestart(0, half)
        if 1 <= j <= nx:
            for half, m, bit, _ in self.plane(j - 1):
                self.corestart(m | bit, half)
        if j == nx + 1:
            for m in span(p.rest):
                for half in (0, 1):
                    self.hop(self.coresem(m, half), m, half, 1, True).wait_recv()


class Scatter:
    @staticmethod
    def scratch(nb, nz, r, wide, paired=False, sums=True, plane=True, line=True):
        c = wide // (2 if paired else nz)
        lines = 2 if paired else 2 * (nz - 1)
        count = nb // 2 + 2 * (nb // 2 - 1) + lines
        made = [pltpu.VMEM((nb // 2 if plane else 1, r, wide), BF16)] if sums else []
        if plane:
            made += [
                pltpu.VMEM((nb // 2, r, wide), BF16),
                pltpu.VMEM((2 * (nb // 2 - 1), r // 2, wide), BF16),
            ]
        if line:
            made += [pltpu.VMEM((lines, r, c), BF16)]
        return made + [
            pltpu.SemaphoreType.DMA((nb // 2,)),
            pltpu.SemaphoreType.DMA((count,)),
            pltpu.SemaphoreType.DMA((count,)),
        ]

    def __init__(self, place, full, share, scratch, paired=False, sums=True, plane=True, line=True):
        self.p, self.full, self.share, self.paired = place, full, share, paired
        scratch = list(scratch)
        self.sums = scratch.pop(0) if sums else None
        self.core, self.flat = (scratch.pop(0), scratch.pop(0)) if plane else (None, None)
        self.got = scratch.pop(0) if line else None
        self.local, self.send, self.recv = scratch
        self.has_plane, self.has_line = plane, line
        _, self.r, self.wide = (full if plane else self.sums).shape
        self.c = self.wide // (2 if paired else place.nz)
        self.zsteps = 1 if paired else place.nz - 1
        self.nx = len(place.rest)
        self.plane_stages = 2 + self.nx
        self.stages = (self.plane_stages if plane else 1) + (self.zsteps if line else 0)
        self.zsem = place.nb // 2 + 2 * (place.nb // 2 - 1)
        self.masks = sorted(span(place.rest))

    def sum(self, m):
        return self.full.at[m] if self.sums is None else self.sums.at[m >> 1]

    def add(self, target, source):
        def body(at):
            target[at] = target[at] + source[at]

        rowwise(target.shape[0], 16, body)

    def corecopy(self, i, m):
        return remote(self.full.at[m | 1], self.core.at[i], self.send.at[i], self.recv.at[i], self.p.at(1))

    def load(self, i, m):
        return pltpu.make_async_copy(self.full.at[m], self.sum(m), self.local.at[i])

    def rows(self, m, half):
        return self.sum(m).at[part(half, self.r // 2)]

    def plane(self, j):
        p = self.p
        made = []
        for half in (0, 1):
            order = p.orders[half]
            base = half * (p.nb // 2 - 1) + sum(len(span(order[q + 1 :])) for q in range(j))
            for i, m in enumerate(span(order[j + 1 :])):
                made.append((half, m, 1 << order[j], base + i))
        return made

    def planecopy(self, half, m, bit, slot):
        sem = self.p.nb // 2 + slot
        return remote(
            self.rows(m | bit, half), self.flat.at[slot], self.send.at[sem], self.recv.at[sem], self.p.at(bit)
        )

    def column(self, index):
        return self.sum(0).at[:, part(index, self.c)]

    def line(self, way, step):
        p, n = self.p, self.p.nz
        here = p.z if way > 0 else n - 1 - p.z
        goes = n + here - step
        comes = goes - 1
        can_send = (goes > here) & (goes <= n - 1)
        can_get = (comes >= here) & (comes <= n - 1) & (here > 0)
        unfold = lambda d: jnp.clip(d if way > 0 else n - 1 - d, 0, n - 1)
        slot = (0 if way > 0 else n - 1) + step - 1
        copy = remote(
            self.column(unfold(goes)),
            self.got.at[slot],
            self.send.at[self.zsem + slot],
            self.recv.at[self.zsem + slot],
            (p.b, jnp.clip(p.z + way, 0, n - 1)),
        )
        return copy, can_send, can_get, unfold(comes), slot

    def paircopy(self, s):
        p = self.p
        copy = remote(
            self.column(s),
            self.got.at[p.group],
            self.send.at[self.zsem + s],
            self.recv.at[self.zsem + p.group],
            (p.b, 2 * p.k + s),
        )
        return copy, 2 * p.k + s != p.z

    def lineout(self, way, step):
        return self.line(way, step)[:2]

    def zstart(self, step):
        p = self.p
        if self.paired:
            for s in (0, 1):
                p.start(self.paircopy, s)
            return
        for way in (1, -1):
            p.start(self.lineout, way, step)

    def zwait(self, step):
        p = self.p
        if self.paired:
            for t in (0, 1):
                copy = remote(
                    self.column(0),
                    self.got.at[t],
                    self.send.at[self.zsem + t],
                    self.recv.at[self.zsem + t],
                    (p.b, p.partner),
                )
                pl.when(lax.div(p.z, 2) + t * p.half != p.z)(lambda copy=copy: copy.wait_recv())
            return
        for way in (1, -1):
            copy, _, can_get, column, slot = self.line(way, step)

            @pl.when(can_get)
            def _(copy=copy, column=column, slot=slot):
                copy.wait_recv()
                if step < self.zsteps:
                    self.add(self.column(column), self.got.at[slot])

    def stage(self, t):
        p, nx = self.p, self.nx
        s = t - (self.plane_stages - 1 if self.has_plane else 0)
        if self.has_plane:
            if t == 0:
                for i, m in enumerate(self.masks):
                    p.start(self.corecopy, i, m)
                    if self.sums is not None:
                        self.load(i, m).start()
            if t == 1:
                for i, m in enumerate(self.masks):
                    if self.sums is not None:
                        self.load(i, m).wait()
                    self.corecopy(i, m).wait_recv()
                    self.add(self.sum(m), self.core.at[i])
            j = t - 1
            if 1 <= j <= nx:
                for half, m, bit, slot in self.plane(j - 1):
                    self.planecopy(half, m, bit, slot).wait_recv()
                    self.add(self.rows(m, half), self.flat.at[slot])
            if 0 <= j < nx:
                for half, m, bit, slot in self.plane(j):
                    p.start(self.planecopy, half, m, bit, slot)
        if self.has_line:
            if 1 <= s <= self.zsteps:
                self.zwait(s)
            if 0 <= s < self.zsteps:
                self.zstart(s + 1)
            if t == self.stages - 1:
                self.finish()

    def finish(self):
        p = self.p
        if self.paired:
            mine = (2 * p.k == p.z) | (2 * p.k + 1 == p.z)
            own = lax.rem(p.z, 2)
            terms = [(self.got.at[t], lax.div(p.z, 2) + t * p.half != p.z) for t in (0, 1)]
        else:
            mine = None
            own = p.z
            n = p.nz
            terms = [(self.got.at[n - 2], p.z > 0), (self.got.at[2 * n - 3], p.z < n - 1)]
        source = self.column(own)

        def first(at):
            value = source[at].astype(F32)
            self.share[at] = value if mine is None else jnp.where(mine, value, 0.0)

        rowwise(self.r, 16, first)
        for ref, ok in terms:

            @pl.when(ok)
            def _(ref=ref):
                def more(at):
                    self.share[at] = self.share[at] + ref[at].astype(F32)

                rowwise(self.r, 16, more)


def perform(steps):
    for step in steps:
        if callable(step):
            step()
        else:
            step[0].stage(step[1])


def normalise(v):
    centred = v - jnp.mean(v, 1, keepdims=True)
    scale = lax.rsqrt(jnp.mean(centred * centred, 1, keepdims=True) + EPSILON)
    return centred * scale, scale


def norm_back(g, v, gain, gain_sum, shift_sum):
    n, scale = normalise(v)
    fold = lambda a: sum(a[i * 8 : (i + 1) * 8] for i in range(a.shape[0] // 8))
    gain_sum[...] += fold(g * n)
    shift_sum[...] += fold(g)
    gg = g * gain
    return (gg - jnp.mean(gg, 1, keepdims=True) - n * jnp.mean(gg * n, 1, keepdims=True)) * scale


def own_half(value, i):
    lane = lax.broadcasted_iota(jnp.int32, value.shape, 1)
    return jnp.where((lane >= HEAD_DIM) if i else (lane < HEAD_DIM), value, jnp.zeros_like(value))


def merge_halves(a, b):
    lane = lax.broadcasted_iota(jnp.int32, a.shape, 1)
    return jnp.where(lane < HEAD_DIM, a, b)


def project(normed, weight, qkv, pz):
    c = pz * 128
    rows = normed.shape[0]
    for j in (0, 1):
        for t in range(3):
            for i in range(rows // 512):
                at = pl.ds(i * 512, 512)
                y = nn(normed[at, :], weight[:, pl.ds((j * 3 + t) * c, c)])
                if t == 0:
                    y = y.astype(BF16).astype(F32) * HEAD_DIM**-0.5
                for w in range(pz):
                    qkv[t, j * pz + w, at, :] = y[:, w * 128 : (w + 1) * 128].astype(BF16)


def distances(dist, length):
    rows, cols = dist.shape

    def body(i, carry):
        row = lax.broadcasted_iota(jnp.int32, (64, cols), 0) + i * 64
        col = lax.broadcasted_iota(jnp.int32, (64, cols), 1)
        gap = jnp.abs(row - col).astype(F32)
        dist[part(i, 64), :] = jnp.where(col < length, gap, 1e33)
        return carry

    lax.fori_loop(0, rows // 64, body, 0)


def forward_tile(qkv, dist, pair, first_head, at, store):
    q, k, v = qkv[0, pair, at, :], qkv[1, pair], qkv[2, pair]
    gap = dist[at, :]
    outs = []
    for i in range(2):
        head = (first_head + 2 * pair + i + 1).astype(F32)
        slope = jnp.exp2(jnp.full((1, 1), -8.0 / HEADS, F32) * head) * LOG2E
        x = nt(own_half(q, i), k) * LOG2E - gap * slope
        e = jnp.exp2(x - jnp.max(x, 1, keepdims=True))
        p = (e * (1.0 / jnp.sum(e, 1, keepdims=True))).astype(BF16)
        store(i, p)
        outs.append(nn(p, v))
    return merge_halves(*outs).astype(BF16)


def backward_tile(qkv, do, do_t, q_t, pair, probs, dk, dv):
    k, v = qkv[1, pair], qkv[2, pair]
    dq = []
    for i in range(2):
        p = probs(i)
        rows = pl.ds(i * HEAD_DIM, HEAD_DIM)
        t = p.astype(F32) * nt(own_half(do, i), v)
        ds = (t - p.astype(F32) * jnp.sum(t, 1, keepdims=True)).astype(BF16)
        dq.append(nn(ds, k))
        dv[rows, :] += nn(do_t[rows, :], p)
        dk[rows, :] += nn(q_t[rows, :], ds)
    return (merge_halves(*dq) * HEAD_DIM**-0.5).astype(BF16)


def forward_kernel(
    nb, nz, lengths, x, skip_x, gain_one, shift_one, gain_two, shift_two,
    skip_w, query_w, key_w, value_w, out_w, up_w, down_w,
    mixed_out, normed_out, norms_out, skip_out, qkvw_out, out_out, ff0_out, ff1_out, ff2_out, ff3_w, qkv_out, probs, attended_out,
    skip, qkvw, joined, mixed, normed, everything, norms, gains, turned, ff_w, qkv, dist, pbuf, attended,
    load, ff_load, norm_send, norm_recv, swap_send, swap_recv, flush, psem, att_send, att_recv, *rest,
):
    place = Place(nb, nz)
    z, group, k, half = place.z, place.group, place.k, place.half
    frames = x.shape[0] // 2
    width = x.shape[1]
    keys = nz * frames
    c = norms.shape[1]
    cw = up_w.shape[1] // 4
    pz = c // 128
    pairs = 2 * pz
    place.greet()

    jobs = [rest[3 * i : 3 * i + 3] for i in range(7)]
    rs = skip_w.shape[0] // 2
    skips = [Gather(place, skip_w.at[pl.ds(h * rs, rs)], skip, jobs[h], h=h, of=2) for h in (0, 1)]
    qkv_job = Gather(place, [query_w, key_w, value_w], qkvw, jobs[2], True)
    out_job = Gather(place, turned, out_out, jobs[3])
    ff = [Gather(place, ff_w.at[i], o, jobs[4 + i]) for i, o in enumerate((ff0_out, ff1_out, ff2_out))]
    last = nz - 1

    def go(job, *stages):
        for t in stages:
            if t < job.stages:
                job.stage(t)

    def both(*stages):
        for t in stages:
            go(skips[0], t)
            go(skips[1], t)

    both(0)
    loads = [
        pltpu.make_async_copy(x, joined.at[:, pl.ds(0, width)], load.at[0]),
        pltpu.make_async_copy(skip_x, joined.at[:, pl.ds(width, width)], load.at[1]),
    ]
    up_loads = [
        pltpu.make_async_copy(up_w.at[:, pl.ds(i * cw, cw)], ff_w.at[i, :, pl.ds(0, cw)], ff_load.at[i]) for i in range(4)
    ]
    for one in loads + up_loads:
        one.start()
    norms[...] = jnp.zeros_like(norms)
    for i, ref in enumerate((gain_one, shift_one, gain_two, shift_two)):
        norms[i : i + 1, :] = ref[...].astype(F32).reshape(1, c)
    own_norms = pltpu.make_async_copy(norms, gains.at[:, part(z, c)], load.at[2])
    own_norms.start()
    norm_copy = lambda r: remote(
        norms, gains.at[:, part(z, c)], norm_send.at[r - 1], norm_recv.at[r - 1], (place.b, lax.rem(z + r, nz))
    )
    for r in range(1, nz):
        place.start(norm_copy, r)
    turned[...] = out_w[...].T
    down_t = down_w[...].T
    for i in range(4):
        ff_w[i, :, cw:] = down_t[:, i * cw : (i + 1) * cw]
    both(*range(1, last))
    go(qkv_job, 0)
    go(skips[0], last)
    go(out_job, 0)
    go(skips[1], last)
    for one in up_loads:
        one.wait()
    go(skips[0], last + 1)
    go(out_job, 1)
    go(skips[1], last + 1)
    go(out_job, *range(2, last))
    go(ff[0], 0)
    go(skips[0], last + 2)
    go(ff[0], 1)
    go(skips[1], last + 2)
    go(ff[0], *range(2, last))
    go(qkv_job, 1)
    go(out_job, last)
    go(ff[1], 0)
    both(*range(last + 3, skips[0].stages))
    flushes = []

    def out_copy(src, dst):
        copy = pltpu.make_async_copy(src, dst, flush.at[len(flushes)])
        flushes.append(copy)
        copy.start()

    out_copy(skip, skip_out)
    out_copy(ff_w.at[3], ff3_w)
    own_norms.wait()
    for one in loads:
        one.wait()
    for r in range(1, nz):
        norm_copy(r).wait_recv()
    out_copy(gains, norms_out)

    def across():
        return remote(
            normed.at[1 - group], everything.at[part(z, frames)], swap_send.at[0], swap_recv.at[0],
            (place.b, place.partner),
        )

    for turn in (0, 1):
        item = 1 - group if turn == 0 else group
        rows = part(item, frames)
        mixed[rows, :] = nn(joined[rows, :], skip[...])
        gain, shift = gains[0:1, :], gains[1:2, :]

        def body(i, carry):
            at = part(i, 32)
            at2 = pl.ds(pl.multiple_of(item * frames + i * 32, 32), 32)
            n, _ = normalise(mixed[at2, :])
            normed[item, at, :] = (n * gain + shift).astype(BF16)
            return carry

        lax.fori_loop(0, frames // 32, body, 0)
        if turn == 0:
            place.start(across)
            go(qkv_job, 2)
            go(out_job, last + 1)
            go(ff[0], last)
            go(ff[1], 1)
        else:
            own = pltpu.make_async_copy(normed.at[item], everything.at[part(z, frames)], load.at[0])
            own.start()

    def mate_copy(src, block, r, sem):
        return remote(
            src, everything.at[part(block, frames)], swap_send.at[sem], swap_recv.at[sem], (place.b, place.mate(r))
        )

    for r in range(1, half):
        place.start(mate_copy, normed.at[group], z, r, r)
    out_copy(mixed, mixed_out)
    go(ff[1], *range(2, last))
    distances(dist, lengths[group])
    go(qkv_job, 3)
    go(out_job, last + 2)
    go(ff[0], last + 1)
    across().wait_recv()
    for r in range(1, half):
        block = everything.at[part(place.partner, frames)]
        place.start(mate_copy, block, place.partner, r, half - 1 + r)
    go(ff[1], last)
    go(ff[2], 0)
    go(qkv_job, *range(4, qkv_job.stages))
    go(out_job, *range(last + 3, out_job.stages))
    out_copy(qkvw, qkvw_out)
    go(ff[0], last + 2)
    own.wait()
    for r in range(1, half):
        mate_copy(normed.at[group], z, r, r).wait_recv()
        mate_copy(normed.at[group], z, r, half - 1 + r).wait_recv()
    out_copy(everything, normed_out)
    go(ff[2], 1)

    project(everything, qkvw, qkv, pz)
    out_copy(qkv, qkv_out)
    first_head = k * 2 * pairs
    blocks = keys // QUERIES
    total = pairs * blocks

    def probs_copy(slot, pair, at):
        return pltpu.make_async_copy(pbuf.at[slot], probs.at[pair, :, at], psem.at[slot])

    def att_copy(pair, r):
        owner = lax.rem(z + r, nz)
        slot = pair * (nz - 1) + r - 1
        return remote(
            attended.at[pair, part(owner, frames)],
            attended_out.at[part(group, frames), part(k * pairs + pair, 128)],
            att_send.at[slot], att_recv.at[slot], (place.b, owner),
        )

    def att_own(pair):
        return pltpu.make_async_copy(
            attended.at[pair, part(z, frames)],
            attended_out.at[part(group, frames), part(k * pairs + pair, 128)],
            flush.at[7 + pair],
        )

    hooks = {}

    def hook(it, *steps):
        hooks.setdefault(min(it, total - 1), []).extend(steps)

    rest_of = lambda job, t: [(job, s) for s in range(t, job.stages)]
    hook(0, *[(ff[2], t) for t in range(2, last)], (ff[1], last + 1))
    hook(total // 8, (ff[2], last), *rest_of(ff[0], last + 3))
    hook(total * 3 // 8, (ff[1], last + 2))
    hook(total * 4 // 8, (ff[2], last + 1))
    hook(total * 6 // 8, *rest_of(ff[1], last + 3))
    hook(total - 1, (ff[2], last + 2))

    def body(it, carry):
        pair, q = lax.div(it, blocks), lax.rem(it, blocks)
        at, slot = part(q, QUERIES), lax.rem(it, 2)
        for when, steps in hooks.items():
            pl.when(it == when)(lambda steps=steps: perform(steps))

        @pl.when(it >= 2)
        def _():
            probs_copy(slot, pair, at).wait()

        def store(i, p):
            pbuf[slot, i] = p

        attended[pair, at, :] = forward_tile(qkv, dist, pair, first_head, at, store)
        probs_copy(slot, pair, at).start()

        @pl.when(q == blocks - 1)
        def _():
            for r in range(1, nz):
                att_copy(pair, r).start()

        return carry

    lax.fori_loop(0, total, body, 0)
    for pair in range(pairs):
        att_own(pair).start()
    go(ff[2], *range(last + 3, ff[2].stages))
    for pair in range(pairs):
        for r in range(1, nz):
            att_copy(pair, r).wait()
    for pair in range(pairs):
        att_own(pair).wait()
    for slot in range(min(2, total)):
        probs_copy(slot, 0, pl.ds(0, QUERIES)).wait()
    for copy in flushes:
        copy.wait()
    place.drain()


def forward(nb, nz, lengths, x, skip_x, norms, skip_w, qkv_w, out_w, up_w, down_w):
    rows, width = x.shape
    frames = rows // 2
    keys = nz * frames
    c = width // nz
    pairs = 2 * c // 128
    r = up_w.shape[0]
    chunk = up_w.shape[1] // 2
    S, V, D = jax.ShapeDtypeStruct, pltpu.VMEM, pltpu.SemaphoreType.DMA
    out_shape = [
        S((rows, width), F32),
        S((keys, width), BF16),
        S((8, width), F32),
        S((nb * skip_w.shape[0], width), BF16),
        S((nb * r, 6 * c), BF16),
        S((nb * r, width), BF16),
        *[S((nb * r, nz * chunk), BF16)] * 3,
        S((r, chunk), BF16),
        S((3, pairs, keys, 128), BF16),
        S((pairs, 2, keys, keys), BF16),
        S((rows, width), BF16),
    ]
    scratch = [
        V((nb * skip_w.shape[0], width), BF16),
        V((nb * r, 6 * c), BF16),
        V((rows, 2 * width), BF16),
        V((rows, width), F32),
        V((2, frames, width), BF16),
        V((keys, width), BF16),
        V((8, c), F32),
        V((8, width), F32),
        V((r, c), BF16),
        V((4, r, chunk), BF16),
        V((3, pairs, keys, 128), BF16),
        V((keys, keys), F32),
        V((2, 2, QUERIES, keys), BF16),
        V((pairs, keys, 128), BF16),
    ]
    scratch += [D((3,)), D((4,)), D((nz - 1,)), D((nz - 1,)), D((nz - 1,)), D((nz - 1,)), D((7 + pairs,)), D((2,))]
    scratch += [D((pairs * (nz - 1),)), D((pairs * (nz - 1),))]
    for _ in range(7):
        scratch += Gather.scratch(nb, nz)
    return pl.pallas_call(
        functools.partial(forward_kernel, nb, nz),
        out_shape=out_shape,
        in_specs=[pl.BlockSpec(memory_space=pltpu.SMEM), ANY, ANY, *[WHOLE] * 4, *[ANY] * 4, WHOLE, ANY, WHOLE],
        out_specs=[ANY] * len(out_shape),
        scratch_shapes=scratch,
        compiler_params=pltpu.CompilerParams(
            collective_id=0, has_side_effects=True, vmem_limit_bytes=VMEM_LIMIT
        ),
    )(lengths, x, skip_x, *norms, skip_w, *qkv_w, out_w, up_w, down_w)


def ffn_kernel(
    nb, nz, mixed_in, attended_in, out_in, norms, cot_in, ff0, ff1, ff2, ff_w,
    output_out, middle_out, att_out, out_grad, part0, grad1, grad2, grad3, sums, ff3,
    middle, attended, out_t, cot, weights, grads, ffn_in, ffn_in_t, cot_t, acc, gacc, low,
    load, wload, flush, *rest,
):
    place = Place(nb, nz)
    rows, d = mixed_in.shape
    r = grads.shape[2]
    cw = ff_w.shape[1] // 2
    subs = nz // 2
    total = 4 * subs
    place.greet()
    gather = Gather(place, ff_w, ff3, rest[:3])
    job = Scatter(place, grads.at[0], None, rest[3:], sums=False, line=False)
    go = lambda job, *stages: [job.stage(t) for t in stages if t < job.stages]
    last = nz - 1
    go(gather, 0)
    loads = [
        pltpu.make_async_copy(src, dst, load.at[i])
        for i, (src, dst) in enumerate(
            ((attended_in, attended), (out_in, out_t), (mixed_in, middle), (cot_in, cot))
        )
    ]
    weight_load = lambda i: pltpu.make_async_copy((ff0, ff1, ff2, ff3)[i], weights.at[i % 2], wload.at[i % 2])
    for one in loads:
        one.start()
    weight_load(0).start()
    weight_load(1).start()
    gain, shift = norms[2:3, :], norms[3:4, :]
    for one in loads[:3]:
        one.wait()
    acc[...] = nt(attended[...], out_t[...])
    go(gather, 1)

    def enter(at):
        v = middle[at, :] + acc[at, :]
        middle[at, :] = v
        n, _ = normalise(v)
        ffn_in[at, :] = (n * gain + shift).astype(BF16)
        acc[at, :] = v
        gacc[at, :] = jnp.zeros_like(v)

    rowwise(rows, 32, enter)
    ffn_in_t[...] = ffn_in[...].T
    loads[3].wait()
    cot_t[...] = cot[...].T
    go(gather, *range(2, last))
    weight_load(0).wait()

    hooks = {}

    def hook(it, *steps):
        hooks.setdefault(min(it, total - 1), []).extend(steps)

    rest_of = lambda job, t: [(job, s) for s in range(t, job.stages)]
    hook(total // 8, (gather, last))
    hook(total * 2 // 8, lambda: weight_load(1).wait(), lambda: weight_load(2).start(), (gather, last + 1), (job, 0))
    hook(total * 4 // 8, lambda: weight_load(2).wait(), (gather, last + 2), lambda: flush_copy(3).start(), (job, 1))
    hook(total * 5 // 8, *rest_of(gather, last + 3), lambda: weight_load(3).start())
    hook(total * 6 // 8, lambda: weight_load(3).wait(), lambda: flush_copy(0).start(), (job, 2))
    hook(total * 7 // 8, *rest_of(job, 3))

    def flush_copy(i):
        pairs = (
            (grads.at[2], grad2), (grads.at[3], grad3), (grads.at[0, 0], part0), (grads.at[1], grad1),
            (low, output_out), (gacc, middle_out), (attended, att_out),
        )
        return pltpu.make_async_copy(*pairs[i], flush.at[i])

    def body(it, carry):
        for when, steps in hooks.items():
            pl.when(it == when)(lambda steps=steps: perform(steps))
        chunk, sub = lax.div(it, subs), lax.rem(it, subs)
        slot = lax.rem(chunk, 2)
        first = [(2 * sub + i) * 2 for i in (0, 1)]
        up = jnp.concatenate([weights[slot, :, part(f, cw)] for f in first], 1)
        dn = jnp.concatenate([weights[slot, :, part(f + 1, cw)] for f in first], 1)
        hidden = nn(ffn_in[...], up)
        active_grad = nn(cot[...], dn)
        cdf = 0.5 * (1.0 + lax.erf(hidden * 0.7071067811865476))
        active = (hidden * cdf).astype(BF16)
        density = jnp.exp2(hidden * hidden * (-0.5 * LOG2E)) * 0.3989422804014327
        hidden_grad = (active_grad * (cdf + hidden * density)).astype(BF16)
        acc[...] += nt(active, dn)
        gacc[...] += nt(hidden_grad, up)
        up_grad = nn(ffn_in_t[...], hidden_grad).astype(BF16)
        dn_grad = nn(cot_t[...], active).astype(BF16)
        for j in range(nb):
            m = flip(place.b, j)
            block = slice(j * r, (j + 1) * r)
            for i in (0, 1):
                cols = slice(i * cw, (i + 1) * cw)
                grads[chunk, m, :, part(first[i], cw)] = up_grad[block, cols]
                grads[chunk, m, :, part(first[i] + 1, cw)] = dn_grad[block, cols]
        return carry

    lax.fori_loop(0, total, body, 0)
    flush_copy(1).start()
    flush_copy(2).start()
    sums[...] = jnp.zeros_like(sums)

    def leave(at):
        low[at, :] = acc[at, :].astype(BF16)
        back = norm_back(gacc[at, :], middle[at, :], gain, sums.at[0], sums.at[1])
        grad = cot[at, :].astype(F32) + back
        gacc[at, :] = grad
        ffn_in[at, :] = grad.astype(BF16)

    rowwise(rows, 32, leave)
    flush_copy(4).start()
    flush_copy(5).start()
    grad_t = ffn_in[...].T
    for j in range(nb):
        out_grad[flip(place.b, j)] = nn(grad_t[j * r : (j + 1) * r, :], attended[...]).astype(BF16)
    attended[...] = nn(ffn_in[...], out_t[...]).astype(BF16)
    flush_copy(6).start()
    for i in range(7):
        flush_copy(i).wait()
    place.drain()


def ffn(nb, nz, mixed, attended, out_t, norms, cot, ff0, ff1, ff2, ff_w):
    rows, d = mixed.shape
    r, width = ff_w.shape
    wide = nz * width
    V, S, D = pltpu.VMEM, jax.ShapeDtypeStruct, pltpu.SemaphoreType.DMA
    scratch = [
        V((rows, d), F32),
        V((rows, d), BF16),
        V((d, d), BF16),
        V((rows, d), BF16),
        V((2, d, wide), BF16),
        V((4, nb, r, wide), BF16),
        V((rows, d), BF16),
        V((d, rows), BF16),
        V((d, rows), BF16),
        V((rows, d), F32),
        V((rows, d), F32),
        V((rows, d), BF16),
        D((4,)), D((2,)), D((7,)),
    ]
    scratch += Gather.scratch(nb, nz)
    scratch += Scatter.scratch(nb, nz, r, wide, sums=False, line=False)
    return pl.pallas_call(
        functools.partial(ffn_kernel, nb, nz),
        out_shape=[
            S((rows, d), BF16),
            S((rows, d), F32),
            S((rows, d), BF16),
            S((nb, r, d), BF16),
            S((r, wide), BF16),
            *[S((nb, r, wide), BF16)] * 3,
            S((2, 8, d), F32),
            S((d, wide), BF16),
        ],
        in_specs=[ANY] * 3 + [WHOLE] + [ANY] * 5,
        out_specs=[ANY] * 3 + [WHOLE] + [ANY] * 4 + [WHOLE, ANY],
        scratch_shapes=scratch,
        compiler_params=pltpu.CompilerParams(
            collective_id=3, has_side_effects=True, vmem_limit_bytes=VMEM_LIMIT
        ),
    )(mixed, attended, out_t, norms, cot, ff0, ff1, ff2, ff_w)


def attention_kernel(
    nb, nz, att_grad, qkv_in, probs, part0, grad1, grad2, out_grad,
    dqkv, ff_share, out_share,
    qkv, dout, pbuf, dk, dv, q_t, do_t, load, psem, att_send, att_recv, *rest,
):
    place = Place(nb, nz)
    z, group, k = place.z, place.group, place.k
    pairs, keys = qkv.shape[1], qkv.shape[2]
    frames = keys // nz
    wide = pairs * 128
    pz = pairs // 2
    place.greet()

    def att_copy(r, pair):
        owner = lax.rem(z + r, nz)
        item, member = lax.div(owner, place.half), lax.rem(owner, place.half)
        slot = pair * (nz - 1) + r - 1
        return remote(
            att_grad.at[part(item, frames), part(member * pairs + pair, 128)],
            dout.at[part(z, frames), part(pair, 128)],
            att_send.at[slot], att_recv.at[slot], (place.b, owner),
        )

    def att_start(pair):
        for r in range(1, nz):
            att_copy(r, pair).start()

    for pair in range(min(2, pairs)):
        att_start(pair)
    own = pltpu.make_async_copy(att_grad.at[part(group, frames), part(k, wide)], dout.at[part(z, frames)], load.at[0])
    own.start()
    qkv_load = pltpu.make_async_copy(qkv_in, qkv, load.at[1])
    qkv_load.start()
    rest = list(rest)

    def job(full, share, **kind):
        count = 3 + sum(kind.get(key, True) and size for key, size in (("sums", 1), ("plane", 2), ("line", 1)))
        mine = [rest.pop(0) for _ in range(count)]
        return Scatter(place, full, share, mine, **kind)

    early = [job(None, ff_share.at[0], plane=False)]
    late = [job(g, ff_share.at[1 + i]) for i, g in enumerate((grad1, grad2))]
    out_job = job(out_grad, out_share)
    go = lambda job, *stages: [job.stage(t) for t in stages if t < job.stages]
    early_loads = [
        pltpu.make_async_copy(p, e.sums.at[0], load.at[2 + i]) for i, (p, e) in enumerate(zip((part0,), early))
    ]
    for one in early_loads:
        one.start()
    go(late[0], 0)
    go(late[1], 0)
    go(out_job, 0)
    go(late[0], 1)
    own.wait()
    qkv_load.wait()

    blocks = keys // QUERIES
    total = pairs * blocks

    def probs_copy(it):
        slot = lax.rem(it, 2)
        pair, q = lax.div(it, blocks), lax.rem(it, blocks)
        return pltpu.make_async_copy(probs.at[pair, :, part(q, QUERIES)], pbuf.at[slot], psem.at[slot])

    probs_copy(0).start()
    hooks = {}

    def hook(it, *steps):
        hooks.setdefault(min(it, total - 1), []).extend(steps)

    zs = place.nz - 1
    rest_of = lambda job, t: [(job, s) for s in range(t, job.stages)]
    hook(0, *[lambda one=one: one.wait() for one in early_loads], (early[0], 0))
    hook(total // 8, (late[1], 1), (early[0], 1))
    hook(total * 2 // 8, (late[0], 2), *[(early[0], t) for t in range(2, zs)])
    hook(total * 3 // 8, (out_job, 1), (early[0], zs))
    hook(total * 4 // 8, (late[1], 2))
    hook(total * 5 // 8, (late[0], 3), (out_job, 2))
    hook(total * 6 // 8, (late[0], 4))
    hook(total * 7 // 8, (late[1], 3), (late[0], 5), (out_job, 3))

    def body(it, carry):
        pair, q = lax.div(it, blocks), lax.rem(it, blocks)
        at, slot = part(q, QUERIES), lax.rem(it, 2)
        for when, steps in hooks.items():
            pl.when(it == when)(lambda steps=steps: perform(steps))

        @pl.when(it + 1 < total)
        def _():
            probs_copy(it + 1).start()

        probs_copy(it).wait()

        @pl.when(q == 0)
        def _():
            for r in range(1, nz):
                att_copy(r, pair).wait_recv()
            pl.when(pair + 2 < pairs)(lambda: att_start(pair + 2))
            dk[...] = jnp.zeros_like(dk)
            dv[...] = jnp.zeros_like(dv)

        do = dout[at, part(pair, 128)]
        q_t[...] = qkv[0, pair, at, :].T
        do_t[...] = do.T
        block = lax.div(pair, pz)
        column = lambda t: part((block * 3 + t) * pz + lax.rem(pair, pz), 128)
        dqkv[at, column(0)] = backward_tile(qkv, do, do_t, q_t, pair, lambda i: pbuf[slot, i], dk, dv)

        @pl.when(q == blocks - 1)
        def _():
            dqkv[:, column(1)] = dk[...].T.astype(BF16)
            dqkv[:, column(2)] = dv[...].T.astype(BF16)

        return carry

    lax.fori_loop(0, total, body, 0)
    for t in range(4, out_job.stages + 1):
        go(out_job, t)
        go(late[1], t)
        go(late[0], t + 2)
    for pair in range(pairs):
        for r in range(1, nz):
            att_copy(r, pair).wait_send()
    place.drain()


def attention_back(nb, nz, att_grad, qkv, probs, part0, grad1, grad2, out_grad):
    _, pairs, keys, _ = qkv.shape
    S, V, D = jax.ShapeDtypeStruct, pltpu.VMEM, pltpu.SemaphoreType.DMA
    _, r, wide = grad2.shape
    scratch = [
        V((3, pairs, keys, 128), BF16),
        V((keys, pairs * 128), BF16),
        V((2, 2, QUERIES, keys), BF16),
        V((128, keys), F32),
        V((128, keys), F32),
        V((128, QUERIES), BF16),
        V((128, QUERIES), BF16),
        D((4,)), D((2,)), D((pairs * (nz - 1),)), D((pairs * (nz - 1),)),
    ]
    scratch += Scatter.scratch(nb, nz, r, wide, plane=False)
    for g in (grad1, grad2, out_grad):
        scratch += Scatter.scratch(nb, nz, r, g.shape[2])
    return pl.pallas_call(
        functools.partial(attention_kernel, nb, nz),
        out_shape=[
            S((keys, 3 * pairs * 128), BF16),
            S((3, r, wide // nz), F32),
            S((r, out_grad.shape[2] // nz), F32),
        ],
        in_specs=[ANY] * 7,
        out_specs=[WHOLE] * 3,
        scratch_shapes=scratch,
        compiler_params=pltpu.CompilerParams(
            collective_id=1, has_side_effects=True, vmem_limit_bytes=VMEM_LIMIT
        ),
    )(att_grad, qkv, probs, part0, grad1, grad2, out_grad)


def first_kernel(
    nb, nz, dqkv_in, everything_in, qkvw_in, x, skip_x, skip_w, mixed_in, middle_in, norms, second_sums, grad3,
    input_grad, skip_grad, qkv_share, skip_share, norm_share, ff_share,
    dqkv, everything, qkvw, mixed, middle_grad,
    qkv_grad, skip_w_grad, weight, joined, joined_t, mixed_low, ahead, mine, from_mate, to_partner, from_partner,
    sums, packed, norm_in, norm_line, load, swap_send, swap_recv, norm_send, norm_recv, *rest,
):
    place = Place(nb, nz)
    z, group, k, half = place.z, place.group, place.k, place.half
    frames = x.shape[0] // 2
    width = x.shape[1]
    loads = [
        pltpu.make_async_copy(src, dst, load.at[i])
        for i, (src, dst) in enumerate(
            (
                (dqkv_in, dqkv),
                (qkvw_in, qkvw),
                (everything_in, everything),
                (mixed_in, mixed),
                (middle_in, middle_grad),
                (x, joined.at[:, pl.ds(0, width)]),
                (skip_x, joined.at[:, pl.ds(width, width)]),
                (skip_w, weight),
            )
        )
    ]
    for one in loads:
        one.start()
    place.greet()
    per = len(rest) // 4
    ff_job = Scatter(place, grad3, ff_share, rest[: per + 1])
    rest = rest[per + 1 :]
    per = len(rest) // 3
    qkv_job = Scatter(place, qkv_grad, qkv_share, rest[:per], True, sums=False)
    rs = skip_w_grad.shape[2]
    skips = [
        Scatter(
            place, skip_w_grad.at[h], skip_share.at[pl.ds(h * rs, rs)], rest[(1 + h) * per : (2 + h) * per], sums=False
        )
        for h in (0, 1)
    ]

    def go(job, *stages):
        for t in stages:
            if t < job.stages:
                job.stage(t)

    go(ff_job, 0)
    for one in loads[:2]:
        one.wait()

    def mate_copy(r, t):
        slot = (r - 1) * 2 + t
        return remote(
            ahead.at[slot], from_mate.at[slot], swap_send.at[slot], swap_recv.at[slot], (place.b, place.mate(r))
        )

    for r in range(1, half):
        for s in (0, 1):
            block = lax.rem(k + r, half) + (1 - group if s == 0 else group) * half
            ahead[(r - 1) * 2 + s] = nt(dqkv[part(block, frames), :], qkvw[...]).astype(BF16)
        place.start(mate_copy, r, 0)
    for s in (0, 1):
        block = k + (1 - group if s == 0 else group) * half
        mine[s] = nt(dqkv[part(block, frames), :], qkvw[...])
    loads[2].wait()
    turned = everything[...].T
    rq = qkv_grad.shape[1]
    for j in range(nb):
        qkv_grad[flip(place.b, j)] = nn(turned[j * rq : (j + 1) * rq, :], dqkv[...]).astype(BF16)
    go(qkv_job, 0)
    go(ff_job, 1)

    def add_mates(s):
        for r in range(1, half):
            mate_copy(r, s).wait_recv()
            slot = (r - 1) * 2 + s

            def body(at):
                mine[s, at] = mine[s, at] + from_mate[slot, at].astype(F32)

            rowwise(frames, 16, body)

    add_mates(0)
    sem = 2 * (half - 1)
    across = lambda: remote(to_partner, from_partner, swap_send.at[sem], swap_recv.at[sem], (place.b, place.partner))

    def narrow(at):
        to_partner[at] = mine[0, at].astype(BF16)

    rowwise(frames, 16, narrow)
    place.start(across)
    for r in range(1, half):
        place.start(mate_copy, r, 1)
    for one in loads[3:]:
        one.wait()
    joined_t[...] = joined[...].T
    go(qkv_job, 1)
    go(ff_job, 2)

    sums[...] = jnp.zeros_like(sums)
    gain = norms[0:1, :]

    def back(item, grad):
        def body(i, carry):
            at = part(i, 32)
            to = pl.ds(pl.multiple_of(item * frames + i * 32, 32), 32)
            part_grad = norm_back(grad(at), mixed[to, :], gain, sums.at[0], sums.at[1])
            mixed_low[to, :] = (middle_grad[to, :] + part_grad).astype(BF16)
            return carry

        lax.fori_loop(0, frames // 32, body, 0)

    add_mates(1)
    back(group, lambda at: mine[1, at])
    go(ff_job, 3)
    across().wait_recv()
    back(1 - group, lambda at: from_partner[at].astype(F32))
    for h in (0, 1):
        for j in range(nb):
            block = slice((2 * j + h) * rs, (2 * j + h + 1) * rs)
            skip_w_grad[h, flip(place.b, j)] = nn(joined_t[block, :], mixed_low[...]).astype(BF16)
        go(skips[h], 0)

    total = lambda a: jnp.sum(a, 0, keepdims=True)
    for i, v in enumerate((sums[0], sums[1], second_sums[0], second_sums[1])):
        packed[i : i + 1, :] = total(v)
    packed[4:8, :] = jnp.zeros_like(packed[4:8, :])
    bits = [0] + place.rest
    norm_copy = lambda i: remote(
        packed, norm_in.at[i], norm_send.at[i], norm_recv.at[i], place.at(1 << bits[i])
    )
    c = norm_share.shape[1]
    line_copy = lambda r: remote(
        packed.at[:, part(lax.rem(z + r, nz), c)], norm_line.at[r - 1],
        norm_send.at[len(bits) + r - 1], norm_recv.at[len(bits) + r - 1], (place.b, lax.rem(z + r, nz)),
    )

    def norm_step(i):
        if i > 0:
            norm_copy(i - 1).wait()
            packed[...] = packed[...] + norm_in[i - 1]
        if i < len(bits):
            norm_copy(i).start()
        else:
            for r in range(1, nz):
                line_copy(r).start()

    norm_step(0)
    go(qkv_job, 2)
    go(skips[0], 1)
    go(skips[1], 1)
    norm_step(1)
    go(ff_job, 4)
    input_grad[...] = nt(mixed_low[...], weight[pl.ds(0, width), :])
    go(skips[0], 2)
    norm_step(2)
    go(qkv_job, 3)
    skip_grad[...] = nt(mixed_low[...], weight[pl.ds(width, width), :])
    go(skips[1], 2)
    norm_step(3)
    for i in range(4, len(bits) + 1):
        norm_step(i)
    for t in range(3, max(skips[0].stages, qkv_job.stages - 1, ff_job.stages - 2)):
        go(skips[0], t)
        go(skips[1], t)
        go(qkv_job, t + 1)
        go(ff_job, t + 2)
    value = packed[:, part(z, c)]
    for r in range(1, nz):
        line_copy(r).wait()
        value = value + norm_line[r - 1]
    norm_share[...] = value
    place.drain()


def first_back(nb, nz, dqkv, everything, qkvw, x, skip_x, skip_w, mixed, middle_grad, norms, second_sums, grad3):
    rows, width = x.shape
    frames = rows // 2
    half = nz // 2
    c = width // nz
    S, V, D = jax.ShapeDtypeStruct, pltpu.VMEM, pltpu.SemaphoreType.DMA
    qkv_wide = qkvw.shape[1]
    bits = nb.bit_length() - 1
    swaps = 2 * (half - 1)
    scratch = [
        V(dqkv.shape, BF16),
        V(everything.shape, BF16),
        V(qkvw.shape, BF16),
        V((rows, width), F32),
        V((rows, width), F32),
        V((nb, qkvw.shape[0] // nb, qkv_wide), BF16),
        V((2, nb, skip_w.shape[0] // nb // 2, width), BF16),
        V(skip_w.shape, BF16),
        V((rows, 2 * width), BF16),
        V((2 * width, rows), BF16),
        V((rows, width), BF16),
        V((max(swaps, 1), frames, width), BF16),
        V((2, frames, width), F32),
        V((max(swaps, 1), frames, width), BF16),
        V((frames, width), BF16),
        V((frames, width), BF16),
        V((2, 8, width), F32),
        V((8, width), F32),
        V((bits, 8, width), F32),
        V((nz - 1, 8, c), F32),
        D((8,)), D((swaps + 1,)), D((swaps + 1,)), D((bits + nz - 1,)), D((bits + nz - 1,)),
    ]
    scratch += Scatter.scratch(nb, nz, grad3.shape[1], grad3.shape[2])
    scratch += Scatter.scratch(nb, nz, qkvw.shape[0] // nb, qkv_wide, True, sums=False)
    for _ in (0, 1):
        scratch += Scatter.scratch(nb, nz, skip_w.shape[0] // nb // 2, width, sums=False)
    return pl.pallas_call(
        functools.partial(first_kernel, nb, nz),
        out_shape=[
            S((rows, width), F32),
            S((rows, width), F32),
            S((qkvw.shape[0] // nb, qkv_wide // 2), F32),
            S((skip_w.shape[0] // nb, c), F32),
            S((8, c), F32),
            S((grad3.shape[1], grad3.shape[2] // nz), F32),
        ],
        in_specs=[ANY] * 8 + [WHOLE] * 2 + [ANY],
        out_specs=[WHOLE] * 6,
        scratch_shapes=scratch,
        compiler_params=pltpu.CompilerParams(
            collective_id=2, has_side_effects=True, vmem_limit_bytes=VMEM_LIMIT
        ),
    )(dqkv, everything, qkvw, x, skip_x, skip_w, mixed, middle_grad, norms, second_sums, grad3)


def shards(
    inputs,
    skip_input,
    lengths,
    skip_weight,
    query_weight,
    key_weight,
    value_weight,
    out_weight,
    up_weight,
    down_weight,
    first_gain,
    first_shift,
    second_gain,
    second_shift,
    cotangent,
):
    nb, nz = lax.axis_size("batch"), lax.axis_size("seq")
    shape = inputs.shape
    flat = lambda a: a.reshape(shape[0] * shape[1], shape[2])
    x, skip_x, cot = flat(inputs), flat(skip_input), flat(cotangent)
    norms = (first_gain, first_shift, second_gain, second_shift)
    qkv_w = (query_weight, key_weight, value_weight)
    (mixed, everything, gains, skip_w, qkvw, out_t, ff0, ff1, ff2, ff3_w, qkv, probs, attended) = forward(
        nb, nz, lengths, x, skip_x, norms, skip_weight, qkv_w, out_weight, up_weight, down_weight
    )
    output, middle_grad, att_grad, out_grad, part0, grad1, grad2, grad3, second_sums, _ = ffn(
        nb, nz, mixed, attended, out_t, gains, cot, ff0, ff1, ff2, ff3_w
    )
    dqkv, ff_share, out_share = attention_back(nb, nz, att_grad, qkv, probs, part0, grad1, grad2, out_grad)
    input_grad, skip_grad, qkv_share, skip_share, norm_share, ff_last = first_back(
        nb, nz, dqkv, everything, qkvw, x, skip_x, skip_w, mixed, middle_grad, gains, second_sums, grad3
    )
    cw = up_weight.shape[1] // 4
    ff_share = jnp.concatenate([ff_share, ff_last[None]], 0)
    up_share, dn_share = [
        ff_share[:, :, i * cw : (i + 1) * cw].transpose(1, 0, 2).reshape(up_weight.shape) for i in (0, 1)
    ]
    c = query_weight.shape[1]
    return (
        output.reshape(shape),
        input_grad.reshape(shape),
        skip_grad.reshape(shape),
        skip_share,
        qkv_share[:, :c],
        qkv_share[:, c : 2 * c],
        qkv_share[:, 2 * c :],
        out_share.T,
        up_share,
        dn_share.T,
        norm_share[0],
        norm_share[1],
        norm_share[2],
        norm_share[3],
    )


def solution(mesh):
    rows = P("batch", "seq", None)
    weight, turned, norm = P("batch", "seq"), P("seq", "batch"), P("seq")
    return jax.shard_map(
        shards,
        mesh=mesh,
        in_specs=(rows, rows, P("batch"), *[weight] * 4, turned, weight, turned, *[norm] * 4, rows),
        out_specs=(rows, rows, rows, *[weight] * 4, turned, weight, turned, *[norm] * 4),
        check_vma=False,
    )
```

```python
import functools

import jax
import jax.numpy as jnp
from jax import lax
from jax.experimental import pallas as pl
from jax.experimental.pallas import tpu as pltpu
from jax.sharding import PartitionSpec as P

HEADS = 16
HEAD_DIM = 64
EPSILON = 1e-05
LOG2E = 1.4426950408889634
QUERIES = 256
F32 = jnp.float32
BF16 = jnp.bfloat16
MESH = pl.DeviceIdType.MESH
VMEM_LIMIT = 60 * 2**20
ANY = pl.BlockSpec(memory_space=pl.ANY)
WHOLE = pl.BlockSpec(memory_space=pltpu.VMEM)


def nt(a, b):
    return lax.dot_general(a, b, (((1,), (1,)), ((), ())), preferred_element_type=F32)


def nn(a, b):
    return jnp.dot(a, b, preferred_element_type=F32)


def part(index, size):
    if isinstance(index, int):
        return pl.ds(index * size, size)
    return pl.ds(pl.multiple_of(index * size, size), size)


def rowwise(rows, step, body):
    def run(i, carry):
        body(part(i, step))
        return carry

    lax.fori_loop(0, rows // step, run, 0)


def flip(index, mask):
    result = index
    bit = 0
    while mask >> bit:
        if (mask >> bit) & 1:
            on = lax.rem(lax.div(index, 1 << bit), 2)
            result = result + (1 << bit) * (1 - 2 * on)
        bit += 1
    return result


def span(bits):
    masks = [0]
    for bit in bits:
        masks = masks + [m | (1 << bit) for m in masks]
    return masks


class Place:
    def __init__(self, nb, nz):
        self.nb, self.nz = nb, nz
        self.b = lax.axis_index("batch")
        self.z = lax.axis_index("seq")
        self.half = nz // 2
        self.group = lax.div(self.z, self.half)
        self.k = lax.rem(self.z, self.half)
        self.partner = lax.rem(self.z + self.half, nz)
        self.rest = list(range(1, nb.bit_length() - 1))
        self.orders = (self.rest, self.rest[::-1])
        self.pending = []

    def at(self, mask):
        return (flip(self.b, mask), self.z)

    def mate(self, r):
        return self.group * self.half + lax.rem(self.k + r, self.half)

    def greet(self):
        barrier = pltpu.get_barrier_semaphore()
        targets = [self.at(1 << k) for k in [0] + self.rest]
        targets += [(self.b, lax.rem(self.z + r, self.nz)) for r in range(1, self.nz)]
        for t in targets:
            pl.semaphore_signal(barrier, inc=1, device_id=t, device_id_type=MESH)
        pl.semaphore_wait(barrier, len(targets))

    def start(self, make, *args):
        copy, ok = self.unpack(make(*args))
        if ok is None:
            copy.start()
        else:
            pl.when(ok)(lambda: copy.start())
        self.pending.append((make, args))

    def drain(self):
        for make, args in self.pending:
            copy, ok = self.unpack(make(*args))
            if ok is None:
                copy.wait_send()
            else:
                pl.when(ok)(lambda copy=copy: copy.wait_send())
        self.pending = []

    @staticmethod
    def unpack(made):
        return made if isinstance(made, tuple) else (made, None)


def remote(src, dst, send, recv, device):
    return pltpu.make_async_remote_copy(
        src_ref=src, dst_ref=dst, send_sem=send, recv_sem=recv, device_id=device, device_id_type=MESH
    )


class Gather:
    @staticmethod
    def sems(nb, nz):
        return max(2 * (nz - 1), 6) + 2 * (nb // 2 - 1) + nb

    @staticmethod
    def scratch(nb, nz):
        count = Gather.sems(nb, nz)
        return [pltpu.SemaphoreType.DMA((3,))] + [pltpu.SemaphoreType.DMA((count,))] * 2

    def __init__(self, place, shard, full, scratch, paired=False, h=0, of=1):
        self.p, self.full, self.paired, self.h, self.of = place, full, paired, h, of
        self.shards = shard if paired else [shard]
        self.shard = self.shards[0]
        self.local, self.send, self.recv = scratch
        self.r, self.c = self.shard.shape
        nb, nz = place.nb, place.nz
        self.xy0 = max(2 * (nz - 1), 6)
        self.core0 = self.xy0 + 2 * (nb // 2 - 1)
        self.zsteps = 1 if paired else nz - 1
        self.stages = self.zsteps + len(place.rest) + 2

    def column(self, index):
        return self.full.at[part(self.p.b * self.of + self.h, self.r), part(index, self.c)]

    def line(self, way, step):
        p, n = self.p, self.p.nz
        sem = (0 if way > 0 else n - 1) + step - 1
        sent, got = p.z - way * (step - 1), p.z - way * step
        inside = lambda v: (v >= 0) & (v < n)
        clip = lambda v: jnp.clip(v, 0, n - 1)
        to = (p.b, clip(p.z + way))
        block = self.column(clip(sent))
        out = lambda: remote(self.shard if step == 1 else block, block, self.send.at[sem], self.recv.at[sem], to)
        land = self.column(clip(got))
        into = lambda: remote(land, land, self.send.at[sem], self.recv.at[sem], to)
        return out, into, inside(sent) & inside(p.z + way), inside(got)

    def zstart(self, step):
        p = self.p
        if self.paired:
            for t in (0, 1):
                for i in range(len(self.shards)):
                    p.start(self.paircopy, t, i)
            return
        for way in (1, -1):
            p.start(self.lineout, way, step)

    def lineout(self, way, step):
        out, _, can_send, _ = self.line(way, step)
        return out(), can_send

    def paircopy(self, t, i):
        p, count = self.p, len(self.shards)
        target = lax.div(p.z, 2) + t * p.half
        slot = lax.rem(p.z, 2) * count + i
        copy = remote(
            self.shards[i], self.column(slot), self.send.at[t * count + i], self.recv.at[slot], (p.b, target)
        )
        return copy, target != p.z

    def zwait(self, step):
        p = self.p
        if self.paired:
            for s in (0, 1):

                @pl.when(2 * p.k + s != p.z)
                def _(s=s):
                    for i in range(len(self.shards)):
                        slot = s * len(self.shards) + i
                        land = self.column(slot)
                        remote(land, land, self.send.at[slot], self.recv.at[slot], (p.b, p.partner)).wait_recv()

            return
        for way in (1, -1):
            _, into, _, can_get = self.line(way, step)
            pl.when(can_get)(lambda into=into: into().wait_recv())

    def owncopy(self, act):
        p, count = self.p, len(self.shards)
        place = lax.rem(p.z, 2) if self.paired else p.z
        copies = lambda: [
            pltpu.make_async_copy(shard, self.column(place * count + i), self.local.at[i])
            for i, shard in enumerate(self.shards)
        ]
        if self.paired:
            pl.when((2 * p.k == p.z) | (2 * p.k + 1 == p.z))(lambda: [act(copy) for copy in copies()][:0] or None)
        else:
            act(copies()[0])

    def rows(self, mask, half):
        h = self.r // 2
        return self.full.at[part((flip(self.p.b, mask) * self.of + self.h) * 2 + half, h)]

    def hop(self, sem, mask, half, bit, incoming):
        block = self.rows(mask | bit if incoming else mask, half)
        return remote(block, block, self.send.at[sem], self.recv.at[sem], self.p.at(bit))

    def plane(self, j):
        made = []
        for half in (0, 1):
            order = self.p.orders[half]
            for i, m in enumerate(span(order[:j])):
                sem = self.xy0 + half * (self.p.nb // 2 - 1) + (1 << j) - 1 + i
                made.append((half, m, 1 << order[j], sem))
        return made

    def coresem(self, mask, half):
        return self.core0 + (mask >> 1) * 2 + half

    def corestart(self, mask, half):
        self.p.start(self.hop, self.coresem(mask, half), mask, half, 1, False)

    def stage(self, t):
        p = self.p
        nx = len(p.rest)
        if t == 0:
            self.owncopy(lambda copy: copy.start())
            self.zstart(1)
        if 1 <= t <= self.zsteps:
            self.zwait(t)
            if t < self.zsteps:
                self.zstart(t + 1)
            else:
                self.owncopy(lambda copy: copy.wait())
        j = t - self.zsteps
        if 1 <= j <= nx:
            for half, m, bit, sem in self.plane(j - 1):
                self.hop(sem, m, half, bit, True).wait_recv()
        if 0 <= j < nx:
            for half, m, bit, sem in self.plane(j):
                p.start(self.hop, sem, m, half, bit, False)
        if j == 0:
            for half in (0, 1):
                self.corestart(0, half)
        if 1 <= j <= nx:
            for half, m, bit, _ in self.plane(j - 1):
                self.corestart(m | bit, half)
        if j == nx + 1:
            for m in span(p.rest):
                for half in (0, 1):
                    self.hop(self.coresem(m, half), m, half, 1, True).wait_recv()


class Scatter:
    @staticmethod
    def scratch(nb, nz, r, wide, paired=False, sums=True, plane=True, line=True):
        c = wide // (2 if paired else nz)
        lines = 2 if paired else 2 * (nz - 1)
        count = nb // 2 + 2 * (nb // 2 - 1) + lines
        made = [pltpu.VMEM((nb // 2 if plane else 1, r, wide), BF16)] if sums else []
        if plane:
            made += [
                pltpu.VMEM((nb // 2, r, wide), BF16),
                pltpu.VMEM((2 * (nb // 2 - 1), r // 2, wide), BF16),
            ]
        if line:
            made += [pltpu.VMEM((lines, r, c), BF16)]
        return made + [
            pltpu.SemaphoreType.DMA((nb // 2,)),
            pltpu.SemaphoreType.DMA((count,)),
            pltpu.SemaphoreType.DMA((count,)),
        ]

    def __init__(self, place, full, share, scratch, paired=False, sums=True, plane=True, line=True):
        self.p, self.full, self.share, self.paired = place, full, share, paired
        scratch = list(scratch)
        self.sums = scratch.pop(0) if sums else None
        self.core, self.flat = (scratch.pop(0), scratch.pop(0)) if plane else (None, None)
        self.got = scratch.pop(0) if line else None
        self.local, self.send, self.recv = scratch
        self.has_plane, self.has_line = plane, line
        _, self.r, self.wide = (full if plane else self.sums).shape
        self.c = self.wide // (2 if paired else place.nz)
        self.zsteps = 1 if paired else place.nz - 1
        self.nx = len(place.rest)
        self.plane_stages = 2 + self.nx
        self.stages = (self.plane_stages if plane else 1) + (self.zsteps if line else 0)
        self.zsem = place.nb // 2 + 2 * (place.nb // 2 - 1)
        self.masks = sorted(span(place.rest))

    def sum(self, m):
        return self.full.at[m] if self.sums is None else self.sums.at[m >> 1]

    def add(self, target, source):
        def body(at):
            target[at] = target[at] + source[at]

        rowwise(target.shape[0], 16, body)

    def corecopy(self, i, m):
        return remote(self.full.at[m | 1], self.core.at[i], self.send.at[i], self.recv.at[i], self.p.at(1))

    def load(self, i, m):
        return pltpu.make_async_copy(self.full.at[m], self.sum(m), self.local.at[i])

    def rows(self, m, half):
        return self.sum(m).at[part(half, self.r // 2)]

    def plane(self, j):
        p = self.p
        made = []
        for half in (0, 1):
            order = p.orders[half]
            base = half * (p.nb // 2 - 1) + sum(len(span(order[q + 1 :])) for q in range(j))
            for i, m in enumerate(span(order[j + 1 :])):
                made.append((half, m, 1 << order[j], base + i))
        return made

    def planecopy(self, half, m, bit, slot):
        sem = self.p.nb // 2 + slot
        return remote(
            self.rows(m | bit, half), self.flat.at[slot], self.send.at[sem], self.recv.at[sem], self.p.at(bit)
        )

    def column(self, index):
        return self.sum(0).at[:, part(index, self.c)]

    def line(self, way, step):
        p, n = self.p, self.p.nz
        here = p.z if way > 0 else n - 1 - p.z
        goes = n + here - step
        comes = goes - 1
        can_send = (goes > here) & (goes <= n - 1)
        can_get = (comes >= here) & (comes <= n - 1) & (here > 0)
        unfold = lambda d: jnp.clip(d if way > 0 else n - 1 - d, 0, n - 1)
        slot = (0 if way > 0 else n - 1) + step - 1
        copy = remote(
            self.column(unfold(goes)),
            self.got.at[slot],
            self.send.at[self.zsem + slot],
            self.recv.at[self.zsem + slot],
            (p.b, jnp.clip(p.z + way, 0, n - 1)),
        )
        return copy, can_send, can_get, unfold(comes), slot

    def paircopy(self, s):
        p = self.p
        copy = remote(
            self.column(s),
            self.got.at[p.group],
            self.send.at[self.zsem + s],
            self.recv.at[self.zsem + p.group],
            (p.b, 2 * p.k + s),
        )
        return copy, 2 * p.k + s != p.z

    def lineout(self, way, step):
        return self.line(way, step)[:2]

    def zstart(self, step):
        p = self.p
        if self.paired:
            for s in (0, 1):
                p.start(self.paircopy, s)
            return
        for way in (1, -1):
            p.start(self.lineout, way, step)

    def zwait(self, step):
        p = self.p
        if self.paired:
            for t in (0, 1):
                copy = remote(
                    self.column(0),
                    self.got.at[t],
                    self.send.at[self.zsem + t],
                    self.recv.at[self.zsem + t],
                    (p.b, p.partner),
                )
                pl.when(lax.div(p.z, 2) + t * p.half != p.z)(lambda copy=copy: copy.wait_recv())
            return
        for way in (1, -1):
            copy, _, can_get, column, slot = self.line(way, step)

            @pl.when(can_get)
            def _(copy=copy, column=column, slot=slot):
                copy.wait_recv()
                if step < self.zsteps:
                    self.add(self.column(column), self.got.at[slot])

    def stage(self, t):
        p, nx = self.p, self.nx
        s = t - (self.plane_stages - 1 if self.has_plane else 0)
        if self.has_plane:
            if t == 0:
                for i, m in enumerate(self.masks):
                    p.start(self.corecopy, i, m)
                    if self.sums is not None:
                        self.load(i, m).start()
            if t == 1:
                for i, m in enumerate(self.masks):
                    if self.sums is not None:
                        self.load(i, m).wait()
                    self.corecopy(i, m).wait_recv()
                    self.add(self.sum(m), self.core.at[i])
            j = t - 1
            if 1 <= j <= nx:
                for half, m, bit, slot in self.plane(j - 1):
                    self.planecopy(half, m, bit, slot).wait_recv()
                    self.add(self.rows(m, half), self.flat.at[slot])
            if 0 <= j < nx:
                for half, m, bit, slot in self.plane(j):
                    p.start(self.planecopy, half, m, bit, slot)
        if self.has_line:
            if 1 <= s <= self.zsteps:
                self.zwait(s)
            if 0 <= s < self.zsteps:
                self.zstart(s + 1)
            if t == self.stages - 1:
                self.finish()

    def finish(self):
        p = self.p
        if self.paired:
            mine = (2 * p.k == p.z) | (2 * p.k + 1 == p.z)
            own = lax.rem(p.z, 2)
            terms = [(self.got.at[t], lax.div(p.z, 2) + t * p.half != p.z) for t in (0, 1)]
        else:
            mine = None
            own = p.z
            n = p.nz
            terms = [(self.got.at[n - 2], p.z > 0), (self.got.at[2 * n - 3], p.z < n - 1)]
        source = self.column(own)

        def first(at):
            value = source[at].astype(F32)
            self.share[at] = value if mine is None else jnp.where(mine, value, 0.0)

        rowwise(self.r, 16, first)
        for ref, ok in terms:

            @pl.when(ok)
            def _(ref=ref):
                def more(at):
                    self.share[at] = self.share[at] + ref[at].astype(F32)

                rowwise(self.r, 16, more)


def perform(steps):
    for step in steps:
        if callable(step):
            step()
        else:
            step[0].stage(step[1])


def normalise(v):
    centred = v - jnp.mean(v, 1, keepdims=True)
    scale = lax.rsqrt(jnp.mean(centred * centred, 1, keepdims=True) + EPSILON)
    return centred * scale, scale


def norm_back(g, v, gain, gain_sum, shift_sum):
    n, scale = normalise(v)
    fold = lambda a: sum(a[i * 8 : (i + 1) * 8] for i in range(a.shape[0] // 8))
    gain_sum[...] += fold(g * n)
    shift_sum[...] += fold(g)
    gg = g * gain
    return (gg - jnp.mean(gg, 1, keepdims=True) - n * jnp.mean(gg * n, 1, keepdims=True)) * scale


def own_half(value, i):
    lane = lax.broadcasted_iota(jnp.int32, value.shape, 1)
    return jnp.where((lane >= HEAD_DIM) if i else (lane < HEAD_DIM), value, jnp.zeros_like(value))


def merge_halves(a, b):
    lane = lax.broadcasted_iota(jnp.int32, a.shape, 1)
    return jnp.where(lane < HEAD_DIM, a, b)


def project(normed, weight, qkv, pz):
    c = pz * 128
    rows = normed.shape[0]
    for j in (0, 1):
        for t in range(3):
            for i in range(rows // 512):
                at = pl.ds(i * 512, 512)
                y = nn(normed[at, :], weight[:, pl.ds((j * 3 + t) * c, c)])
                if t == 0:
                    y = y.astype(BF16).astype(F32) * HEAD_DIM**-0.5
                for w in range(pz):
                    qkv[t, j * pz + w, at, :] = y[:, w * 128 : (w + 1) * 128].astype(BF16)


def distances(dist, length):
    rows, cols = dist.shape

    def body(i, carry):
        row = lax.broadcasted_iota(jnp.int32, (64, cols), 0) + i * 64
        col = lax.broadcasted_iota(jnp.int32, (64, cols), 1)
        gap = jnp.abs(row - col).astype(F32)
        dist[part(i, 64), :] = jnp.where(col < length, gap, 1e33)
        return carry

    lax.fori_loop(0, rows // 64, body, 0)


def forward_tile(qkv, dist, pair, first_head, at, store):
    q, k, v = qkv[0, pair, at, :], qkv[1, pair], qkv[2, pair]
    gap = dist[at, :]
    outs = []
    for i in range(2):
        head = (first_head + 2 * pair + i + 1).astype(F32)
        slope = jnp.exp2(jnp.full((1, 1), -8.0 / HEADS, F32) * head) * LOG2E
        x = nt(own_half(q, i), k) * LOG2E - gap * slope
        e = jnp.exp2(x - jnp.max(x, 1, keepdims=True))
        p = (e * (1.0 / jnp.sum(e, 1, keepdims=True))).astype(BF16)
        store(i, p)
        outs.append(nn(p, v))
    return merge_halves(*outs).astype(BF16)


def backward_tile(qkv, do, do_t, q_t, pair, probs, dk, dv):
    k, v = qkv[1, pair], qkv[2, pair]
    dq = []
    for i in range(2):
        p = probs(i)
        rows = pl.ds(i * HEAD_DIM, HEAD_DIM)
        t = p.astype(F32) * nt(own_half(do, i), v)
        ds = (t - p.astype(F32) * jnp.sum(t, 1, keepdims=True)).astype(BF16)
        dq.append(nn(ds, k))
        dv[rows, :] += nn(do_t[rows, :], p)
        dk[rows, :] += nn(q_t[rows, :], ds)
    return (merge_halves(*dq) * HEAD_DIM**-0.5).astype(BF16)


def forward_kernel(
    nb, nz, lengths, x, skip_x, gain_one, shift_one, gain_two, shift_two,
    skip_w, query_w, key_w, value_w, out_w, up_w, down_w,
    mixed_out, normed_out, norms_out, skip_out, qkvw_out, out_out, ff0_out, ff1_out, ff2_out, ff3_w, qkv_out, probs, attended_out,
    skip, qkvw, joined, mixed, normed, everything, norms, gains, turned, ff_w, qkv, dist, pbuf, attended,
    load, ff_load, norm_send, norm_recv, swap_send, swap_recv, flush, psem, att_send, att_recv, *rest,
):
    place = Place(nb, nz)
    z, group, k, half = place.z, place.group, place.k, place.half
    frames = x.shape[0] // 2
    width = x.shape[1]
    keys = nz * frames
    c = norms.shape[1]
    cw = up_w.shape[1] // 4
    pz = c // 128
    pairs = 2 * pz
    place.greet()

    jobs = [rest[3 * i : 3 * i + 3] for i in range(7)]
    rs = skip_w.shape[0] // 2
    skips = [Gather(place, skip_w.at[pl.ds(h * rs, rs)], skip, jobs[h], h=h, of=2) for h in (0, 1)]
    qkv_job = Gather(place, [query_w, key_w, value_w], qkvw, jobs[2], True)
    out_job = Gather(place, turned, out_out, jobs[3])
    ff = [Gather(place, ff_w.at[i], o, jobs[4 + i]) for i, o in enumerate((ff0_out, ff1_out, ff2_out))]
    last = nz - 1

    def go(job, *stages):
        for t in stages:
            if t < job.stages:
                job.stage(t)

    def both(*stages):
        for t in stages:
            go(skips[0], t)
            go(skips[1], t)

    both(0)
    loads = [
        pltpu.make_async_copy(x, joined.at[:, pl.ds(0, width)], load.at[0]),
        pltpu.make_async_copy(skip_x, joined.at[:, pl.ds(width, width)], load.at[1]),
    ]
    up_loads = [
        pltpu.make_async_copy(up_w.at[:, pl.ds(i * cw, cw)], ff_w.at[i, :, pl.ds(0, cw)], ff_load.at[i]) for i in range(4)
    ]
    for one in loads + up_loads:
        one.start()
    norms[...] = jnp.zeros_like(norms)
    for i, ref in enumerate((gain_one, shift_one, gain_two, shift_two)):
        norms[i : i + 1, :] = ref[...].astype(F32).reshape(1, c)
    own_norms = pltpu.make_async_copy(norms, gains.at[:, part(z, c)], load.at[2])
    own_norms.start()
    norm_copy = lambda r: remote(
        norms, gains.at[:, part(z, c)], norm_send.at[r - 1], norm_recv.at[r - 1], (place.b, lax.rem(z + r, nz))
    )
    for r in range(1, nz):
        place.start(norm_copy, r)
    turned[...] = out_w[...].T
    down_t = down_w[...].T
    for i in range(4):
        ff_w[i, :, cw:] = down_t[:, i * cw : (i + 1) * cw]
    both(*range(1, last))
    go(qkv_job, 0)
    both(last)
    for one in up_loads:
        one.wait()
    go(ff[0], 0)
    both(last + 1)
    go(skips[0], last + 2)
    go(ff[0], *range(1, last))
    go(ff[1], 0)
    go(skips[1], last + 2)
    go(ff[1], *range(1, last - 1))
    go(qkv_job, 1)
    go(ff[0], last)
    both(*range(last + 3, skips[0].stages))
    go(ff[1], last - 1)
    flushes = []

    def out_copy(src, dst):
        copy = pltpu.make_async_copy(src, dst, flush.at[len(flushes)])
        flushes.append(copy)
        copy.start()

    out_copy(skip, skip_out)
    out_copy(ff_w.at[3], ff3_w)
    own_norms.wait()
    for one in loads:
        one.wait()
    for r in range(1, nz):
        norm_copy(r).wait_recv()
    out_copy(gains, norms_out)

    def across():
        return remote(
            normed.at[1 - group], everything.at[part(z, frames)], swap_send.at[0], swap_recv.at[0],
            (place.b, place.partner),
        )

    for turn in (0, 1):
        item = 1 - group if turn == 0 else group
        rows = part(item, frames)
        mixed[rows, :] = nn(joined[rows, :], skip[...])
        gain, shift = gains[0:1, :], gains[1:2, :]

        def body(i, carry):
            at = part(i, 32)
            at2 = pl.ds(pl.multiple_of(item * frames + i * 32, 32), 32)
            n, _ = normalise(mixed[at2, :])
            normed[item, at, :] = (n * gain + shift).astype(BF16)
            return carry

        lax.fori_loop(0, frames // 32, body, 0)
        if turn == 0:
            place.start(across)
            go(qkv_job, 2)
        else:
            own = pltpu.make_async_copy(normed.at[item], everything.at[part(z, frames)], load.at[0])
            own.start()

    def mate_copy(src, block, r, sem):
        return remote(
            src, everything.at[part(block, frames)], swap_send.at[sem], swap_recv.at[sem], (place.b, place.mate(r))
        )

    for r in range(1, half):
        place.start(mate_copy, normed.at[group], z, r, r)
    out_copy(mixed, mixed_out)
    go(ff[0], last + 1)
    go(ff[1], last)
    distances(dist, lengths[group])
    go(qkv_job, 3)
    go(ff[0], last + 2)
    across().wait_recv()
    for r in range(1, half):
        block = everything.at[part(place.partner, frames)]
        place.start(mate_copy, block, place.partner, r, half - 1 + r)
    go(ff[1], last + 1)
    go(qkv_job, *range(4, qkv_job.stages))
    out_copy(qkvw, qkvw_out)
    own.wait()
    for r in range(1, half):
        mate_copy(normed.at[group], z, r, r).wait_recv()
        mate_copy(normed.at[group], z, r, half - 1 + r).wait_recv()
    out_copy(everything, normed_out)
    go(ff[2], 0)
    go(out_job, 0)

    project(everything, qkvw, qkv, pz)
    out_copy(qkv, qkv_out)
    first_head = k * 2 * pairs
    blocks = keys // QUERIES
    total = pairs * blocks

    def probs_copy(slot, pair, at):
        return pltpu.make_async_copy(pbuf.at[slot], probs.at[pair, :, at], psem.at[slot])

    def att_copy(pair, r):
        owner = lax.rem(z + r, nz)
        slot = pair * (nz - 1) + r - 1
        return remote(
            attended.at[pair, part(owner, frames)],
            attended_out.at[part(group, frames), part(k * pairs + pair, 128)],
            att_send.at[slot], att_recv.at[slot], (place.b, owner),
        )

    def att_own(pair):
        return pltpu.make_async_copy(
            attended.at[pair, part(z, frames)],
            attended_out.at[part(group, frames), part(k * pairs + pair, 128)],
            flush.at[7 + pair],
        )

    hooks = {}

    def hook(it, *steps):
        hooks.setdefault(min(it, total - 1), []).extend(steps)

    rest_of = lambda job, t: [(job, s) for s in range(t, job.stages)]
    for t in range(1, last):
        hook(t - 1, (ff[2], t), (out_job, t))
    hook(last - 1, (ff[1], last + 2), (ff[2], last), (out_job, last))
    hook(total * 4 // 16, *rest_of(ff[0], last + 3))
    hook(total * 6 // 16, (ff[2], last + 1), (out_job, last + 1))
    hook(total * 8 // 16, *rest_of(ff[1], last + 3))
    hook(total * 13 // 16, (ff[2], last + 2))
    hook(total * 15 // 16, (out_job, last + 2))

    def body(it, carry):
        pair, q = lax.div(it, blocks), lax.rem(it, blocks)
        at, slot = part(q, QUERIES), lax.rem(it, 2)
        for when, steps in hooks.items():
            pl.when(it == when)(lambda steps=steps: perform(steps))

        @pl.when(it >= 2)
        def _():
            probs_copy(slot, pair, at).wait()

        def store(i, p):
            pbuf[slot, i] = p

        attended[pair, at, :] = forward_tile(qkv, dist, pair, first_head, at, store)
        probs_copy(slot, pair, at).start()

        @pl.when(q == blocks - 1)
        def _():
            for r in range(1, nz):
                att_copy(pair, r).start()

        return carry

    lax.fori_loop(0, total, body, 0)
    for pair in range(pairs):
        att_own(pair).start()
    go(ff[2], *range(last + 3, ff[2].stages))
    go(out_job, *range(last + 3, out_job.stages))
    for pair in range(pairs):
        for r in range(1, nz):
            att_copy(pair, r).wait()
    for pair in range(pairs):
        att_own(pair).wait()
    for slot in range(min(2, total)):
        probs_copy(slot, 0, pl.ds(0, QUERIES)).wait()
    for copy in flushes:
        copy.wait()
    place.drain()


def forward(nb, nz, lengths, x, skip_x, norms, skip_w, qkv_w, out_w, up_w, down_w):
    rows, width = x.shape
    frames = rows // 2
    keys = nz * frames
    c = width // nz
    pairs = 2 * c // 128
    r = up_w.shape[0]
    chunk = up_w.shape[1] // 2
    S, V, D = jax.ShapeDtypeStruct, pltpu.VMEM, pltpu.SemaphoreType.DMA
    out_shape = [
        S((rows, width), F32),
        S((keys, width), BF16),
        S((8, width), F32),
        S((nb * skip_w.shape[0], width), BF16),
        S((nb * r, 6 * c), BF16),
        S((nb * r, width), BF16),
        *[S((nb * r, nz * chunk), BF16)] * 3,
        S((r, chunk), BF16),
        S((3, pairs, keys, 128), BF16),
        S((pairs, 2, keys, keys), BF16),
        S((rows, width), BF16),
    ]
    scratch = [
        V((nb * skip_w.shape[0], width), BF16),
        V((nb * r, 6 * c), BF16),
        V((rows, 2 * width), BF16),
        V((rows, width), F32),
        V((2, frames, width), BF16),
        V((keys, width), BF16),
        V((8, c), F32),
        V((8, width), F32),
        V((r, c), BF16),
        V((4, r, chunk), BF16),
        V((3, pairs, keys, 128), BF16),
        V((keys, keys), F32),
        V((2, 2, QUERIES, keys), BF16),
        V((pairs, keys, 128), BF16),
    ]
    scratch += [D((3,)), D((4,)), D((nz - 1,)), D((nz - 1,)), D((nz - 1,)), D((nz - 1,)), D((7 + pairs,)), D((2,))]
    scratch += [D((pairs * (nz - 1),)), D((pairs * (nz - 1),))]
    for _ in range(7):
        scratch += Gather.scratch(nb, nz)
    return pl.pallas_call(
        functools.partial(forward_kernel, nb, nz),
        out_shape=out_shape,
        in_specs=[pl.BlockSpec(memory_space=pltpu.SMEM), ANY, ANY, *[WHOLE] * 4, *[ANY] * 4, WHOLE, ANY, WHOLE],
        out_specs=[ANY] * len(out_shape),
        scratch_shapes=scratch,
        compiler_params=pltpu.CompilerParams(
            collective_id=0, has_side_effects=True, vmem_limit_bytes=VMEM_LIMIT
        ),
    )(lengths, x, skip_x, *norms, skip_w, *qkv_w, out_w, up_w, down_w)


def ffn_kernel(
    nb, nz, mixed_in, attended_in, out_in, norms, cot_in, ff0, ff1, ff2, ff_w,
    output_out, middle_out, att_out, out_grad, part0, grad1, grad2, grad3, sums, ff3,
    middle, attended, out_t, cot, weights, grads, ffn_in, ffn_in_t, cot_t, acc, gacc, low,
    load, wload, flush, *rest,
):
    place = Place(nb, nz)
    rows, d = mixed_in.shape
    r = grads.shape[2]
    cw = ff_w.shape[1] // 2
    subs = nz // 2
    total = 4 * subs
    place.greet()
    gather = Gather(place, ff_w, ff3, rest[:3])
    job = Scatter(place, grads.at[0], None, rest[3:], sums=False, line=False)
    go = lambda job, *stages: [job.stage(t) for t in stages if t < job.stages]
    last = nz - 1
    go(gather, 0)
    loads = [
        pltpu.make_async_copy(src, dst, load.at[i])
        for i, (src, dst) in enumerate(
            ((attended_in, attended), (out_in, out_t), (mixed_in, middle), (cot_in, cot))
        )
    ]
    weight_load = lambda i: pltpu.make_async_copy((ff0, ff1, ff2, ff3)[i], weights.at[i % 2], wload.at[i % 2])
    for one in loads:
        one.start()
    weight_load(0).start()
    weight_load(1).start()
    gain, shift = norms[2:3, :], norms[3:4, :]
    for one in loads[:3]:
        one.wait()
    acc[...] = nt(attended[...], out_t[...])
    go(gather, 1)

    def enter(at):
        v = middle[at, :] + acc[at, :]
        middle[at, :] = v
        n, _ = normalise(v)
        ffn_in[at, :] = (n * gain + shift).astype(BF16)
        acc[at, :] = v
        gacc[at, :] = jnp.zeros_like(v)

    rowwise(rows, 32, enter)
    ffn_in_t[...] = ffn_in[...].T
    loads[3].wait()
    cot_t[...] = cot[...].T
    go(gather, *range(2, last))
    weight_load(0).wait()

    hooks = {}

    def hook(it, *steps):
        hooks.setdefault(min(it, total - 1), []).extend(steps)

    rest_of = lambda job, t: [(job, s) for s in range(t, job.stages)]
    hook(total // 8, (gather, last))
    hook(total * 2 // 8, lambda: weight_load(1).wait(), lambda: weight_load(2).start(), (gather, last + 1), (job, 0))
    hook(total * 4 // 8, lambda: weight_load(2).wait(), (gather, last + 2), lambda: flush_copy(3).start(), (job, 1))
    hook(total * 5 // 8, *rest_of(gather, last + 3), lambda: weight_load(3).start())
    hook(total * 6 // 8, lambda: weight_load(3).wait(), lambda: flush_copy(0).start(), (job, 2))
    hook(total * 7 // 8, *rest_of(job, 3))

    def flush_copy(i):
        pairs = (
            (grads.at[2], grad2), (grads.at[3], grad3), (grads.at[0, 0], part0), (grads.at[1], grad1),
            (low, output_out), (gacc, middle_out), (attended, att_out),
        )
        return pltpu.make_async_copy(*pairs[i], flush.at[i])

    def body(it, carry):
        for when, steps in hooks.items():
            pl.when(it == when)(lambda steps=steps: perform(steps))
        chunk, sub = lax.div(it, subs), lax.rem(it, subs)
        slot = lax.rem(chunk, 2)
        first = [(2 * sub + i) * 2 for i in (0, 1)]
        up = jnp.concatenate([weights[slot, :, part(f, cw)] for f in first], 1)
        dn = jnp.concatenate([weights[slot, :, part(f + 1, cw)] for f in first], 1)
        hidden = nn(ffn_in[...], up)
        active_grad = nn(cot[...], dn)
        cdf = 0.5 * (1.0 + lax.erf(hidden * 0.7071067811865476))
        active = (hidden * cdf).astype(BF16)
        density = jnp.exp2(hidden * hidden * (-0.5 * LOG2E)) * 0.3989422804014327
        hidden_grad = (active_grad * (cdf + hidden * density)).astype(BF16)
        acc[...] += nt(active, dn)
        gacc[...] += nt(hidden_grad, up)
        up_grad = nn(ffn_in_t[...], hidden_grad).astype(BF16)
        dn_grad = nn(cot_t[...], active).astype(BF16)
        for j in range(nb):
            m = flip(place.b, j)
            block = slice(j * r, (j + 1) * r)
            for i in (0, 1):
                cols = slice(i * cw, (i + 1) * cw)
                grads[chunk, m, :, part(first[i], cw)] = up_grad[block, cols]
                grads[chunk, m, :, part(first[i] + 1, cw)] = dn_grad[block, cols]
        return carry

    lax.fori_loop(0, total, body, 0)
    flush_copy(1).start()
    flush_copy(2).start()
    sums[...] = jnp.zeros_like(sums)

    def leave(at):
        low[at, :] = acc[at, :].astype(BF16)
        back = norm_back(gacc[at, :], middle[at, :], gain, sums.at[0], sums.at[1])
        grad = cot[at, :].astype(F32) + back
        gacc[at, :] = grad
        ffn_in[at, :] = grad.astype(BF16)

    rowwise(rows, 32, leave)
    flush_copy(4).start()
    flush_copy(5).start()
    grad_t = ffn_in[...].T
    for j in range(nb):
        out_grad[flip(place.b, j)] = nn(grad_t[j * r : (j + 1) * r, :], attended[...]).astype(BF16)
    attended[...] = nn(ffn_in[...], out_t[...]).astype(BF16)
    flush_copy(6).start()
    for i in range(7):
        flush_copy(i).wait()
    place.drain()


def ffn(nb, nz, mixed, attended, out_t, norms, cot, ff0, ff1, ff2, ff_w):
    rows, d = mixed.shape
    r, width = ff_w.shape
    wide = nz * width
    V, S, D = pltpu.VMEM, jax.ShapeDtypeStruct, pltpu.SemaphoreType.DMA
    scratch = [
        V((rows, d), F32),
        V((rows, d), BF16),
        V((d, d), BF16),
        V((rows, d), BF16),
        V((2, d, wide), BF16),
        V((4, nb, r, wide), BF16),
        V((rows, d), BF16),
        V((d, rows), BF16),
        V((d, rows), BF16),
        V((rows, d), F32),
        V((rows, d), F32),
        V((rows, d), BF16),
        D((4,)), D((2,)), D((7,)),
    ]
    scratch += Gather.scratch(nb, nz)
    scratch += Scatter.scratch(nb, nz, r, wide, sums=False, line=False)
    return pl.pallas_call(
        functools.partial(ffn_kernel, nb, nz),
        out_shape=[
            S((rows, d), BF16),
            S((rows, d), F32),
            S((rows, d), BF16),
            S((nb, r, d), BF16),
            S((r, wide), BF16),
            *[S((nb, r, wide), BF16)] * 3,
            S((2, 8, d), F32),
            S((d, wide), BF16),
        ],
        in_specs=[ANY] * 3 + [WHOLE] + [ANY] * 5,
        out_specs=[ANY] * 3 + [WHOLE] + [ANY] * 4 + [WHOLE, ANY],
        scratch_shapes=scratch,
        compiler_params=pltpu.CompilerParams(
            collective_id=3, has_side_effects=True, vmem_limit_bytes=VMEM_LIMIT
        ),
    )(mixed, attended, out_t, norms, cot, ff0, ff1, ff2, ff_w)


def attention_kernel(
    nb, nz, att_grad, qkv_in, probs, part0, grad1, grad2,
    dqkv, ff_share, part2,
    qkv, dout, pbuf, dk, dv, q_t, do_t, load, psem, att_send, att_recv, *rest,
):
    place = Place(nb, nz)
    z, group, k = place.z, place.group, place.k
    pairs, keys = qkv.shape[1], qkv.shape[2]
    frames = keys // nz
    wide = pairs * 128
    pz = pairs // 2
    place.greet()

    def att_copy(r, pair):
        owner = lax.rem(z + r, nz)
        item, member = lax.div(owner, place.half), lax.rem(owner, place.half)
        slot = pair * (nz - 1) + r - 1
        return remote(
            att_grad.at[part(item, frames), part(member * pairs + pair, 128)],
            dout.at[part(z, frames), part(pair, 128)],
            att_send.at[slot], att_recv.at[slot], (place.b, owner),
        )

    def att_start(pair):
        for r in range(1, nz):
            att_copy(r, pair).start()

    for pair in range(min(2, pairs)):
        att_start(pair)
    own = pltpu.make_async_copy(att_grad.at[part(group, frames), part(k, wide)], dout.at[part(z, frames)], load.at[0])
    own.start()
    qkv_load = pltpu.make_async_copy(qkv_in, qkv, load.at[1])
    qkv_load.start()
    rest = list(rest)

    def job(full, share, **kind):
        count = 3 + sum(kind.get(key, True) and size for key, size in (("sums", 1), ("plane", 2), ("line", 1)))
        mine = [rest.pop(0) for _ in range(count)]
        return Scatter(place, full, share, mine, **kind)

    early = [job(None, ff_share.at[0], plane=False)]
    late = [job(grad1, ff_share.at[1]), job(grad2, None, line=False)]
    go = lambda job, *stages: [job.stage(t) for t in stages if t < job.stages]
    early_loads = [
        pltpu.make_async_copy(p, e.sums.at[0], load.at[2 + i]) for i, (p, e) in enumerate(zip((part0,), early))
    ]
    for one in early_loads:
        one.start()
    go(late[0], 0)
    go(late[1], 0)
    go(late[0], 1)
    own.wait()
    qkv_load.wait()

    blocks = keys // QUERIES
    total = pairs * blocks

    def probs_copy(it):
        slot = lax.rem(it, 2)
        pair, q = lax.div(it, blocks), lax.rem(it, blocks)
        return pltpu.make_async_copy(probs.at[pair, :, part(q, QUERIES)], pbuf.at[slot], psem.at[slot])

    probs_copy(0).start()
    hooks = {}

    def hook(it, *steps):
        hooks.setdefault(min(it, total - 1), []).extend(steps)

    zs = place.nz - 1
    rest_of = lambda job, t: [(job, s) for s in range(t, job.stages)]
    hook(0, *[lambda one=one: one.wait() for one in early_loads], (early[0], 0))
    hook(total * 2 // 16, (early[0], 1))
    hook(total * 4 // 16, (late[0], 2), *[(early[0], t) for t in range(2, zs)])
    hook(total * 5 // 16, (late[1], 1))
    hook(total * 6 // 16, (early[0], zs))
    hook(total * 8 // 16, (late[0], 3))
    hook(total * 10 // 16, (late[0], 4))
    hook(total * 11 // 16, (late[1], 2))
    hook(total * 12 // 16, (late[0], 5))

    def body(it, carry):
        pair, q = lax.div(it, blocks), lax.rem(it, blocks)
        at, slot = part(q, QUERIES), lax.rem(it, 2)
        for when, steps in hooks.items():
            pl.when(it == when)(lambda steps=steps: perform(steps))

        @pl.when(it + 1 < total)
        def _():
            probs_copy(it + 1).start()

        probs_copy(it).wait()

        @pl.when(q == 0)
        def _():
            for r in range(1, nz):
                att_copy(r, pair).wait_recv()
            pl.when(pair + 2 < pairs)(lambda: att_start(pair + 2))
            dk[...] = jnp.zeros_like(dk)
            dv[...] = jnp.zeros_like(dv)

        do = dout[at, part(pair, 128)]
        q_t[...] = qkv[0, pair, at, :].T
        do_t[...] = do.T
        block = lax.div(pair, pz)
        column = lambda t: part((block * 3 + t) * pz + lax.rem(pair, pz), 128)
        dqkv[at, column(0)] = backward_tile(qkv, do, do_t, q_t, pair, lambda i: pbuf[slot, i], dk, dv)

        @pl.when(q == blocks - 1)
        def _():
            dqkv[:, column(1)] = dk[...].T.astype(BF16)
            dqkv[:, column(2)] = dv[...].T.astype(BF16)

        return carry

    lax.fori_loop(0, total, body, 0)
    go(late[0], *range(6, late[0].stages))
    go(late[1], *range(3, late[1].stages))
    part_copy = pltpu.make_async_copy(late[1].sums.at[0], part2, load.at[0])
    part_copy.start()
    for pair in range(pairs):
        for r in range(1, nz):
            att_copy(r, pair).wait_send()
    part_copy.wait()
    place.drain()


def attention_back(nb, nz, att_grad, qkv, probs, part0, grad1, grad2):
    _, pairs, keys, _ = qkv.shape
    S, V, D = jax.ShapeDtypeStruct, pltpu.VMEM, pltpu.SemaphoreType.DMA
    _, r, wide = grad2.shape
    scratch = [
        V((3, pairs, keys, 128), BF16),
        V((keys, pairs * 128), BF16),
        V((2, 2, QUERIES, keys), BF16),
        V((128, keys), F32),
        V((128, keys), F32),
        V((128, QUERIES), BF16),
        V((128, QUERIES), BF16),
        D((4,)), D((2,)), D((pairs * (nz - 1),)), D((pairs * (nz - 1),)),
    ]
    scratch += Scatter.scratch(nb, nz, r, wide, plane=False)
    scratch += Scatter.scratch(nb, nz, r, wide)
    scratch += Scatter.scratch(nb, nz, r, wide, line=False)
    return pl.pallas_call(
        functools.partial(attention_kernel, nb, nz),
        out_shape=[
            S((keys, 3 * pairs * 128), BF16),
            S((2, r, wide // nz), F32),
            S((r, wide), BF16),
        ],
        in_specs=[ANY] * 6,
        out_specs=[WHOLE, WHOLE, ANY],
        scratch_shapes=scratch,
        compiler_params=pltpu.CompilerParams(
            collective_id=1, has_side_effects=True, vmem_limit_bytes=VMEM_LIMIT
        ),
    )(att_grad, qkv, probs, part0, grad1, grad2)


def first_kernel(
    nb, nz, dqkv_in, everything_in, qkvw_in, x, skip_x, skip_w, mixed_in, middle_in, norms, second_sums, ff_early, part2, grad3, out_grad,
    input_grad, skip_grad, query_out, key_out, value_out, skip_share, norm_share, up_out, down_out, out_out,
    qkv_share, ff_share, out_share,
    dqkv, everything, qkvw, mixed, middle_grad,
    qkv_grad, skip_w_grad, spare, joined, joined_t, mixed_low, ahead, mine, from_mate, to_partner, from_partner,
    sums, packed, norm_in, norm_line, load, swap_send, swap_recv, norm_send, norm_recv, *rest,
):
    place = Place(nb, nz)
    z, group, k, half = place.z, place.group, place.k, place.half
    frames = x.shape[0] // 2
    width = x.shape[1]
    loads = [
        pltpu.make_async_copy(src, dst, load.at[i])
        for i, (src, dst) in enumerate(
            (
                (dqkv_in, dqkv),
                (qkvw_in, qkvw),
                (everything_in, everything),
                (mixed_in, mixed),
                (middle_in, middle_grad),
                (x, joined.at[:, pl.ds(0, width)]),
                (skip_x, joined.at[:, pl.ds(width, width)]),
            )
        )
    ]
    rest = list(rest)

    def job(full, share, paired=False, **kind):
        count = 3 + sum(kind.get(key, True) and size for key, size in (("sums", 1), ("plane", 2), ("line", 1)))
        mine = [rest.pop(0) for _ in range(count)]
        return Scatter(place, full, share, mine, paired, **kind)

    for one in loads:
        one.start()
    place.greet()
    line_job = job(None, ff_share.at[0], plane=False)
    ff_job = job(grad3, ff_share.at[1])
    out_job = job(out_grad, out_share)
    qkv_job = job(qkv_grad, qkv_share, True, sums=False)
    rs = skip_w_grad.shape[2]
    skips = [job(skip_w_grad.at[h], skip_share.at[pl.ds(h * rs, rs)], sums=False) for h in (0, 1)]
    loads.append(pltpu.make_async_copy(part2, line_job.sums.at[0], load.at[7]))
    loads[7].start()

    def go(job, *stages):
        for t in stages:
            if t < job.stages:
                job.stage(t)

    go(ff_job, 0)
    go(out_job, 0)
    for one in loads[:2]:
        one.wait()

    def mate_copy(r, t):
        slot = (r - 1) * 2 + t
        return remote(
            ahead.at[slot], from_mate.at[slot], swap_send.at[slot], swap_recv.at[slot], (place.b, place.mate(r))
        )

    for r in range(1, half):
        for s in (0, 1):
            block = lax.rem(k + r, half) + (1 - group if s == 0 else group) * half
            ahead[(r - 1) * 2 + s] = nt(dqkv[part(block, frames), :], qkvw[...]).astype(BF16)
        place.start(mate_copy, r, 0)
    for s in (0, 1):
        block = k + (1 - group if s == 0 else group) * half
        mine[s] = nt(dqkv[part(block, frames), :], qkvw[...])
    loads[2].wait()
    turned = everything[...].T
    rq = qkv_grad.shape[1]
    for j in range(nb):
        qkv_grad[flip(place.b, j)] = nn(turned[j * rq : (j + 1) * rq, :], dqkv[...]).astype(BF16)
    weights = [everything.at[pl.ds(0, width)], qkvw.at[:, pl.ds(0, width)] if qkvw.shape[1] >= width else spare]
    for i, ref in enumerate(weights):
        loads.append(pltpu.make_async_copy(skip_w.at[pl.ds(i * width, width)], ref, load.at[8 + i]))
        loads[-1].start()
    go(ff_job, 1)
    go(qkv_job, 0)
    go(out_job, 1)

    def add_mates(s):
        for r in range(1, half):
            mate_copy(r, s).wait_recv()
            slot = (r - 1) * 2 + s

            def body(at):
                mine[s, at] = mine[s, at] + from_mate[slot, at].astype(F32)

            rowwise(frames, 16, body)

    add_mates(0)
    sem = 2 * (half - 1)
    across = lambda: remote(to_partner, from_partner, swap_send.at[sem], swap_recv.at[sem], (place.b, place.partner))

    def narrow(at):
        to_partner[at] = mine[0, at].astype(BF16)

    rowwise(frames, 16, narrow)
    place.start(across)
    for r in range(1, half):
        place.start(mate_copy, r, 1)
    for one in loads[3:8]:
        one.wait()
    joined_t[...] = joined[...].T
    go(qkv_job, 1)
    go(ff_job, 2)
    go(out_job, 2)

    sums[...] = jnp.zeros_like(sums)
    gain = norms[0:1, :]

    def back(item, grad):
        def body(i, carry):
            at = part(i, 32)
            to = pl.ds(pl.multiple_of(item * frames + i * 32, 32), 32)
            part_grad = norm_back(grad(at), mixed[to, :], gain, sums.at[0], sums.at[1])
            mixed_low[to, :] = (middle_grad[to, :] + part_grad).astype(BF16)
            return carry

        lax.fori_loop(0, frames // 32, body, 0)

    add_mates(1)
    back(group, lambda at: mine[1, at])
    go(qkv_job, 2)
    go(ff_job, 3)
    across().wait_recv()
    back(1 - group, lambda at: from_partner[at].astype(F32))
    for h in (0, 1):
        for j in range(nb):
            block = slice((2 * j + h) * rs, (2 * j + h + 1) * rs)
            skip_w_grad[h, flip(place.b, j)] = nn(joined_t[block, :], mixed_low[...]).astype(BF16)
        go(skips[h], 0)

    total = lambda a: jnp.sum(a, 0, keepdims=True)
    for i, v in enumerate((sums[0], sums[1], second_sums[0], second_sums[1])):
        packed[i : i + 1, :] = total(v)
    packed[4:8, :] = jnp.zeros_like(packed[4:8, :])
    bits = [0] + place.rest
    norm_copy = lambda i: remote(
        packed, norm_in.at[i], norm_send.at[i], norm_recv.at[i], place.at(1 << bits[i])
    )
    c = norm_share.shape[1]
    line_copy = lambda r: remote(
        packed.at[:, part(lax.rem(z + r, nz), c)], norm_line.at[r - 1],
        norm_send.at[len(bits) + r - 1], norm_recv.at[len(bits) + r - 1], (place.b, lax.rem(z + r, nz)),
    )

    def norm_step(i):
        if i > 0:
            norm_copy(i - 1).wait()
            packed[...] = packed[...] + norm_in[i - 1]
        if i < len(bits):
            norm_copy(i).start()
        else:
            for r in range(1, nz):
                line_copy(r).start()

    norm_step(0)
    go(out_job, 3)
    go(qkv_job, 3)
    go(line_job, 0)
    go(skips[0], 1)
    go(skips[1], 1)
    norm_step(1)
    go(ff_job, 4)
    go(out_job, 4)
    go(line_job, 1)
    for one in loads[8:]:
        one.wait()
    input_grad[...] = nt(mixed_low[...], weights[0][...])
    go(skips[0], 2)
    norm_step(2)
    go(ff_job, 5)
    go(out_job, 5)
    go(line_job, 2)
    go(qkv_job, *range(4, qkv_job.stages))
    skip_grad[...] = nt(mixed_low[...], weights[1][...])
    go(skips[1], 2)
    norm_step(3)
    go(ff_job, *range(6, ff_job.stages))
    go(out_job, *range(6, out_job.stages))
    go(line_job, *range(3, line_job.stages))
    for i in range(4, len(bits) + 1):
        norm_step(i)
    for i, ref in enumerate((query_out, key_out, value_out)):
        ref[...] = qkv_share[:, i * c : (i + 1) * c]
    out_out[...] = out_share[...].T
    cw = ff_share.shape[2] // 2
    for i in range(4):
        source = ff_early.at[i] if i < 2 else ff_share.at[i - 2]
        up_out[:, i * cw : (i + 1) * cw] = source[:, :cw]
        down_out[i * cw : (i + 1) * cw, :] = source[:, cw:].T
    for t in range(3, skips[0].stages):
        go(skips[0], t)
        go(skips[1], t)
    value = packed[:, part(z, c)]
    for r in range(1, nz):
        line_copy(r).wait()
        value = value + norm_line[r - 1]
    norm_share[...] = value
    place.drain()


def first_back(nb, nz, dqkv, everything, qkvw, x, skip_x, skip_w, mixed, middle_grad, norms, second_sums, ff_early, part2, grad3, out_grad):
    rows, width = x.shape
    frames = rows // 2
    half = nz // 2
    c = width // nz
    S, V, D = jax.ShapeDtypeStruct, pltpu.VMEM, pltpu.SemaphoreType.DMA
    qkv_wide = qkvw.shape[1]
    bits = nb.bit_length() - 1
    swaps = 2 * (half - 1)
    r, wide = ff_early.shape[1:]
    scratch = [
        V((r, 3 * c), F32),
        V((2, r, wide), F32),
        V((r, c), F32),
        V(dqkv.shape, BF16),
        V(everything.shape, BF16),
        V(qkvw.shape, BF16),
        V((rows, width), F32),
        V((rows, width), F32),
        V((nb, qkvw.shape[0] // nb, qkv_wide), BF16),
        V((2, nb, skip_w.shape[0] // nb // 2, width), BF16),
        V((width, width) if qkv_wide < width else (16, 128), BF16),
        V((rows, 2 * width), BF16),
        V((2 * width, rows), BF16),
        V((rows, width), BF16),
        V((max(swaps, 1), frames, width), BF16),
        V((2, frames, width), F32),
        V((max(swaps, 1), frames, width), BF16),
        V((frames, width), BF16),
        V((frames, width), BF16),
        V((2, 8, width), F32),
        V((8, width), F32),
        V((bits, 8, width), F32),
        V((nz - 1, 8, c), F32),
        D((10,)), D((swaps + 1,)), D((swaps + 1,)), D((bits + nz - 1,)), D((bits + nz - 1,)),
    ]
    scratch += Scatter.scratch(nb, nz, grad3.shape[1], grad3.shape[2], plane=False)
    scratch += Scatter.scratch(nb, nz, grad3.shape[1], grad3.shape[2])
    scratch += Scatter.scratch(nb, nz, out_grad.shape[1], out_grad.shape[2])
    scratch += Scatter.scratch(nb, nz, qkvw.shape[0] // nb, qkv_wide, True, sums=False)
    for _ in (0, 1):
        scratch += Scatter.scratch(nb, nz, skip_w.shape[0] // nb // 2, width, sums=False)
    return pl.pallas_call(
        functools.partial(first_kernel, nb, nz),
        out_shape=[
            S((rows, width), F32),
            S((rows, width), F32),
            *[S((r, c), F32)] * 3,
            S((skip_w.shape[0] // nb, c), F32),
            S((8, c), F32),
            S((r, 2 * wide), F32),
            S((2 * wide, r), F32),
            S((c, r), F32),
        ],
        in_specs=[ANY] * 8 + [WHOLE] * 3 + [ANY] * 3,
        out_specs=[WHOLE] * 10,
        scratch_shapes=scratch,
        compiler_params=pltpu.CompilerParams(
            collective_id=2, has_side_effects=True, vmem_limit_bytes=VMEM_LIMIT
        ),
    )(dqkv, everything, qkvw, x, skip_x, skip_w, mixed, middle_grad, norms, second_sums, ff_early, part2, grad3, out_grad)


def shards(
    inputs,
    skip_input,
    lengths,
    skip_weight,
    query_weight,
    key_weight,
    value_weight,
    out_weight,
    up_weight,
    down_weight,
    first_gain,
    first_shift,
    second_gain,
    second_shift,
    cotangent,
):
    nb, nz = lax.axis_size("batch"), lax.axis_size("seq")
    shape = inputs.shape
    flat = lambda a: a.reshape(shape[0] * shape[1], shape[2])
    x, skip_x, cot = flat(inputs), flat(skip_input), flat(cotangent)
    norms = (first_gain, first_shift, second_gain, second_shift)
    qkv_w = (query_weight, key_weight, value_weight)
    (mixed, everything, gains, skip_w, qkvw, out_t, ff0, ff1, ff2, ff3_w, qkv, probs, attended) = forward(
        nb, nz, lengths, x, skip_x, norms, skip_weight, qkv_w, out_weight, up_weight, down_weight
    )
    output, middle_grad, att_grad, out_grad, part0, grad1, grad2, grad3, second_sums, _ = ffn(
        nb, nz, mixed, attended, out_t, gains, cot, ff0, ff1, ff2, ff3_w
    )
    dqkv, ff_early, part2 = attention_back(nb, nz, att_grad, qkv, probs, part0, grad1, grad2)
    input_grad, skip_grad, query_share, key_share, value_share, skip_share, norm_share, up_share, down_share, out_share = (
        first_back(
            nb, nz, dqkv, everything, qkvw, x, skip_x, skip_w, mixed, middle_grad, gains, second_sums, ff_early, part2,
            grad3, out_grad,
        )
    )
    return (
        output.reshape(shape),
        input_grad.reshape(shape),
        skip_grad.reshape(shape),
        skip_share,
        query_share,
        key_share,
        value_share,
        out_share,
        up_share,
        down_share,
        norm_share[0],
        norm_share[1],
        norm_share[2],
        norm_share[3],
    )


def solution(mesh):
    rows = P("batch", "seq", None)
    weight, turned, norm = P("batch", "seq"), P("seq", "batch"), P("seq")
    return jax.shard_map(
        shards,
        mesh=mesh,
        in_specs=(rows, rows, P("batch"), *[weight] * 4, turned, weight, turned, *[norm] * 4, rows),
        out_specs=(rows, rows, rows, *[weight] * 4, turned, weight, turned, *[norm] * 4),
        check_vma=False,
    )
```

```python
import functools

import jax
import jax.numpy as jnp
from jax import lax
from jax.experimental import pallas as pl
from jax.experimental.pallas import tpu as pltpu
from jax.sharding import PartitionSpec as P

HEADS = 16
HEAD_DIM = 64
EPSILON = 1e-05
LOG2E = 1.4426950408889634
QUERIES = 512
F32 = jnp.float32
BF16 = jnp.bfloat16
MESH = pl.DeviceIdType.MESH
VMEM_LIMIT = 60 * 2**20
ANY = pl.BlockSpec(memory_space=pl.ANY)
WHOLE = pl.BlockSpec(memory_space=pltpu.VMEM)


def nt(a, b):
    return lax.dot_general(a, b, (((1,), (1,)), ((), ())), preferred_element_type=F32)


def nn(a, b):
    return jnp.dot(a, b, preferred_element_type=F32)


def part(index, size):
    if isinstance(index, int):
        return pl.ds(index * size, size)
    return pl.ds(pl.multiple_of(index * size, size), size)


def rowwise(rows, step, body):
    def run(i, carry):
        body(part(i, step))
        return carry

    lax.fori_loop(0, rows // step, run, 0)


def flip(index, mask):
    result = index
    bit = 0
    while mask >> bit:
        if (mask >> bit) & 1:
            on = lax.rem(lax.div(index, 1 << bit), 2)
            result = result + (1 << bit) * (1 - 2 * on)
        bit += 1
    return result


def span(bits):
    masks = [0]
    for bit in bits:
        masks = masks + [m | (1 << bit) for m in masks]
    return masks


class Place:
    def __init__(self, nb, nz):
        self.nb, self.nz = nb, nz
        self.b = lax.axis_index("batch")
        self.z = lax.axis_index("seq")
        self.half = nz // 2
        self.group = lax.div(self.z, self.half)
        self.k = lax.rem(self.z, self.half)
        self.partner = lax.rem(self.z + self.half, nz)
        self.rest = list(range(1, nb.bit_length() - 1))
        self.orders = (self.rest, self.rest[::-1])
        self.pending = []

    def at(self, mask):
        return (flip(self.b, mask), self.z)

    def mate(self, r):
        return self.group * self.half + lax.rem(self.k + r, self.half)

    def greet(self):
        barrier = pltpu.get_barrier_semaphore()
        targets = [self.at(1 << k) for k in [0] + self.rest]
        targets += [(self.b, lax.rem(self.z + r, self.nz)) for r in range(1, self.nz)]
        for t in targets:
            pl.semaphore_signal(barrier, inc=1, device_id=t, device_id_type=MESH)
        pl.semaphore_wait(barrier, len(targets))

    def start(self, make, *args):
        copy, ok = self.unpack(make(*args))
        if ok is None:
            copy.start()
        else:
            pl.when(ok)(lambda: copy.start())
        self.pending.append((make, args))

    def drain(self):
        for make, args in self.pending:
            copy, ok = self.unpack(make(*args))
            if ok is None:
                copy.wait_send()
            else:
                pl.when(ok)(lambda copy=copy: copy.wait_send())
        self.pending = []

    @staticmethod
    def unpack(made):
        return made if isinstance(made, tuple) else (made, None)


def remote(src, dst, send, recv, device):
    return pltpu.make_async_remote_copy(
        src_ref=src, dst_ref=dst, send_sem=send, recv_sem=recv, device_id=device, device_id_type=MESH
    )


class Gather:
    @staticmethod
    def sems(nb, nz):
        return max(2 * (nz - 1), 6) + 2 * (nb // 2 - 1) + nb

    @staticmethod
    def scratch(nb, nz):
        count = Gather.sems(nb, nz)
        return [pltpu.SemaphoreType.DMA((3,))] + [pltpu.SemaphoreType.DMA((count,))] * 2

    def __init__(self, place, shard, full, scratch, paired=False, h=0, of=1):
        self.p, self.full, self.paired, self.h, self.of = place, full, paired, h, of
        self.shards = shard if paired else [shard]
        self.shard = self.shards[0]
        self.local, self.send, self.recv = scratch
        self.r, self.c = self.shard.shape
        nb, nz = place.nb, place.nz
        self.xy0 = max(2 * (nz - 1), 6)
        self.core0 = self.xy0 + 2 * (nb // 2 - 1)
        self.zsteps = 1 if paired else nz - 1
        self.stages = self.zsteps + len(place.rest) + 2

    def column(self, index):
        return self.full.at[part(self.p.b * self.of + self.h, self.r), part(index, self.c)]

    def line(self, way, step):
        p, n = self.p, self.p.nz
        sem = (0 if way > 0 else n - 1) + step - 1
        sent, got = p.z - way * (step - 1), p.z - way * step
        inside = lambda v: (v >= 0) & (v < n)
        clip = lambda v: jnp.clip(v, 0, n - 1)
        to = (p.b, clip(p.z + way))
        block = self.column(clip(sent))
        out = lambda: remote(self.shard if step == 1 else block, block, self.send.at[sem], self.recv.at[sem], to)
        land = self.column(clip(got))
        into = lambda: remote(land, land, self.send.at[sem], self.recv.at[sem], to)
        return out, into, inside(sent) & inside(p.z + way), inside(got)

    def zstart(self, step):
        p = self.p
        if self.paired:
            for t in (0, 1):
                for i in range(len(self.shards)):
                    p.start(self.paircopy, t, i)
            return
        for way in (1, -1):
            p.start(self.lineout, way, step)

    def lineout(self, way, step):
        out, _, can_send, _ = self.line(way, step)
        return out(), can_send

    def paircopy(self, t, i):
        p, count = self.p, len(self.shards)
        target = lax.div(p.z, 2) + t * p.half
        slot = lax.rem(p.z, 2) * count + i
        copy = remote(
            self.shards[i], self.column(slot), self.send.at[t * count + i], self.recv.at[slot], (p.b, target)
        )
        return copy, target != p.z

    def zwait(self, step):
        p = self.p
        if self.paired:
            for s in (0, 1):

                @pl.when(2 * p.k + s != p.z)
                def _(s=s):
                    for i in range(len(self.shards)):
                        slot = s * len(self.shards) + i
                        land = self.column(slot)
                        remote(land, land, self.send.at[slot], self.recv.at[slot], (p.b, p.partner)).wait_recv()

            return
        for way in (1, -1):
            _, into, _, can_get = self.line(way, step)
            pl.when(can_get)(lambda into=into: into().wait_recv())

    def owncopy(self, act):
        p, count = self.p, len(self.shards)
        place = lax.rem(p.z, 2) if self.paired else p.z
        copies = lambda: [
            pltpu.make_async_copy(shard, self.column(place * count + i), self.local.at[i])
            for i, shard in enumerate(self.shards)
        ]
        if self.paired:
            pl.when((2 * p.k == p.z) | (2 * p.k + 1 == p.z))(lambda: [act(copy) for copy in copies()][:0] or None)
        else:
            act(copies()[0])

    def rows(self, mask, half):
        h = self.r // 2
        return self.full.at[part((flip(self.p.b, mask) * self.of + self.h) * 2 + half, h)]

    def hop(self, sem, mask, half, bit, incoming):
        block = self.rows(mask | bit if incoming else mask, half)
        return remote(block, block, self.send.at[sem], self.recv.at[sem], self.p.at(bit))

    def plane(self, j):
        made = []
        for half in (0, 1):
            order = self.p.orders[half]
            for i, m in enumerate(span(order[:j])):
                sem = self.xy0 + half * (self.p.nb // 2 - 1) + (1 << j) - 1 + i
                made.append((half, m, 1 << order[j], sem))
        return made

    def coresem(self, mask, half):
        return self.core0 + (mask >> 1) * 2 + half

    def corestart(self, mask, half):
        self.p.start(self.hop, self.coresem(mask, half), mask, half, 1, False)

    def stage(self, t):
        p = self.p
        nx = len(p.rest)
        if t == 0:
            self.owncopy(lambda copy: copy.start())
            self.zstart(1)
        if 1 <= t <= self.zsteps:
            self.zwait(t)
            if t < self.zsteps:
                self.zstart(t + 1)
            else:
                self.owncopy(lambda copy: copy.wait())
        j = t - self.zsteps
        if 1 <= j <= nx:
            for half, m, bit, sem in self.plane(j - 1):
                self.hop(sem, m, half, bit, True).wait_recv()
        if 0 <= j < nx:
            for half, m, bit, sem in self.plane(j):
                p.start(self.hop, sem, m, half, bit, False)
        if j == 0:
            for half in (0, 1):
                self.corestart(0, half)
        if 1 <= j <= nx:
            for half, m, bit, _ in self.plane(j - 1):
                self.corestart(m | bit, half)
        if j == nx + 1:
            for m in span(p.rest):
                for half in (0, 1):
                    self.hop(self.coresem(m, half), m, half, 1, True).wait_recv()


class Scatter:
    @staticmethod
    def scratch(nb, nz, r, wide, paired=False, sums=True, plane=True, line=True):
        c = wide // (2 if paired else nz)
        lines = 2 if paired else 2 * (nz - 1)
        count = nb // 2 + 2 * (nb // 2 - 1) + lines
        made = [pltpu.VMEM((nb // 2 if plane else 1, r, wide), BF16)] if sums else []
        if plane:
            made += [
                pltpu.VMEM((nb // 2, r, wide), BF16),
                pltpu.VMEM((2 * (nb // 2 - 1), r // 2, wide), BF16),
            ]
        if line:
            made += [pltpu.VMEM((lines, r, c), BF16)]
        return made + [
            pltpu.SemaphoreType.DMA((nb // 2,)),
            pltpu.SemaphoreType.DMA((count,)),
            pltpu.SemaphoreType.DMA((count,)),
        ]

    def __init__(self, place, full, share, scratch, paired=False, sums=True, plane=True, line=True):
        self.p, self.full, self.share, self.paired = place, full, share, paired
        scratch = list(scratch)
        self.sums = scratch.pop(0) if sums else None
        self.core, self.flat = (scratch.pop(0), scratch.pop(0)) if plane else (None, None)
        self.got = scratch.pop(0) if line else None
        self.local, self.send, self.recv = scratch
        self.has_plane, self.has_line = plane, line
        _, self.r, self.wide = (full if plane else self.sums).shape
        self.c = self.wide // (2 if paired else place.nz)
        self.zsteps = 1 if paired else place.nz - 1
        self.nx = len(place.rest)
        self.plane_stages = 2 + self.nx
        self.stages = (self.plane_stages if plane else 1) + (self.zsteps if line else 0)
        self.zsem = place.nb // 2 + 2 * (place.nb // 2 - 1)
        self.masks = sorted(span(place.rest))

    def sum(self, m):
        return self.full.at[m] if self.sums is None else self.sums.at[m >> 1]

    def add(self, target, source):
        def body(at):
            target[at] = target[at] + source[at]

        rowwise(target.shape[0], 16, body)

    def corecopy(self, i, m):
        return remote(self.full.at[m | 1], self.core.at[i], self.send.at[i], self.recv.at[i], self.p.at(1))

    def load(self, i, m):
        return pltpu.make_async_copy(self.full.at[m], self.sum(m), self.local.at[i])

    def rows(self, m, half):
        return self.sum(m).at[part(half, self.r // 2)]

    def plane(self, j):
        p = self.p
        made = []
        for half in (0, 1):
            order = p.orders[half]
            base = half * (p.nb // 2 - 1) + sum(len(span(order[q + 1 :])) for q in range(j))
            for i, m in enumerate(span(order[j + 1 :])):
                made.append((half, m, 1 << order[j], base + i))
        return made

    def planecopy(self, half, m, bit, slot):
        sem = self.p.nb // 2 + slot
        return remote(
            self.rows(m | bit, half), self.flat.at[slot], self.send.at[sem], self.recv.at[sem], self.p.at(bit)
        )

    def column(self, index):
        return self.sum(0).at[:, part(index, self.c)]

    def line(self, way, step):
        p, n = self.p, self.p.nz
        here = p.z if way > 0 else n - 1 - p.z
        goes = n + here - step
        comes = goes - 1
        can_send = (goes > here) & (goes <= n - 1)
        can_get = (comes >= here) & (comes <= n - 1) & (here > 0)
        unfold = lambda d: jnp.clip(d if way > 0 else n - 1 - d, 0, n - 1)
        slot = (0 if way > 0 else n - 1) + step - 1
        copy = remote(
            self.column(unfold(goes)),
            self.got.at[slot],
            self.send.at[self.zsem + slot],
            self.recv.at[self.zsem + slot],
            (p.b, jnp.clip(p.z + way, 0, n - 1)),
        )
        return copy, can_send, can_get, unfold(comes), slot

    def paircopy(self, s):
        p = self.p
        copy = remote(
            self.column(s),
            self.got.at[p.group],
            self.send.at[self.zsem + s],
            self.recv.at[self.zsem + p.group],
            (p.b, 2 * p.k + s),
        )
        return copy, 2 * p.k + s != p.z

    def lineout(self, way, step):
        return self.line(way, step)[:2]

    def zstart(self, step):
        p = self.p
        if self.paired:
            for s in (0, 1):
                p.start(self.paircopy, s)
            return
        for way in (1, -1):
            p.start(self.lineout, way, step)

    def zwait(self, step):
        p = self.p
        if self.paired:
            for t in (0, 1):
                copy = remote(
                    self.column(0),
                    self.got.at[t],
                    self.send.at[self.zsem + t],
                    self.recv.at[self.zsem + t],
                    (p.b, p.partner),
                )
                pl.when(lax.div(p.z, 2) + t * p.half != p.z)(lambda copy=copy: copy.wait_recv())
            return
        for way in (1, -1):
            copy, _, can_get, column, slot = self.line(way, step)

            @pl.when(can_get)
            def _(copy=copy, column=column, slot=slot):
                copy.wait_recv()
                if step < self.zsteps:
                    self.add(self.column(column), self.got.at[slot])

    def stage(self, t):
        p, nx = self.p, self.nx
        s = t - (self.plane_stages - 1 if self.has_plane else 0)
        if self.has_plane:
            if t == 0:
                for i, m in enumerate(self.masks):
                    p.start(self.corecopy, i, m)
                    if self.sums is not None:
                        self.load(i, m).start()
            if t == 1:
                for i, m in enumerate(self.masks):
                    if self.sums is not None:
                        self.load(i, m).wait()
                    self.corecopy(i, m).wait_recv()
                    self.add(self.sum(m), self.core.at[i])
            j = t - 1
            if 1 <= j <= nx:
                for half, m, bit, slot in self.plane(j - 1):
                    self.planecopy(half, m, bit, slot).wait_recv()
                    self.add(self.rows(m, half), self.flat.at[slot])
            if 0 <= j < nx:
                for half, m, bit, slot in self.plane(j):
                    p.start(self.planecopy, half, m, bit, slot)
        if self.has_line:
            if 1 <= s <= self.zsteps:
                self.zwait(s)
            if 0 <= s < self.zsteps:
                self.zstart(s + 1)
            if t == self.stages - 1:
                self.finish()

    def finish(self):
        p = self.p
        if self.paired:
            mine = (2 * p.k == p.z) | (2 * p.k + 1 == p.z)
            own = lax.rem(p.z, 2)
            terms = [(self.got.at[t], lax.div(p.z, 2) + t * p.half != p.z) for t in (0, 1)]
        else:
            mine = None
            own = p.z
            n = p.nz
            terms = [(self.got.at[n - 2], p.z > 0), (self.got.at[2 * n - 3], p.z < n - 1)]
        source = self.column(own)

        def first(at):
            value = source[at].astype(F32)
            self.share[at] = value if mine is None else jnp.where(mine, value, 0.0)

        rowwise(self.r, 16, first)
        for ref, ok in terms:

            @pl.when(ok)
            def _(ref=ref):
                def more(at):
                    self.share[at] = self.share[at] + ref[at].astype(F32)

                rowwise(self.r, 16, more)


def perform(steps):
    for step in steps:
        if callable(step):
            step()
        else:
            step[0].stage(step[1])


def normalise(v):
    centred = v - jnp.mean(v, 1, keepdims=True)
    scale = lax.rsqrt(jnp.mean(centred * centred, 1, keepdims=True) + EPSILON)
    return centred * scale, scale


def norm_back(g, v, gain, gain_sum, shift_sum):
    n, scale = normalise(v)
    fold = lambda a: sum(a[i * 8 : (i + 1) * 8] for i in range(a.shape[0] // 8))
    gain_sum[...] += fold(g * n)
    shift_sum[...] += fold(g)
    gg = g * gain
    return (gg - jnp.mean(gg, 1, keepdims=True) - n * jnp.mean(gg * n, 1, keepdims=True)) * scale


def own_half(value, i):
    lane = lax.broadcasted_iota(jnp.int32, value.shape, 1)
    return jnp.where((lane >= HEAD_DIM) if i else (lane < HEAD_DIM), value, jnp.zeros_like(value))


def merge_halves(a, b):
    lane = lax.broadcasted_iota(jnp.int32, a.shape, 1)
    return jnp.where(lane < HEAD_DIM, a, b)


def project(normed, weight, qkv, pz):
    c = pz * 128
    rows = normed.shape[0]
    for j in (0, 1):
        for t in range(3):
            for i in range(rows // 512):
                at = pl.ds(i * 512, 512)
                y = nn(normed[at, :], weight[:, pl.ds((j * 3 + t) * c, c)])
                if t == 0:
                    y = y.astype(BF16).astype(F32) * HEAD_DIM**-0.5
                for w in range(pz):
                    qkv[t, j * pz + w, at, :] = y[:, w * 128 : (w + 1) * 128].astype(BF16)


def distances(dist, length):
    rows, cols = dist.shape

    def body(i, carry):
        row = lax.broadcasted_iota(jnp.int32, (64, cols), 0) + i * 64
        col = lax.broadcasted_iota(jnp.int32, (64, cols), 1)
        gap = jnp.abs(row - col).astype(F32)
        dist[part(i, 64), :] = jnp.where(col < length, gap, 1e33)
        return carry

    lax.fori_loop(0, rows // 64, body, 0)


def forward_tile(qkv, dist, pair, first_head, at, store):
    q, k, v = qkv[0, pair, at, :], qkv[1, pair], qkv[2, pair]
    gap = dist[at, :]
    outs = []
    for i in range(2):
        head = (first_head + 2 * pair + i + 1).astype(F32)
        slope = jnp.exp2(jnp.full((1, 1), -8.0 / HEADS, F32) * head) * LOG2E
        x = nt(own_half(q, i), k) * LOG2E - gap * slope
        e = jnp.exp2(x - jnp.max(x, 1, keepdims=True))
        p = (e * (1.0 / jnp.sum(e, 1, keepdims=True))).astype(BF16)
        store(i, p)
        outs.append(nn(p, v))
    return merge_halves(*outs).astype(BF16)


def backward_tile(qkv, do, do_t, q_t, pair, probs, dk, dv):
    k, v = qkv[1, pair], qkv[2, pair]
    dq = []
    for i in range(2):
        p = probs(i)
        rows = pl.ds(i * HEAD_DIM, HEAD_DIM)
        t = p.astype(F32) * nt(own_half(do, i), v)
        ds = (t - p.astype(F32) * jnp.sum(t, 1, keepdims=True)).astype(BF16)
        dq.append(nn(ds, k))
        dv[rows, :] += nn(do_t[rows, :], p)
        dk[rows, :] += nn(q_t[rows, :], ds)
    return (merge_halves(*dq) * HEAD_DIM**-0.5).astype(BF16)


def forward_kernel(
    nb, nz, lengths, x, skip_x, gain_one, shift_one, gain_two, shift_two,
    skip_w, query_w, key_w, value_w, out_w, up_w, down_w,
    mixed_out, normed_out, norms_out, skip_out, qkvw_out, out_out, ff0_out, ff1_out, ff2_out, ff3_w, qkv_out, probs, attended_out,
    skip, qkvw, joined, mixed, normed, everything, norms, gains, turned, ff_w, qkv, dist, pbuf, attended,
    load, ff_load, norm_send, norm_recv, swap_send, swap_recv, flush, psem, att_send, att_recv, *rest,
):
    place = Place(nb, nz)
    z, group, k, half = place.z, place.group, place.k, place.half
    frames = x.shape[0] // 2
    width = x.shape[1]
    keys = nz * frames
    c = norms.shape[1]
    cw = up_w.shape[1] // 4
    pz = c // 128
    pairs = 2 * pz
    place.greet()

    jobs = [rest[3 * i : 3 * i + 3] for i in range(7)]
    rs = skip_w.shape[0] // 2
    skips = [Gather(place, skip_w.at[pl.ds(h * rs, rs)], skip, jobs[h], h=h, of=2) for h in (0, 1)]
    qkv_job = Gather(place, [query_w, key_w, value_w], qkvw, jobs[2], True)
    out_job = Gather(place, turned, out_out, jobs[3])
    ff = [Gather(place, ff_w.at[i], o, jobs[4 + i]) for i, o in enumerate((ff0_out, ff1_out, ff2_out))]
    last = nz - 1

    def go(job, *stages):
        for t in stages:
            if t < job.stages:
                job.stage(t)

    def both(*stages):
        for t in stages:
            go(skips[0], t)
            go(skips[1], t)

    both(0)
    loads = [
        pltpu.make_async_copy(x, joined.at[:, pl.ds(0, width)], load.at[0]),
        pltpu.make_async_copy(skip_x, joined.at[:, pl.ds(width, width)], load.at[1]),
    ]
    up_loads = [
        pltpu.make_async_copy(up_w.at[:, pl.ds(i * cw, cw)], ff_w.at[i, :, pl.ds(0, cw)], ff_load.at[i]) for i in range(4)
    ]
    for one in loads + up_loads:
        one.start()
    norms[...] = jnp.zeros_like(norms)
    for i, ref in enumerate((gain_one, shift_one, gain_two, shift_two)):
        norms[i : i + 1, :] = ref[...].astype(F32).reshape(1, c)
    own_norms = pltpu.make_async_copy(norms, gains.at[:, part(z, c)], load.at[2])
    own_norms.start()
    norm_copy = lambda r: remote(
        norms, gains.at[:, part(z, c)], norm_send.at[r - 1], norm_recv.at[r - 1], (place.b, lax.rem(z + r, nz))
    )
    for r in range(1, nz):
        place.start(norm_copy, r)
    turned[...] = out_w[...].T
    down_t = down_w[...].T
    for i in range(4):
        ff_w[i, :, cw:] = down_t[:, i * cw : (i + 1) * cw]
    both(*range(1, last))
    go(qkv_job, 0)
    both(last)
    for one in up_loads:
        one.wait()
    go(ff[0], 0)
    both(last + 1)
    go(skips[0], last + 2)
    go(ff[0], *range(1, last))
    go(ff[1], 0)
    go(skips[1], last + 2)
    go(ff[1], *range(1, last - 1))
    go(qkv_job, 1)
    go(ff[0], last)
    both(*range(last + 3, skips[0].stages))
    go(ff[1], last - 1)
    flushes = []

    def out_copy(src, dst):
        copy = pltpu.make_async_copy(src, dst, flush.at[len(flushes)])
        flushes.append(copy)
        copy.start()

    out_copy(skip, skip_out)
    out_copy(ff_w.at[3], ff3_w)
    own_norms.wait()
    for one in loads:
        one.wait()
    for r in range(1, nz):
        norm_copy(r).wait_recv()
    out_copy(gains, norms_out)

    def across():
        return remote(
            normed.at[1 - group], everything.at[part(z, frames)], swap_send.at[0], swap_recv.at[0],
            (place.b, place.partner),
        )

    for turn in (0, 1):
        item = 1 - group if turn == 0 else group
        rows = part(item, frames)
        mixed[rows, :] = nn(joined[rows, :], skip[...])
        gain, shift = gains[0:1, :], gains[1:2, :]

        def body(i, carry):
            at = part(i, 32)
            at2 = pl.ds(pl.multiple_of(item * frames + i * 32, 32), 32)
            n, _ = normalise(mixed[at2, :])
            normed[item, at, :] = (n * gain + shift).astype(BF16)
            return carry

        lax.fori_loop(0, frames // 32, body, 0)
        if turn == 0:
            place.start(across)
            go(qkv_job, 2)
        else:
            own = pltpu.make_async_copy(normed.at[item], everything.at[part(z, frames)], load.at[0])
            own.start()

    def mate_copy(src, block, r, sem):
        return remote(
            src, everything.at[part(block, frames)], swap_send.at[sem], swap_recv.at[sem], (place.b, place.mate(r))
        )

    for r in range(1, half):
        place.start(mate_copy, normed.at[group], z, r, r)
    out_copy(mixed, mixed_out)
    go(ff[0], last + 1)
    go(ff[1], last)
    distances(dist, lengths[group])
    go(qkv_job, 3)
    go(ff[0], last + 2)
    across().wait_recv()
    for r in range(1, half):
        block = everything.at[part(place.partner, frames)]
        place.start(mate_copy, block, place.partner, r, half - 1 + r)
    go(ff[1], last + 1)
    go(qkv_job, *range(4, qkv_job.stages))
    out_copy(qkvw, qkvw_out)
    own.wait()
    for r in range(1, half):
        mate_copy(normed.at[group], z, r, r).wait_recv()
        mate_copy(normed.at[group], z, r, half - 1 + r).wait_recv()
    out_copy(everything, normed_out)
    go(ff[2], 0)
    go(out_job, 0)

    project(everything, qkvw, qkv, pz)
    out_copy(qkv, qkv_out)
    first_head = k * 2 * pairs
    blocks = keys // QUERIES
    total = pairs * blocks

    def probs_copy(slot, pair, at):
        return pltpu.make_async_copy(pbuf.at[slot], probs.at[pair, :, at], psem.at[slot])

    def att_copy(pair, r):
        owner = lax.rem(z + r, nz)
        slot = pair * (nz - 1) + r - 1
        return remote(
            attended.at[pair, part(owner, frames)],
            attended_out.at[part(group, frames), part(k * pairs + pair, 128)],
            att_send.at[slot], att_recv.at[slot], (place.b, owner),
        )

    def att_own(pair):
        return pltpu.make_async_copy(
            attended.at[pair, part(z, frames)],
            attended_out.at[part(group, frames), part(k * pairs + pair, 128)],
            flush.at[7 + pair],
        )

    hooks = {}

    def hook(it, *steps):
        hooks.setdefault(min(it, total - 1), []).extend(steps)

    rest_of = lambda job, t: [(job, s) for s in range(t, job.stages)]
    for t in range(1, last):
        hook(t - 1, (ff[2], t), (out_job, t))
    hook(last - 1, (ff[1], last + 2), (ff[2], last), (out_job, last))
    hook(total * 4 // 16, *rest_of(ff[0], last + 3))
    hook(total * 6 // 16, (ff[2], last + 1), (out_job, last + 1))
    hook(total * 8 // 16, *rest_of(ff[1], last + 3))
    hook(total * 13 // 16, (ff[2], last + 2))
    hook(total * 15 // 16, (out_job, last + 2))

    def body(it, carry):
        pair, q = lax.div(it, blocks), lax.rem(it, blocks)
        at, slot = part(q, QUERIES), lax.rem(it, 2)
        for when, steps in hooks.items():
            pl.when(it == when)(lambda steps=steps: perform(steps))

        @pl.when(it >= 2)
        def _():
            probs_copy(slot, pair, at).wait()

        def store(i, p):
            pbuf[slot, i] = p

        attended[pair, at, :] = forward_tile(qkv, dist, pair, first_head, at, store)
        probs_copy(slot, pair, at).start()

        @pl.when(q == blocks - 1)
        def _():
            for r in range(1, nz):
                att_copy(pair, r).start()

        return carry

    lax.fori_loop(0, total, body, 0)
    for pair in range(pairs):
        att_own(pair).start()
    go(ff[2], *range(last + 3, ff[2].stages))
    go(out_job, *range(last + 3, out_job.stages))
    for pair in range(pairs):
        for r in range(1, nz):
            att_copy(pair, r).wait()
    for pair in range(pairs):
        att_own(pair).wait()
    for slot in range(min(2, total)):
        probs_copy(slot, 0, pl.ds(0, QUERIES)).wait()
    for copy in flushes:
        copy.wait()
    place.drain()


def forward(nb, nz, lengths, x, skip_x, norms, skip_w, qkv_w, out_w, up_w, down_w):
    rows, width = x.shape
    frames = rows // 2
    keys = nz * frames
    c = width // nz
    pairs = 2 * c // 128
    r = up_w.shape[0]
    chunk = up_w.shape[1] // 2
    S, V, D = jax.ShapeDtypeStruct, pltpu.VMEM, pltpu.SemaphoreType.DMA
    out_shape = [
        S((rows, width), F32),
        S((keys, width), BF16),
        S((8, width), F32),
        S((nb * skip_w.shape[0], width), BF16),
        S((nb * r, 6 * c), BF16),
        S((nb * r, width), BF16),
        *[S((nb * r, nz * chunk), BF16)] * 3,
        S((r, chunk), BF16),
        S((3, pairs, keys, 128), BF16),
        S((pairs, 2, keys, keys), BF16),
        S((rows, width), BF16),
    ]
    scratch = [
        V((nb * skip_w.shape[0], width), BF16),
        V((nb * r, 6 * c), BF16),
        V((rows, 2 * width), BF16),
        V((rows, width), F32),
        V((2, frames, width), BF16),
        V((keys, width), BF16),
        V((8, c), F32),
        V((8, width), F32),
        V((r, c), BF16),
        V((4, r, chunk), BF16),
        V((3, pairs, keys, 128), BF16),
        V((keys, keys), F32),
        V((2, 2, QUERIES, keys), BF16),
        V((pairs, keys, 128), BF16),
    ]
    scratch += [D((3,)), D((4,)), D((nz - 1,)), D((nz - 1,)), D((nz - 1,)), D((nz - 1,)), D((7 + pairs,)), D((2,))]
    scratch += [D((pairs * (nz - 1),)), D((pairs * (nz - 1),))]
    for _ in range(7):
        scratch += Gather.scratch(nb, nz)
    return pl.pallas_call(
        functools.partial(forward_kernel, nb, nz),
        out_shape=out_shape,
        in_specs=[pl.BlockSpec(memory_space=pltpu.SMEM), ANY, ANY, *[WHOLE] * 4, *[ANY] * 4, WHOLE, ANY, WHOLE],
        out_specs=[ANY] * len(out_shape),
        scratch_shapes=scratch,
        compiler_params=pltpu.CompilerParams(
            collective_id=0, has_side_effects=True, vmem_limit_bytes=VMEM_LIMIT
        ),
    )(lengths, x, skip_x, *norms, skip_w, *qkv_w, out_w, up_w, down_w)


def ffn_kernel(
    nb, nz, mixed_in, attended_in, out_in, norms, cot_in, ff0, ff1, ff2, ff_w,
    output_out, middle_out, att_out, out_grad_out, part0, grad1, grad2, grad3, sums, ff3,
    middle, attended, out_t, cot, weights, grads, ffn_in, ffn_in_t, cot_t, acc, gacc, low, out_grad,
    load, wload, flush, *rest,
):
    place = Place(nb, nz)
    rows, d = mixed_in.shape
    r = grads.shape[2]
    cw = ff_w.shape[1] // 2
    subs = nz // 2
    total = 4 * subs
    place.greet()
    gather = Gather(place, ff_w, ff3, rest[:3])
    job = Scatter(place, grads.at[0], None, rest[3:], sums=False, line=False)
    go = lambda job, *stages: [job.stage(t) for t in stages if t < job.stages]
    last = nz - 1
    go(gather, 0)
    loads = [
        pltpu.make_async_copy(src, dst, load.at[i])
        for i, (src, dst) in enumerate(
            ((attended_in, attended), (out_in, out_t), (mixed_in, middle), (cot_in, cot))
        )
    ]
    weight_load = lambda i: pltpu.make_async_copy((ff0, ff1, ff2, ff3)[i], weights.at[i % 2], wload.at[i % 2])
    for one in loads:
        one.start()
    weight_load(0).start()
    weight_load(1).start()
    gain, shift = norms[2:3, :], norms[3:4, :]
    for one in loads[:3]:
        one.wait()
    acc[...] = nt(attended[...], out_t[...])
    go(gather, 1)

    def enter(at):
        v = middle[at, :] + acc[at, :]
        middle[at, :] = v
        n, _ = normalise(v)
        ffn_in[at, :] = (n * gain + shift).astype(BF16)
        acc[at, :] = v
        gacc[at, :] = jnp.zeros_like(v)

    rowwise(rows, 32, enter)
    ffn_in_t[...] = ffn_in[...].T
    loads[3].wait()
    cot_t[...] = cot[...].T
    go(gather, *range(2, last))
    weight_load(0).wait()

    hooks = {}

    def hook(it, *steps):
        hooks.setdefault(min(it, total - 1), []).extend(steps)

    rest_of = lambda job, t: [(job, s) for s in range(t, job.stages)]
    hook(total // 8, (gather, last))
    hook(total * 2 // 8, lambda: weight_load(1).wait(), lambda: weight_load(2).start(), (job, 0))
    hook(total * 3 // 8, (gather, last + 1))
    hook(total * 4 // 8, lambda: weight_load(2).wait(), lambda: flush_copy(3).start(), (job, 1))
    hook(
        total * 6 // 8,
        (gather, last + 2),
        *rest_of(gather, last + 3),
        lambda: weight_load(3).start(),
        lambda: flush_copy(0).start(),
        lambda: weight_load(3).wait(),
    )
    hook(total * 7 // 8, (job, 2))

    def flush_copy(i):
        pairs = (
            (grads.at[2], grad2), (grads.at[3], grad3), (grads.at[0, 0], part0), (grads.at[1], grad1),
            (low, output_out), (gacc, middle_out), (attended, att_out), (out_grad, out_grad_out),
        )
        return pltpu.make_async_copy(*pairs[i], flush.at[i])

    def body(it, carry):
        for when, steps in hooks.items():
            pl.when(it == when)(lambda steps=steps: perform(steps))
        chunk, sub = lax.div(it, subs), lax.rem(it, subs)
        slot = lax.rem(chunk, 2)
        first = [(2 * sub + i) * 2 for i in (0, 1)]
        up = jnp.concatenate([weights[slot, :, part(f, cw)] for f in first], 1)
        dn = jnp.concatenate([weights[slot, :, part(f + 1, cw)] for f in first], 1)
        hidden = nn(ffn_in[...], up)
        active_grad = nn(cot[...], dn)
        cdf = 0.5 * (1.0 + lax.erf(hidden * 0.7071067811865476))
        active = (hidden * cdf).astype(BF16)
        density = jnp.exp2(hidden * hidden * (-0.5 * LOG2E)) * 0.3989422804014327
        hidden_grad = (active_grad * (cdf + hidden * density)).astype(BF16)
        acc[...] += nt(active, dn)
        gacc[...] += nt(hidden_grad, up)
        up_grad = nn(ffn_in_t[...], hidden_grad).astype(BF16)
        dn_grad = nn(cot_t[...], active).astype(BF16)
        for j in range(nb):
            m = flip(place.b, j)
            block = slice(j * r, (j + 1) * r)
            for i in (0, 1):
                cols = slice(i * cw, (i + 1) * cw)
                grads[chunk, m, :, part(first[i], cw)] = up_grad[block, cols]
                grads[chunk, m, :, part(first[i] + 1, cw)] = dn_grad[block, cols]
        return carry

    lax.fori_loop(0, total, body, 0)
    flush_copy(1).start()
    sums[...] = jnp.zeros_like(sums)

    def leave(at):
        low[at, :] = acc[at, :].astype(BF16)
        back = norm_back(gacc[at, :], middle[at, :], gain, sums.at[0], sums.at[1])
        grad = cot[at, :].astype(F32) + back
        gacc[at, :] = grad
        ffn_in[at, :] = grad.astype(BF16)

    rowwise(rows, 32, leave)
    flush_copy(4).start()
    flush_copy(5).start()
    grad_t = ffn_in[...].T
    for j in range(nb):
        out_grad[flip(place.b, j)] = nn(grad_t[j * r : (j + 1) * r, :], attended[...]).astype(BF16)
    flush_copy(7).start()
    attended[...] = nn(ffn_in[...], out_t[...]).astype(BF16)
    flush_copy(6).start()
    go(job, *range(3, job.stages))
    flush_copy(2).start()
    for i in range(8):
        flush_copy(i).wait()
    place.drain()


def ffn(nb, nz, mixed, attended, out_t, norms, cot, ff0, ff1, ff2, ff_w):
    rows, d = mixed.shape
    r, width = ff_w.shape
    wide = nz * width
    V, S, D = pltpu.VMEM, jax.ShapeDtypeStruct, pltpu.SemaphoreType.DMA
    scratch = [
        V((rows, d), F32),
        V((rows, d), BF16),
        V((d, d), BF16),
        V((rows, d), BF16),
        V((2, d, wide), BF16),
        V((4, nb, r, wide), BF16),
        V((rows, d), BF16),
        V((d, rows), BF16),
        V((d, rows), BF16),
        V((rows, d), F32),
        V((rows, d), F32),
        V((rows, d), BF16),
        V((nb, r, d), BF16),
        D((4,)), D((2,)), D((8,)),
    ]
    scratch += Gather.scratch(nb, nz)
    scratch += Scatter.scratch(nb, nz, r, wide, sums=False, line=False)
    return pl.pallas_call(
        functools.partial(ffn_kernel, nb, nz),
        out_shape=[
            S((rows, d), BF16),
            S((rows, d), F32),
            S((rows, d), BF16),
            S((nb, r, d), BF16),
            S((r, wide), BF16),
            *[S((nb, r, wide), BF16)] * 3,
            S((2, 8, d), F32),
            S((d, wide), BF16),
        ],
        in_specs=[ANY] * 3 + [WHOLE] + [ANY] * 5,
        out_specs=[ANY] * 8 + [WHOLE, ANY],
        scratch_shapes=scratch,
        compiler_params=pltpu.CompilerParams(
            collective_id=3, has_side_effects=True, vmem_limit_bytes=VMEM_LIMIT
        ),
    )(mixed, attended, out_t, norms, cot, ff0, ff1, ff2, ff_w)


def attention_kernel(
    nb, nz, att_grad, qkv_in, probs, part0, grad1, grad2,
    dqkv_out, ff_share, part2,
    dqkv, qkv, dout, pbuf, dk, dv, q_t, do_t, load, psem, att_send, att_recv, *rest,
):
    place = Place(nb, nz)
    z, group, k = place.z, place.group, place.k
    pairs, keys = qkv.shape[1], qkv.shape[2]
    frames = keys // nz
    wide = pairs * 128
    pz = pairs // 2
    place.greet()

    def att_copy(r, pair):
        owner = lax.rem(z + r, nz)
        item, member = lax.div(owner, place.half), lax.rem(owner, place.half)
        slot = pair * (nz - 1) + r - 1
        return remote(
            att_grad.at[part(item, frames), part(member * pairs + pair, 128)],
            dout.at[part(z, frames), part(pair, 128)],
            att_send.at[slot], att_recv.at[slot], (place.b, owner),
        )

    def att_start(pair):
        for r in range(1, nz):
            att_copy(r, pair).start()

    for pair in range(min(2, pairs)):
        att_start(pair)
    own = pltpu.make_async_copy(att_grad.at[part(group, frames), part(k, wide)], dout.at[part(z, frames)], load.at[0])
    own.start()
    qkv_load = pltpu.make_async_copy(qkv_in, qkv, load.at[1])
    qkv_load.start()
    rest = list(rest)

    def job(full, share, **kind):
        count = 3 + sum(kind.get(key, True) and size for key, size in (("sums", 1), ("plane", 2), ("line", 1)))
        mine = [rest.pop(0) for _ in range(count)]
        return Scatter(place, full, share, mine, **kind)

    early = [job(None, ff_share.at[0], plane=False)]
    late = [job(grad1, ff_share.at[1]), job(grad2, None, line=False)]
    go = lambda job, *stages: [job.stage(t) for t in stages if t < job.stages]
    early_loads = [
        pltpu.make_async_copy(p, e.sums.at[0], load.at[2 + i]) for i, (p, e) in enumerate(zip((part0,), early))
    ]
    for one in early_loads:
        one.start()
    go(late[0], 0)
    go(late[1], 0)
    go(late[0], 1)
    own.wait()
    qkv_load.wait()

    blocks = keys // QUERIES
    total = pairs * blocks

    def probs_copy(it):
        slot = lax.rem(it, 2)
        pair, q = lax.div(it, blocks), lax.rem(it, blocks)
        return pltpu.make_async_copy(probs.at[pair, :, part(q, QUERIES)], pbuf.at[slot], psem.at[slot])

    probs_copy(0).start()
    hooks = {}

    def hook(it, *steps):
        hooks.setdefault(min(it, total - 1), []).extend(steps)

    zs = place.nz - 1
    rest_of = lambda job, t: [(job, s) for s in range(t, job.stages)]
    hook(0, *[lambda one=one: one.wait() for one in early_loads], (early[0], 0))
    hook(total * 2 // 16, (early[0], 1))
    hook(total * 4 // 16, (late[0], 2), *[(early[0], t) for t in range(2, zs)])
    hook(total * 5 // 16, (late[1], 1))
    hook(total * 6 // 16, (early[0], zs))
    hook(total * 8 // 16, (late[0], 3))
    hook(total * 10 // 16, (late[0], 4))
    hook(total * 11 // 16, (late[1], 2))
    hook(total * 12 // 16, (late[0], 5))

    def body(it, carry):
        pair, q = lax.div(it, blocks), lax.rem(it, blocks)
        at, slot = part(q, QUERIES), lax.rem(it, 2)
        for when, steps in hooks.items():
            pl.when(it == when)(lambda steps=steps: perform(steps))

        @pl.when(it + 1 < total)
        def _():
            probs_copy(it + 1).start()

        probs_copy(it).wait()

        @pl.when(q == 0)
        def _():
            for r in range(1, nz):
                att_copy(r, pair).wait_recv()
            pl.when(pair + 2 < pairs)(lambda: att_start(pair + 2))
            dk[...] = jnp.zeros_like(dk)
            dv[...] = jnp.zeros_like(dv)

        do = dout[at, part(pair, 128)]
        q_t[...] = qkv[0, pair, at, :].T
        do_t[...] = do.T
        block = lax.div(pair, pz)
        column = lambda t: part((block * 3 + t) * pz + lax.rem(pair, pz), 128)
        dqkv[at, column(0)] = backward_tile(qkv, do, do_t, q_t, pair, lambda i: pbuf[slot, i], dk, dv)

        @pl.when(q == blocks - 1)
        def _():
            dqkv[:, column(1)] = dk[...].T.astype(BF16)
            dqkv[:, column(2)] = dv[...].T.astype(BF16)

        return carry

    lax.fori_loop(0, total, body, 0)
    dqkv_copy = pltpu.make_async_copy(dqkv, dqkv_out, load.at[1])
    dqkv_copy.start()
    go(late[0], *range(6, late[0].stages))
    go(late[1], *range(3, late[1].stages))
    part_copy = pltpu.make_async_copy(late[1].sums.at[0], part2, load.at[0])
    part_copy.start()
    for pair in range(pairs):
        for r in range(1, nz):
            att_copy(r, pair).wait_send()
    part_copy.wait()
    dqkv_copy.wait()
    place.drain()


def attention_back(nb, nz, att_grad, qkv, probs, part0, grad1, grad2):
    _, pairs, keys, _ = qkv.shape
    S, V, D = jax.ShapeDtypeStruct, pltpu.VMEM, pltpu.SemaphoreType.DMA
    _, r, wide = grad2.shape
    scratch = [
        V((keys, 3 * pairs * 128), BF16),
        V((3, pairs, keys, 128), BF16),
        V((keys, pairs * 128), BF16),
        V((2, 2, QUERIES, keys), BF16),
        V((128, keys), F32),
        V((128, keys), F32),
        V((128, QUERIES), BF16),
        V((128, QUERIES), BF16),
        D((4,)), D((2,)), D((pairs * (nz - 1),)), D((pairs * (nz - 1),)),
    ]
    scratch += Scatter.scratch(nb, nz, r, wide, plane=False)
    scratch += Scatter.scratch(nb, nz, r, wide)
    scratch += Scatter.scratch(nb, nz, r, wide, line=False)
    return pl.pallas_call(
        functools.partial(attention_kernel, nb, nz),
        out_shape=[
            S((keys, 3 * pairs * 128), BF16),
            S((2, r, wide // nz), F32),
            S((r, wide), BF16),
        ],
        in_specs=[ANY] * 6,
        out_specs=[ANY, WHOLE, ANY],
        scratch_shapes=scratch,
        compiler_params=pltpu.CompilerParams(
            collective_id=1, has_side_effects=True, vmem_limit_bytes=VMEM_LIMIT
        ),
    )(att_grad, qkv, probs, part0, grad1, grad2)


def first_kernel(
    nb, nz, dqkv_in, everything_in, qkvw_in, x, skip_x, skip_w, mixed_in, middle_in, norms, second_sums, ff_early, part2, grad3, out_grad,
    input_out, skip_out, query_out, key_out, value_out, skip_share, norm_share, up_out, down_out, out_out,
    input_grad, skip_grad, qkv_share, ff_share, out_share,
    dqkv, everything, qkvw, mixed, middle_grad,
    qkv_grad, skip_w_grad, spare, joined, joined_t, mixed_low, ahead, mine, from_mate, to_partner, from_partner,
    sums, packed, norm_in, norm_line, load, swap_send, swap_recv, norm_send, norm_recv, flush, *rest,
):
    place = Place(nb, nz)
    z, group, k, half = place.z, place.group, place.k, place.half
    frames = x.shape[0] // 2
    width = x.shape[1]
    loads = [
        pltpu.make_async_copy(src, dst, load.at[i])
        for i, (src, dst) in enumerate(
            (
                (dqkv_in, dqkv),
                (qkvw_in, qkvw),
                (everything_in, everything),
                (mixed_in, mixed),
                (middle_in, middle_grad),
                (x, joined.at[:, pl.ds(0, width)]),
                (skip_x, joined.at[:, pl.ds(width, width)]),
            )
        )
    ]
    rest = list(rest)

    def job(full, share, paired=False, **kind):
        count = 3 + sum(kind.get(key, True) and size for key, size in (("sums", 1), ("plane", 2), ("line", 1)))
        mine = [rest.pop(0) for _ in range(count)]
        return Scatter(place, full, share, mine, paired, **kind)

    for one in loads:
        one.start()
    place.greet()
    line_job = job(None, ff_share.at[0], plane=False)
    ff_job = job(grad3, ff_share.at[1])
    out_job = job(out_grad, out_share)
    qkv_job = job(qkv_grad, qkv_share, True, sums=False)
    rs = skip_w_grad.shape[2]
    skips = [job(skip_w_grad.at[h], skip_share.at[pl.ds(h * rs, rs)], sums=False) for h in (0, 1)]
    loads.append(pltpu.make_async_copy(part2, line_job.sums.at[0], load.at[7]))
    loads[7].start()

    def go(job, *stages):
        for t in stages:
            if t < job.stages:
                job.stage(t)

    go(ff_job, 0)
    go(out_job, 0)
    for one in loads[:2]:
        one.wait()

    def mate_copy(r, t):
        slot = (r - 1) * 2 + t
        return remote(
            ahead.at[slot], from_mate.at[slot], swap_send.at[slot], swap_recv.at[slot], (place.b, place.mate(r))
        )

    for r in range(1, half):
        for s in (0, 1):
            block = lax.rem(k + r, half) + (1 - group if s == 0 else group) * half
            ahead[(r - 1) * 2 + s] = nt(dqkv[part(block, frames), :], qkvw[...]).astype(BF16)
        place.start(mate_copy, r, 0)
    for s in (0, 1):
        block = k + (1 - group if s == 0 else group) * half
        mine[s] = nt(dqkv[part(block, frames), :], qkvw[...])
    loads[2].wait()
    turned = everything[...].T
    rq = qkv_grad.shape[1]
    for j in range(nb):
        qkv_grad[flip(place.b, j)] = nn(turned[j * rq : (j + 1) * rq, :], dqkv[...]).astype(BF16)
    weights = [everything.at[pl.ds(0, width)], qkvw.at[:, pl.ds(0, width)] if qkvw.shape[1] >= width else spare]
    for i, ref in enumerate(weights):
        loads.append(pltpu.make_async_copy(skip_w.at[pl.ds(i * width, width)], ref, load.at[8 + i]))
        loads[-1].start()
    go(ff_job, 1)
    go(qkv_job, 0)
    go(out_job, 1)

    def add_mates(s):
        for r in range(1, half):
            mate_copy(r, s).wait_recv()
            slot = (r - 1) * 2 + s

            def body(at):
                mine[s, at] = mine[s, at] + from_mate[slot, at].astype(F32)

            rowwise(frames, 16, body)

    add_mates(0)
    sem = 2 * (half - 1)
    across = lambda: remote(to_partner, from_partner, swap_send.at[sem], swap_recv.at[sem], (place.b, place.partner))

    def narrow(at):
        to_partner[at] = mine[0, at].astype(BF16)

    rowwise(frames, 16, narrow)
    place.start(across)
    for r in range(1, half):
        place.start(mate_copy, r, 1)
    for one in loads[3:8]:
        one.wait()
    joined_t[...] = joined[...].T
    go(qkv_job, 1)
    go(ff_job, 2)
    go(out_job, 2)

    sums[...] = jnp.zeros_like(sums)
    gain = norms[0:1, :]

    def back(item, grad):
        def body(i, carry):
            at = part(i, 32)
            to = pl.ds(pl.multiple_of(item * frames + i * 32, 32), 32)
            part_grad = norm_back(grad(at), mixed[to, :], gain, sums.at[0], sums.at[1])
            mixed_low[to, :] = (middle_grad[to, :] + part_grad).astype(BF16)
            return carry

        lax.fori_loop(0, frames // 32, body, 0)

    add_mates(1)
    back(group, lambda at: mine[1, at])
    go(qkv_job, 2)
    go(ff_job, 3)
    across().wait_recv()
    back(1 - group, lambda at: from_partner[at].astype(F32))
    for h in (0, 1):
        for j in range(nb):
            block = slice((2 * j + h) * rs, (2 * j + h + 1) * rs)
            skip_w_grad[h, flip(place.b, j)] = nn(joined_t[block, :], mixed_low[...]).astype(BF16)
        go(skips[h], 0)

    total = lambda a: jnp.sum(a, 0, keepdims=True)
    for i, v in enumerate((sums[0], sums[1], second_sums[0], second_sums[1])):
        packed[i : i + 1, :] = total(v)
    packed[4:8, :] = jnp.zeros_like(packed[4:8, :])
    bits = [0] + place.rest
    norm_copy = lambda i: remote(
        packed, norm_in.at[i], norm_send.at[i], norm_recv.at[i], place.at(1 << bits[i])
    )
    c = norm_share.shape[1]
    line_copy = lambda r: remote(
        packed.at[:, part(lax.rem(z + r, nz), c)], norm_line.at[r - 1],
        norm_send.at[len(bits) + r - 1], norm_recv.at[len(bits) + r - 1], (place.b, lax.rem(z + r, nz)),
    )

    def norm_step(i):
        if i > 0:
            norm_copy(i - 1).wait()
            packed[...] = packed[...] + norm_in[i - 1]
        if i < len(bits):
            norm_copy(i).start()
        else:
            for r in range(1, nz):
                line_copy(r).start()

    norm_step(0)
    go(out_job, 3)
    go(qkv_job, 3)
    go(line_job, 0)
    go(skips[0], 1)
    go(skips[1], 1)
    norm_step(1)
    go(ff_job, 4)
    go(out_job, 4)
    go(line_job, 1)
    for one in loads[8:]:
        one.wait()
    input_grad[...] = nt(mixed_low[...], weights[0][...])
    flushes = [pltpu.make_async_copy(input_grad, input_out, flush.at[0])]
    flushes[0].start()
    go(skips[0], 2)
    norm_step(2)
    go(ff_job, 5)
    go(out_job, 5)
    go(line_job, 2)
    go(qkv_job, *range(4, qkv_job.stages))
    skip_grad[...] = nt(mixed_low[...], weights[1][...])
    flushes.append(pltpu.make_async_copy(skip_grad, skip_out, flush.at[1]))
    flushes[1].start()
    go(skips[1], 2)
    go(skips[0], 3)
    norm_step(3)
    go(ff_job, *range(6, ff_job.stages))
    go(out_job, *range(6, out_job.stages))
    go(skips[1], 3)
    go(line_job, *range(3, line_job.stages))
    for i in range(4, len(bits) + 1):
        norm_step(i)
    go(skips[0], 4)
    go(skips[1], 4)
    for i, ref in enumerate((query_out, key_out, value_out)):
        ref[...] = qkv_share[:, i * c : (i + 1) * c]
    out_out[...] = out_share[...].T
    cw = ff_share.shape[2] // 2
    for i in range(4):
        source = ff_early.at[i] if i < 2 else ff_share.at[i - 2]
        up_out[:, i * cw : (i + 1) * cw] = source[:, :cw]
        down_out[i * cw : (i + 1) * cw, :] = source[:, cw:].T
    for t in range(5, skips[0].stages):
        go(skips[0], t)
        go(skips[1], t)
    for one in flushes:
        one.wait()
    value = packed[:, part(z, c)]
    for r in range(1, nz):
        line_copy(r).wait()
        value = value + norm_line[r - 1]
    norm_share[...] = value
    place.drain()


def first_back(nb, nz, dqkv, everything, qkvw, x, skip_x, skip_w, mixed, middle_grad, norms, second_sums, ff_early, part2, grad3, out_grad):
    rows, width = x.shape
    frames = rows // 2
    half = nz // 2
    c = width // nz
    S, V, D = jax.ShapeDtypeStruct, pltpu.VMEM, pltpu.SemaphoreType.DMA
    qkv_wide = qkvw.shape[1]
    bits = nb.bit_length() - 1
    swaps = 2 * (half - 1)
    r, wide = ff_early.shape[1:]
    scratch = [
        V((rows, width), F32),
        V((rows, width), F32),
        V((r, 3 * c), F32),
        V((2, r, wide), F32),
        V((r, c), F32),
        V(dqkv.shape, BF16),
        V(everything.shape, BF16),
        V(qkvw.shape, BF16),
        V((rows, width), F32),
        V((rows, width), F32),
        V((nb, qkvw.shape[0] // nb, qkv_wide), BF16),
        V((2, nb, skip_w.shape[0] // nb // 2, width), BF16),
        V((width, width) if qkv_wide < width else (16, 128), BF16),
        V((rows, 2 * width), BF16),
        V((2 * width, rows), BF16),
        V((rows, width), BF16),
        V((max(swaps, 1), frames, width), BF16),
        V((2, frames, width), F32),
        V((max(swaps, 1), frames, width), BF16),
        V((frames, width), BF16),
        V((frames, width), BF16),
        V((2, 8, width), F32),
        V((8, width), F32),
        V((bits, 8, width), F32),
        V((nz - 1, 8, c), F32),
        D((10,)), D((swaps + 1,)), D((swaps + 1,)), D((bits + nz - 1,)), D((bits + nz - 1,)), D((2,)),
    ]
    scratch += Scatter.scratch(nb, nz, grad3.shape[1], grad3.shape[2], plane=False)
    scratch += Scatter.scratch(nb, nz, grad3.shape[1], grad3.shape[2])
    scratch += Scatter.scratch(nb, nz, out_grad.shape[1], out_grad.shape[2])
    scratch += Scatter.scratch(nb, nz, qkvw.shape[0] // nb, qkv_wide, True, sums=False)
    for _ in (0, 1):
        scratch += Scatter.scratch(nb, nz, skip_w.shape[0] // nb // 2, width, sums=False)
    return pl.pallas_call(
        functools.partial(first_kernel, nb, nz),
        out_shape=[
            S((rows, width), F32),
            S((rows, width), F32),
            *[S((r, c), F32)] * 3,
            S((skip_w.shape[0] // nb, c), F32),
            S((8, c), F32),
            S((r, 2 * wide), F32),
            S((2 * wide, r), F32),
            S((c, r), F32),
        ],
        in_specs=[ANY] * 8 + [WHOLE] * 3 + [ANY] * 3,
        out_specs=[ANY] * 2 + [WHOLE] * 8,
        scratch_shapes=scratch,
        compiler_params=pltpu.CompilerParams(
            collective_id=2, has_side_effects=True, vmem_limit_bytes=VMEM_LIMIT
        ),
    )(dqkv, everything, qkvw, x, skip_x, skip_w, mixed, middle_grad, norms, second_sums, ff_early, part2, grad3, out_grad)


def shards(
    inputs,
    skip_input,
    lengths,
    skip_weight,
    query_weight,
    key_weight,
    value_weight,
    out_weight,
    up_weight,
    down_weight,
    first_gain,
    first_shift,
    second_gain,
    second_shift,
    cotangent,
):
    nb, nz = lax.axis_size("batch"), lax.axis_size("seq")
    shape = inputs.shape
    flat = lambda a: a.reshape(shape[0] * shape[1], shape[2])
    x, skip_x, cot = flat(inputs), flat(skip_input), flat(cotangent)
    norms = (first_gain, first_shift, second_gain, second_shift)
    qkv_w = (query_weight, key_weight, value_weight)
    (mixed, everything, gains, skip_w, qkvw, out_t, ff0, ff1, ff2, ff3_w, qkv, probs, attended) = forward(
        nb, nz, lengths, x, skip_x, norms, skip_weight, qkv_w, out_weight, up_weight, down_weight
    )
    output, middle_grad, att_grad, out_grad, part0, grad1, grad2, grad3, second_sums, _ = ffn(
        nb, nz, mixed, attended, out_t, gains, cot, ff0, ff1, ff2, ff3_w
    )
    dqkv, ff_early, part2 = attention_back(nb, nz, att_grad, qkv, probs, part0, grad1, grad2)
    input_grad, skip_grad, query_share, key_share, value_share, skip_share, norm_share, up_share, down_share, out_share = (
        first_back(
            nb, nz, dqkv, everything, qkvw, x, skip_x, skip_w, mixed, middle_grad, gains, second_sums, ff_early, part2,
            grad3, out_grad,
        )
    )
    return (
        output.reshape(shape),
        input_grad.reshape(shape),
        skip_grad.reshape(shape),
        skip_share,
        query_share,
        key_share,
        value_share,
        out_share,
        up_share,
        down_share,
        norm_share[0],
        norm_share[1],
        norm_share[2],
        norm_share[3],
    )


def solution(mesh):
    rows = P("batch", "seq", None)
    weight, turned, norm = P("batch", "seq"), P("seq", "batch"), P("seq")
    return jax.shard_map(
        shards,
        mesh=mesh,
        in_specs=(rows, rows, P("batch"), *[weight] * 4, turned, weight, turned, *[norm] * 4, rows),
        out_specs=(rows, rows, rows, *[weight] * 4, turned, weight, turned, *[norm] * 4),
        check_vma=False,
    )
```

```python
import functools

import jax
import jax.numpy as jnp
from jax import lax
from jax.experimental import pallas as pl
from jax.experimental.pallas import tpu as pltpu
from jax.sharding import PartitionSpec as P

HEADS = 16
HEAD_DIM = 64
EPSILON = 1e-05
LOG2E = 1.4426950408889634
QUERIES = 512
F32 = jnp.float32
BF16 = jnp.bfloat16
MESH = pl.DeviceIdType.MESH
VMEM_LIMIT = 60 * 2**20
ANY = pl.BlockSpec(memory_space=pl.ANY)
WHOLE = pl.BlockSpec(memory_space=pltpu.VMEM)


def nt(a, b):
    return lax.dot_general(a, b, (((1,), (1,)), ((), ())), preferred_element_type=F32)


def nn(a, b):
    return jnp.dot(a, b, preferred_element_type=F32)


def part(index, size):
    if isinstance(index, int):
        return pl.ds(index * size, size)
    return pl.ds(pl.multiple_of(index * size, size), size)


def rowwise(rows, step, body):
    def run(i, carry):
        body(part(i, step))
        return carry

    lax.fori_loop(0, rows // step, run, 0)


def flip(index, mask):
    result = index
    bit = 0
    while mask >> bit:
        if (mask >> bit) & 1:
            on = lax.rem(lax.div(index, 1 << bit), 2)
            result = result + (1 << bit) * (1 - 2 * on)
        bit += 1
    return result


def span(bits):
    masks = [0]
    for bit in bits:
        masks = masks + [m | (1 << bit) for m in masks]
    return masks


class Place:
    def __init__(self, nb, nz):
        self.nb, self.nz = nb, nz
        self.b = lax.axis_index("batch")
        self.z = lax.axis_index("seq")
        self.half = nz // 2
        self.group = lax.div(self.z, self.half)
        self.k = lax.rem(self.z, self.half)
        self.partner = lax.rem(self.z + self.half, nz)
        self.rest = list(range(1, nb.bit_length() - 1))
        self.orders = (self.rest, self.rest[::-1])
        self.pending = []

    def at(self, mask):
        return (flip(self.b, mask), self.z)

    def mate(self, r):
        return self.group * self.half + lax.rem(self.k + r, self.half)

    def greet(self):
        barrier = pltpu.get_barrier_semaphore()
        targets = [self.at(1 << k) for k in [0] + self.rest]
        targets += [(self.b, lax.rem(self.z + r, self.nz)) for r in range(1, self.nz)]
        for t in targets:
            pl.semaphore_signal(barrier, inc=1, device_id=t, device_id_type=MESH)
        pl.semaphore_wait(barrier, len(targets))

    def start(self, make, *args):
        copy, ok = self.unpack(make(*args))
        if ok is None:
            copy.start()
        else:
            pl.when(ok)(lambda: copy.start())
        self.pending.append((make, args))

    def drain(self):
        for make, args in self.pending:
            copy, ok = self.unpack(make(*args))
            if ok is None:
                copy.wait_send()
            else:
                pl.when(ok)(lambda copy=copy: copy.wait_send())
        self.pending = []

    @staticmethod
    def unpack(made):
        return made if isinstance(made, tuple) else (made, None)


def remote(src, dst, send, recv, device):
    return pltpu.make_async_remote_copy(
        src_ref=src, dst_ref=dst, send_sem=send, recv_sem=recv, device_id=device, device_id_type=MESH
    )


class Gather:
    @staticmethod
    def sems(nb, nz):
        return max(2 * (nz - 1), 6) + 2 * (nb // 2 - 1) + nb

    @staticmethod
    def scratch(nb, nz):
        count = Gather.sems(nb, nz)
        return [pltpu.SemaphoreType.DMA((3,))] + [pltpu.SemaphoreType.DMA((count,))] * 2

    def __init__(self, place, shard, full, scratch, paired=False, h=0, of=1):
        self.p, self.full, self.paired, self.h, self.of = place, full, paired, h, of
        self.shards = shard if paired else [shard]
        self.shard = self.shards[0]
        self.local, self.send, self.recv = scratch
        self.r, self.c = self.shard.shape
        nb, nz = place.nb, place.nz
        self.xy0 = max(2 * (nz - 1), 6)
        self.core0 = self.xy0 + 2 * (nb // 2 - 1)
        self.zsteps = 1 if paired else nz - 1
        self.stages = self.zsteps + len(place.rest) + 2

    def column(self, index):
        return self.full.at[part(self.p.b * self.of + self.h, self.r), part(index, self.c)]

    def line(self, way, step):
        p, n = self.p, self.p.nz
        sem = (0 if way > 0 else n - 1) + step - 1
        sent, got = p.z - way * (step - 1), p.z - way * step
        inside = lambda v: (v >= 0) & (v < n)
        clip = lambda v: jnp.clip(v, 0, n - 1)
        to = (p.b, clip(p.z + way))
        block = self.column(clip(sent))
        out = lambda: remote(self.shard if step == 1 else block, block, self.send.at[sem], self.recv.at[sem], to)
        land = self.column(clip(got))
        into = lambda: remote(land, land, self.send.at[sem], self.recv.at[sem], to)
        return out, into, inside(sent) & inside(p.z + way), inside(got)

    def zstart(self, step):
        p = self.p
        if self.paired:
            for t in (0, 1):
                for i in range(len(self.shards)):
                    p.start(self.paircopy, t, i)
            return
        for way in (1, -1):
            p.start(self.lineout, way, step)

    def lineout(self, way, step):
        out, _, can_send, _ = self.line(way, step)
        return out(), can_send

    def paircopy(self, t, i):
        p, count = self.p, len(self.shards)
        target = lax.div(p.z, 2) + t * p.half
        slot = lax.rem(p.z, 2) * count + i
        copy = remote(
            self.shards[i], self.column(slot), self.send.at[t * count + i], self.recv.at[slot], (p.b, target)
        )
        return copy, target != p.z

    def zwait(self, step):
        p = self.p
        if self.paired:
            for s in (0, 1):

                @pl.when(2 * p.k + s != p.z)
                def _(s=s):
                    for i in range(len(self.shards)):
                        slot = s * len(self.shards) + i
                        land = self.column(slot)
                        remote(land, land, self.send.at[slot], self.recv.at[slot], (p.b, p.partner)).wait_recv()

            return
        for way in (1, -1):
            _, into, _, can_get = self.line(way, step)
            pl.when(can_get)(lambda into=into: into().wait_recv())

    def owncopy(self, act):
        p, count = self.p, len(self.shards)
        place = lax.rem(p.z, 2) if self.paired else p.z
        copies = lambda: [
            pltpu.make_async_copy(shard, self.column(place * count + i), self.local.at[i])
            for i, shard in enumerate(self.shards)
        ]
        if self.paired:
            pl.when((2 * p.k == p.z) | (2 * p.k + 1 == p.z))(lambda: [act(copy) for copy in copies()][:0] or None)
        else:
            act(copies()[0])

    def rows(self, mask, half):
        h = self.r // 2
        return self.full.at[part((flip(self.p.b, mask) * self.of + self.h) * 2 + half, h)]

    def hop(self, sem, mask, half, bit, incoming):
        block = self.rows(mask | bit if incoming else mask, half)
        return remote(block, block, self.send.at[sem], self.recv.at[sem], self.p.at(bit))

    def plane(self, j):
        made = []
        for half in (0, 1):
            order = self.p.orders[half]
            for i, m in enumerate(span(order[:j])):
                sem = self.xy0 + half * (self.p.nb // 2 - 1) + (1 << j) - 1 + i
                made.append((half, m, 1 << order[j], sem))
        return made

    def coresem(self, mask, half):
        return self.core0 + (mask >> 1) * 2 + half

    def corestart(self, mask, half):
        self.p.start(self.hop, self.coresem(mask, half), mask, half, 1, False)

    def stage(self, t):
        p = self.p
        nx = len(p.rest)
        if t == 0:
            self.owncopy(lambda copy: copy.start())
            self.zstart(1)
        if 1 <= t <= self.zsteps:
            self.zwait(t)
            if t < self.zsteps:
                self.zstart(t + 1)
            else:
                self.owncopy(lambda copy: copy.wait())
        j = t - self.zsteps
        if 1 <= j <= nx:
            for half, m, bit, sem in self.plane(j - 1):
                self.hop(sem, m, half, bit, True).wait_recv()
        if 0 <= j < nx:
            for half, m, bit, sem in self.plane(j):
                p.start(self.hop, sem, m, half, bit, False)
        if j == 0:
            for half in (0, 1):
                self.corestart(0, half)
        if 1 <= j <= nx:
            for half, m, bit, _ in self.plane(j - 1):
                self.corestart(m | bit, half)
        if j == nx + 1:
            for m in span(p.rest):
                for half in (0, 1):
                    self.hop(self.coresem(m, half), m, half, 1, True).wait_recv()


class Scatter:
    @staticmethod
    def scratch(nb, nz, r, wide, paired=False, sums=True, plane=True, line=True):
        c = wide // (2 if paired else nz)
        lines = 2 if paired else 2 * (nz - 1)
        count = nb // 2 + 2 * (nb // 2 - 1) + lines
        made = [pltpu.VMEM((nb // 2 if plane else 1, r, wide), BF16)] if sums else []
        if plane:
            made += [
                pltpu.VMEM((nb // 2, r, wide), BF16),
                pltpu.VMEM((2 * (nb // 2 - 1), r // 2, wide), BF16),
            ]
        if line:
            made += [pltpu.VMEM((lines, r, c), BF16)]
        return made + [
            pltpu.SemaphoreType.DMA((nb // 2,)),
            pltpu.SemaphoreType.DMA((count,)),
            pltpu.SemaphoreType.DMA((count,)),
        ]

    def __init__(self, place, full, share, scratch, paired=False, sums=True, plane=True, line=True):
        self.p, self.full, self.share, self.paired = place, full, share, paired
        scratch = list(scratch)
        self.sums = scratch.pop(0) if sums else None
        self.core, self.flat = (scratch.pop(0), scratch.pop(0)) if plane else (None, None)
        self.got = scratch.pop(0) if line else None
        self.local, self.send, self.recv = scratch
        self.has_plane, self.has_line = plane, line
        _, self.r, self.wide = (full if plane else self.sums).shape
        self.c = self.wide // (2 if paired else place.nz)
        self.zsteps = 1 if paired else place.nz - 1
        self.nx = len(place.rest)
        self.plane_stages = 2 + self.nx
        self.stages = (self.plane_stages if plane else 1) + (self.zsteps if line else 0)
        self.zsem = place.nb // 2 + 2 * (place.nb // 2 - 1)
        self.masks = sorted(span(place.rest))

    def sum(self, m):
        return self.full.at[m] if self.sums is None else self.sums.at[m >> 1]

    def add(self, target, source):
        def body(at):
            target[at] = target[at] + source[at]

        rowwise(target.shape[0], 16, body)

    def corecopy(self, i, m):
        return remote(self.full.at[m | 1], self.core.at[i], self.send.at[i], self.recv.at[i], self.p.at(1))

    def load(self, i, m):
        return pltpu.make_async_copy(self.full.at[m], self.sum(m), self.local.at[i])

    def rows(self, m, half):
        return self.sum(m).at[part(half, self.r // 2)]

    def plane(self, j):
        p = self.p
        made = []
        for half in (0, 1):
            order = p.orders[half]
            base = half * (p.nb // 2 - 1) + sum(len(span(order[q + 1 :])) for q in range(j))
            for i, m in enumerate(span(order[j + 1 :])):
                made.append((half, m, 1 << order[j], base + i))
        return made

    def planecopy(self, half, m, bit, slot):
        sem = self.p.nb // 2 + slot
        return remote(
            self.rows(m | bit, half), self.flat.at[slot], self.send.at[sem], self.recv.at[sem], self.p.at(bit)
        )

    def column(self, index):
        return self.sum(0).at[:, part(index, self.c)]

    def line(self, way, step):
        p, n = self.p, self.p.nz
        here = p.z if way > 0 else n - 1 - p.z
        goes = n + here - step
        comes = goes - 1
        can_send = (goes > here) & (goes <= n - 1)
        can_get = (comes >= here) & (comes <= n - 1) & (here > 0)
        unfold = lambda d: jnp.clip(d if way > 0 else n - 1 - d, 0, n - 1)
        slot = (0 if way > 0 else n - 1) + step - 1
        copy = remote(
            self.column(unfold(goes)),
            self.got.at[slot],
            self.send.at[self.zsem + slot],
            self.recv.at[self.zsem + slot],
            (p.b, jnp.clip(p.z + way, 0, n - 1)),
        )
        return copy, can_send, can_get, unfold(comes), slot

    def paircopy(self, s):
        p = self.p
        copy = remote(
            self.column(s),
            self.got.at[p.group],
            self.send.at[self.zsem + s],
            self.recv.at[self.zsem + p.group],
            (p.b, 2 * p.k + s),
        )
        return copy, 2 * p.k + s != p.z

    def lineout(self, way, step):
        return self.line(way, step)[:2]

    def zstart(self, step):
        p = self.p
        if self.paired:
            for s in (0, 1):
                p.start(self.paircopy, s)
            return
        for way in (1, -1):
            p.start(self.lineout, way, step)

    def zwait(self, step):
        p = self.p
        if self.paired:
            for t in (0, 1):
                copy = remote(
                    self.column(0),
                    self.got.at[t],
                    self.send.at[self.zsem + t],
                    self.recv.at[self.zsem + t],
                    (p.b, p.partner),
                )
                pl.when(lax.div(p.z, 2) + t * p.half != p.z)(lambda copy=copy: copy.wait_recv())
            return
        for way in (1, -1):
            copy, _, can_get, column, slot = self.line(way, step)

            @pl.when(can_get)
            def _(copy=copy, column=column, slot=slot):
                copy.wait_recv()
                if step < self.zsteps:
                    self.add(self.column(column), self.got.at[slot])

    def stage(self, t):
        p, nx = self.p, self.nx
        s = t - (self.plane_stages - 1 if self.has_plane else 0)
        if self.has_plane:
            if t == 0:
                for i, m in enumerate(self.masks):
                    p.start(self.corecopy, i, m)
                    if self.sums is not None:
                        self.load(i, m).start()
            if t == 1:
                for i, m in enumerate(self.masks):
                    if self.sums is not None:
                        self.load(i, m).wait()
                    self.corecopy(i, m).wait_recv()
                    self.add(self.sum(m), self.core.at[i])
            j = t - 1
            if 1 <= j <= nx:
                for half, m, bit, slot in self.plane(j - 1):
                    self.planecopy(half, m, bit, slot).wait_recv()
                    self.add(self.rows(m, half), self.flat.at[slot])
            if 0 <= j < nx:
                for half, m, bit, slot in self.plane(j):
                    p.start(self.planecopy, half, m, bit, slot)
        if self.has_line:
            if 1 <= s <= self.zsteps:
                self.zwait(s)
            if 0 <= s < self.zsteps:
                self.zstart(s + 1)
            if t == self.stages - 1:
                self.finish()

    def finish(self):
        p = self.p
        if self.paired:
            mine = (2 * p.k == p.z) | (2 * p.k + 1 == p.z)
            own = lax.rem(p.z, 2)
            terms = [(self.got.at[t], lax.div(p.z, 2) + t * p.half != p.z) for t in (0, 1)]
        else:
            mine = None
            own = p.z
            n = p.nz
            terms = [(self.got.at[n - 2], p.z > 0), (self.got.at[2 * n - 3], p.z < n - 1)]
        source = self.column(own)

        def first(at):
            value = source[at].astype(F32)
            self.share[at] = value if mine is None else jnp.where(mine, value, 0.0)

        rowwise(self.r, 16, first)
        for ref, ok in terms:

            @pl.when(ok)
            def _(ref=ref):
                def more(at):
                    self.share[at] = self.share[at] + ref[at].astype(F32)

                rowwise(self.r, 16, more)


def perform(steps):
    for step in steps:
        if callable(step):
            step()
        else:
            step[0].stage(step[1])


def normalise(v):
    centred = v - jnp.mean(v, 1, keepdims=True)
    scale = lax.rsqrt(jnp.mean(centred * centred, 1, keepdims=True) + EPSILON)
    return centred * scale, scale


def norm_back(g, v, gain, gain_sum, shift_sum):
    n, scale = normalise(v)
    fold = lambda a: sum(a[i * 8 : (i + 1) * 8] for i in range(a.shape[0] // 8))
    gain_sum[...] += fold(g * n)
    shift_sum[...] += fold(g)
    gg = g * gain
    return (gg - jnp.mean(gg, 1, keepdims=True) - n * jnp.mean(gg * n, 1, keepdims=True)) * scale


def own_half(value, i):
    lane = lax.broadcasted_iota(jnp.int32, value.shape, 1)
    return jnp.where((lane >= HEAD_DIM) if i else (lane < HEAD_DIM), value, jnp.zeros_like(value))


def merge_halves(a, b):
    lane = lax.broadcasted_iota(jnp.int32, a.shape, 1)
    return jnp.where(lane < HEAD_DIM, a, b)


def project(normed, weight, qkv, pz):
    c = pz * 128
    rows = normed.shape[0]
    for j in (0, 1):
        for t in range(3):
            for i in range(rows // 512):
                at = pl.ds(i * 512, 512)
                y = nn(normed[at, :], weight[:, pl.ds((j * 3 + t) * c, c)])
                if t == 0:
                    y = y.astype(BF16).astype(F32) * HEAD_DIM**-0.5
                for w in range(pz):
                    qkv[t, j * pz + w, at, :] = y[:, w * 128 : (w + 1) * 128].astype(BF16)


def distances(dist, length):
    rows, cols = dist.shape

    def body(i, carry):
        row = lax.broadcasted_iota(jnp.int32, (64, cols), 0) + i * 64
        col = lax.broadcasted_iota(jnp.int32, (64, cols), 1)
        gap = jnp.abs(row - col).astype(F32)
        dist[part(i, 64), :] = jnp.where(col < length, gap, 1e33)
        return carry

    lax.fori_loop(0, rows // 64, body, 0)


def forward_tile(qkv, dist, pair, first_head, at, store):
    q, k, v = qkv[0, pair, at, :], qkv[1, pair], qkv[2, pair]
    gap = dist[at, :]
    outs = []
    for i in range(2):
        head = (first_head + 2 * pair + i + 1).astype(F32)
        slope = jnp.exp2(jnp.full((1, 1), -8.0 / HEADS, F32) * head) * LOG2E
        x = nt(own_half(q, i), k) * LOG2E - gap * slope
        e = jnp.exp2(x - jnp.max(x, 1, keepdims=True))
        p = (e * (1.0 / jnp.sum(e, 1, keepdims=True))).astype(BF16)
        store(i, p)
        outs.append(nn(p, v))
    return merge_halves(*outs).astype(BF16)


def backward_tile(qkv, do, do_t, q_t, pair, probs, dk, dv):
    k, v = qkv[1, pair], qkv[2, pair]
    dq = []
    for i in range(2):
        p = probs(i)
        rows = pl.ds(i * HEAD_DIM, HEAD_DIM)
        t = p.astype(F32) * nt(own_half(do, i), v)
        ds = (t - p.astype(F32) * jnp.sum(t, 1, keepdims=True)).astype(BF16)
        dq.append(nn(ds, k))
        dv[rows, :] += nn(do_t[rows, :], p)
        dk[rows, :] += nn(q_t[rows, :], ds)
    return (merge_halves(*dq) * HEAD_DIM**-0.5).astype(BF16)


def forward_kernel(
    nb, nz, lengths, x, skip_x, gain_one, shift_one, gain_two, shift_two,
    skip_w, query_w, key_w, value_w, out_w, up_w, down_w,
    mixed_out, normed_out, norms_out, skip_out, qkvw_out, out_out, ff0_out, ff1_out, ff2_out, ff3_w, qkv_out, probs, attended_out,
    skip, qkvw, joined, mixed, normed, everything, norms, gains, turned, ff_w, qkv, dist, pbuf, attended,
    load, ff_load, norm_send, norm_recv, swap_send, swap_recv, flush, psem, att_send, att_recv, *rest,
):
    place = Place(nb, nz)
    z, group, k, half = place.z, place.group, place.k, place.half
    frames = x.shape[0] // 2
    width = x.shape[1]
    keys = nz * frames
    c = norms.shape[1]
    cw = up_w.shape[1] // 4
    pz = c // 128
    pairs = 2 * pz
    place.greet()

    jobs = [rest[3 * i : 3 * i + 3] for i in range(7)]
    rs = skip_w.shape[0] // 2
    skips = [Gather(place, skip_w.at[pl.ds(h * rs, rs)], skip, jobs[h], h=h, of=2) for h in (0, 1)]
    qkv_job = Gather(place, [query_w, key_w, value_w], qkvw, jobs[2], True)
    out_job = Gather(place, turned, out_out, jobs[3])
    ff = [Gather(place, ff_w.at[i], o, jobs[4 + i]) for i, o in enumerate((ff0_out, ff1_out, ff2_out))]
    last = nz - 1

    def go(job, *stages):
        for t in stages:
            if t < job.stages:
                job.stage(t)

    def both(*stages):
        for t in stages:
            go(skips[0], t)
            go(skips[1], t)

    both(0)
    loads = [
        pltpu.make_async_copy(x, joined.at[:, pl.ds(0, width)], load.at[0]),
        pltpu.make_async_copy(skip_x, joined.at[:, pl.ds(width, width)], load.at[1]),
    ]
    up_loads = [
        pltpu.make_async_copy(up_w.at[:, pl.ds(i * cw, cw)], ff_w.at[i, :, pl.ds(0, cw)], ff_load.at[i]) for i in range(4)
    ]
    for one in loads + up_loads:
        one.start()
    norms[...] = jnp.zeros_like(norms)
    for i, ref in enumerate((gain_one, shift_one, gain_two, shift_two)):
        norms[i : i + 1, :] = ref[...].astype(F32).reshape(1, c)
    own_norms = pltpu.make_async_copy(norms, gains.at[:, part(z, c)], load.at[2])
    own_norms.start()
    norm_copy = lambda r: remote(
        norms, gains.at[:, part(z, c)], norm_send.at[r - 1], norm_recv.at[r - 1], (place.b, lax.rem(z + r, nz))
    )
    for r in range(1, nz):
        place.start(norm_copy, r)
    turned[...] = out_w[...].T
    down_t = down_w[...].T
    for i in range(4):
        ff_w[i, :, cw:] = down_t[:, i * cw : (i + 1) * cw]
    both(*range(1, last))
    go(qkv_job, 0)
    both(last)
    for one in up_loads:
        one.wait()
    go(ff[0], 0)
    both(last + 1)
    go(skips[0], last + 2)
    go(ff[0], *range(1, last))
    go(ff[1], 0)
    go(skips[1], last + 2)
    go(ff[1], *range(1, last - 1))
    go(qkv_job, 1)
    go(ff[0], last)
    both(*range(last + 3, skips[0].stages))
    go(ff[1], last - 1)
    flushes = []

    def out_copy(src, dst):
        copy = pltpu.make_async_copy(src, dst, flush.at[len(flushes)])
        flushes.append(copy)
        copy.start()

    out_copy(skip, skip_out)
    out_copy(ff_w.at[3], ff3_w)
    own_norms.wait()
    for one in loads:
        one.wait()
    for r in range(1, nz):
        norm_copy(r).wait_recv()
    out_copy(gains, norms_out)

    def across():
        return remote(
            normed.at[1 - group], everything.at[part(z, frames)], swap_send.at[0], swap_recv.at[0],
            (place.b, place.partner),
        )

    for turn in (0, 1):
        item = 1 - group if turn == 0 else group
        rows = part(item, frames)
        mixed[rows, :] = nn(joined[rows, :], skip[...])
        gain, shift = gains[0:1, :], gains[1:2, :]

        def body(i, carry):
            at = part(i, 32)
            at2 = pl.ds(pl.multiple_of(item * frames + i * 32, 32), 32)
            n, _ = normalise(mixed[at2, :])
            normed[item, at, :] = (n * gain + shift).astype(BF16)
            return carry

        lax.fori_loop(0, frames // 32, body, 0)
        if turn == 0:
            place.start(across)
            go(qkv_job, 2)
        else:
            own = pltpu.make_async_copy(normed.at[item], everything.at[part(z, frames)], load.at[0])
            own.start()

    def mate_copy(src, block, r, sem):
        return remote(
            src, everything.at[part(block, frames)], swap_send.at[sem], swap_recv.at[sem], (place.b, place.mate(r))
        )

    for r in range(1, half):
        place.start(mate_copy, normed.at[group], z, r, r)
    out_copy(mixed, mixed_out)
    go(ff[0], last + 1)
    go(ff[1], last)
    distances(dist, lengths[group])
    go(qkv_job, 3)
    go(ff[0], last + 2)
    across().wait_recv()
    for r in range(1, half):
        block = everything.at[part(place.partner, frames)]
        place.start(mate_copy, block, place.partner, r, half - 1 + r)
    go(ff[1], last + 1)
    go(qkv_job, *range(4, qkv_job.stages))
    out_copy(qkvw, qkvw_out)
    own.wait()
    for r in range(1, half):
        mate_copy(normed.at[group], z, r, r).wait_recv()
        mate_copy(normed.at[group], z, r, half - 1 + r).wait_recv()
    out_copy(everything, normed_out)
    go(ff[2], 0)
    go(out_job, 0)

    project(everything, qkvw, qkv, pz)
    out_copy(qkv, qkv_out)
    first_head = k * 2 * pairs
    blocks = keys // QUERIES
    total = pairs * blocks

    def probs_copy(slot, pair, at):
        return pltpu.make_async_copy(pbuf.at[slot], probs.at[pair, :, at], psem.at[slot])

    def att_copy(pair, r):
        owner = lax.rem(z + r, nz)
        slot = pair * (nz - 1) + r - 1
        return remote(
            attended.at[pair, part(owner, frames)],
            attended_out.at[part(group, frames), part(k * pairs + pair, 128)],
            att_send.at[slot], att_recv.at[slot], (place.b, owner),
        )

    def att_own(pair):
        return pltpu.make_async_copy(
            attended.at[pair, part(z, frames)],
            attended_out.at[part(group, frames), part(k * pairs + pair, 128)],
            flush.at[7 + pair],
        )

    hooks = {}

    placed = {}

    def hook(it, *steps):
        at = min(it, total - 1)
        for step in steps:
            if not callable(step):
                at = max(at, placed.get(id(step[0]), 0))
                placed[id(step[0])] = at
            hooks.setdefault(at, []).append(step)

    rest_of = lambda job, t: [(job, s) for s in range(t, job.stages)]
    for t in range(1, last):
        hook(t - 1, (ff[2], t), (out_job, t))
    hook(2, (ff[1], last + 2), (out_job, last), (ff[2], last), *rest_of(ff[0], last + 3))
    hook(4, (out_job, last + 1), (ff[2], last + 1))
    hook(5, *rest_of(ff[1], last + 3))
    hook(7, (out_job, last + 2), (ff[2], last + 2))

    def body(it, carry):
        pair, q = lax.div(it, blocks), lax.rem(it, blocks)
        at, slot = part(q, QUERIES), lax.rem(it, 2)
        for when, steps in hooks.items():
            pl.when(it == when)(lambda steps=steps: perform(steps))

        @pl.when(it >= 2)
        def _():
            probs_copy(slot, pair, at).wait()

        def store(i, p):
            pbuf[slot, i] = p

        attended[pair, at, :] = forward_tile(qkv, dist, pair, first_head, at, store)
        probs_copy(slot, pair, at).start()

        @pl.when(q == blocks - 1)
        def _():
            for r in range(1, nz):
                att_copy(pair, r).start()

        return carry

    lax.fori_loop(0, total, body, 0)
    for pair in range(pairs):
        att_own(pair).start()
    go(ff[2], *range(last + 3, ff[2].stages))
    go(out_job, *range(last + 3, out_job.stages))
    for pair in range(pairs):
        for r in range(1, nz):
            att_copy(pair, r).wait()
    for pair in range(pairs):
        att_own(pair).wait()
    for slot in range(min(2, total)):
        probs_copy(slot, 0, pl.ds(0, QUERIES)).wait()
    for copy in flushes:
        copy.wait()
    place.drain()


def forward(nb, nz, lengths, x, skip_x, norms, skip_w, qkv_w, out_w, up_w, down_w):
    rows, width = x.shape
    frames = rows // 2
    keys = nz * frames
    c = width // nz
    pairs = 2 * c // 128
    r = up_w.shape[0]
    chunk = up_w.shape[1] // 2
    S, V, D = jax.ShapeDtypeStruct, pltpu.VMEM, pltpu.SemaphoreType.DMA
    out_shape = [
        S((rows, width), F32),
        S((keys, width), BF16),
        S((8, width), F32),
        S((nb * skip_w.shape[0], width), BF16),
        S((nb * r, 6 * c), BF16),
        S((nb * r, width), BF16),
        *[S((nb * r, nz * chunk), BF16)] * 3,
        S((r, chunk), BF16),
        S((3, pairs, keys, 128), BF16),
        S((pairs, 2, keys, keys), BF16),
        S((rows, width), BF16),
    ]
    scratch = [
        V((nb * skip_w.shape[0], width), BF16),
        V((nb * r, 6 * c), BF16),
        V((rows, 2 * width), BF16),
        V((rows, width), F32),
        V((2, frames, width), BF16),
        V((keys, width), BF16),
        V((8, c), F32),
        V((8, width), F32),
        V((r, c), BF16),
        V((4, r, chunk), BF16),
        V((3, pairs, keys, 128), BF16),
        V((keys, keys), F32),
        V((2, 2, QUERIES, keys), BF16),
        V((pairs, keys, 128), BF16),
    ]
    scratch += [D((3,)), D((4,)), D((nz - 1,)), D((nz - 1,)), D((nz - 1,)), D((nz - 1,)), D((7 + pairs,)), D((2,))]
    scratch += [D((pairs * (nz - 1),)), D((pairs * (nz - 1),))]
    for _ in range(7):
        scratch += Gather.scratch(nb, nz)
    return pl.pallas_call(
        functools.partial(forward_kernel, nb, nz),
        out_shape=out_shape,
        in_specs=[pl.BlockSpec(memory_space=pltpu.SMEM), ANY, ANY, *[WHOLE] * 4, *[ANY] * 4, WHOLE, ANY, WHOLE],
        out_specs=[ANY] * len(out_shape),
        scratch_shapes=scratch,
        compiler_params=pltpu.CompilerParams(
            collective_id=0, has_side_effects=True, vmem_limit_bytes=VMEM_LIMIT
        ),
    )(lengths, x, skip_x, *norms, skip_w, *qkv_w, out_w, up_w, down_w)


def ffn_kernel(
    nb, nz, mixed_in, attended_in, out_in, norms, cot_in, ff0, ff1, ff2, ff_w,
    output_out, middle_out, att_out, out_grad_out, part0, grad1, grad2, grad3, sums, ff3,
    middle, attended, out_t, cot, weights, grads, ffn_in, ffn_in_t, cot_t, acc, gacc, low, out_grad,
    load, wload, flush, *rest,
):
    place = Place(nb, nz)
    rows, d = mixed_in.shape
    r = grads.shape[2]
    cw = ff_w.shape[1] // 2
    subs = nz // 2
    total = 4 * subs
    gather = Gather(place, ff_w, ff3, rest[:3])
    job = Scatter(place, grads.at[0], None, rest[3:], sums=False, line=False)
    go = lambda job, *stages: [job.stage(t) for t in stages if t < job.stages]
    last = nz - 1
    loads = [
        pltpu.make_async_copy(src, dst, load.at[i])
        for i, (src, dst) in enumerate(
            ((attended_in, attended), (out_in, out_t), (mixed_in, middle), (cot_in, cot))
        )
    ]
    weight_load = lambda i: pltpu.make_async_copy((ff0, ff1, ff2, ff3)[i], weights.at[i % 2], wload.at[i % 2])
    for one in loads:
        one.start()
    weight_load(0).start()
    weight_load(1).start()
    place.greet()
    go(gather, 0)
    gain, shift = norms[2:3, :], norms[3:4, :]
    for one in loads[:3]:
        one.wait()
    acc[...] = nt(attended[...], out_t[...])
    go(gather, 1)

    def enter(at):
        v = middle[at, :] + acc[at, :]
        middle[at, :] = v
        n, _ = normalise(v)
        ffn_in[at, :] = (n * gain + shift).astype(BF16)
        acc[at, :] = v
        gacc[at, :] = jnp.zeros_like(v)

    rowwise(rows, 32, enter)
    ffn_in_t[...] = ffn_in[...].T
    loads[3].wait()
    cot_t[...] = cot[...].T
    go(gather, *range(2, last))
    weight_load(0).wait()

    hooks = {}

    placed = {}

    def hook(it, *steps):
        at = min(it, total - 1)
        for step in steps:
            if not callable(step):
                at = max(at, placed.get(id(step[0]), 0))
                placed[id(step[0])] = at
            hooks.setdefault(at, []).append(step)

    rest_of = lambda job, t: [(job, s) for s in range(t, job.stages)]
    hook(total // 8, (gather, last))
    hook(total * 2 // 8, lambda: weight_load(1).wait(), lambda: weight_load(2).start(), (job, 0))
    hook(total * 3 // 8, (gather, last + 1))
    hook(total * 4 // 8, lambda: weight_load(2).wait(), lambda: flush_copy(3).start(), (job, 1))
    hook(
        total * 6 // 8,
        (gather, last + 2),
        *rest_of(gather, last + 3),
        lambda: weight_load(3).start(),
        lambda: flush_copy(0).start(),
        lambda: weight_load(3).wait(),
    )
    hook(total * 7 // 8, (job, 2))

    def flush_copy(i):
        pairs = (
            (grads.at[2], grad2), (grads.at[3], grad3), (grads.at[0, 0], part0), (grads.at[1], grad1),
            (low, output_out), (gacc, middle_out), (attended, att_out), (out_grad, out_grad_out),
        )
        return pltpu.make_async_copy(*pairs[i], flush.at[i])

    def body(it, carry):
        for when, steps in hooks.items():
            pl.when(it == when)(lambda steps=steps: perform(steps))
        chunk, sub = lax.div(it, subs), lax.rem(it, subs)
        slot = lax.rem(chunk, 2)
        first = [(2 * sub + i) * 2 for i in (0, 1)]
        up = jnp.concatenate([weights[slot, :, part(f, cw)] for f in first], 1)
        dn = jnp.concatenate([weights[slot, :, part(f + 1, cw)] for f in first], 1)
        hidden = nn(ffn_in[...], up)
        active_grad = nn(cot[...], dn)
        cdf = 0.5 * (1.0 + lax.erf(hidden * 0.7071067811865476))
        active = (hidden * cdf).astype(BF16)
        density = jnp.exp2(hidden * hidden * (-0.5 * LOG2E)) * 0.3989422804014327
        hidden_grad = (active_grad * (cdf + hidden * density)).astype(BF16)
        acc[...] += nt(active, dn)
        gacc[...] += nt(hidden_grad, up)
        up_grad = nn(ffn_in_t[...], hidden_grad).astype(BF16)
        dn_grad = nn(cot_t[...], active).astype(BF16)
        for j in range(nb):
            m = flip(place.b, j)
            block = slice(j * r, (j + 1) * r)
            for i in (0, 1):
                cols = slice(i * cw, (i + 1) * cw)
                grads[chunk, m, :, part(first[i], cw)] = up_grad[block, cols]
                grads[chunk, m, :, part(first[i] + 1, cw)] = dn_grad[block, cols]
        return carry

    lax.fori_loop(0, total, body, 0)
    flush_copy(1).start()
    sums[...] = jnp.zeros_like(sums)

    def leave(at):
        low[at, :] = acc[at, :].astype(BF16)
        back = norm_back(gacc[at, :], middle[at, :], gain, sums.at[0], sums.at[1])
        grad = cot[at, :].astype(F32) + back
        gacc[at, :] = grad
        ffn_in[at, :] = grad.astype(BF16)

    rowwise(rows, 32, leave)
    flush_copy(4).start()
    flush_copy(5).start()
    grad_t = ffn_in[...].T
    for j in range(nb):
        out_grad[flip(place.b, j)] = nn(grad_t[j * r : (j + 1) * r, :], attended[...]).astype(BF16)
    flush_copy(7).start()
    attended[...] = nn(ffn_in[...], out_t[...]).astype(BF16)
    flush_copy(6).start()
    go(job, *range(3, job.stages))
    flush_copy(2).start()
    for i in range(8):
        flush_copy(i).wait()
    place.drain()


def ffn(nb, nz, mixed, attended, out_t, norms, cot, ff0, ff1, ff2, ff_w):
    rows, d = mixed.shape
    r, width = ff_w.shape
    wide = nz * width
    V, S, D = pltpu.VMEM, jax.ShapeDtypeStruct, pltpu.SemaphoreType.DMA
    scratch = [
        V((rows, d), F32),
        V((rows, d), BF16),
        V((d, d), BF16),
        V((rows, d), BF16),
        V((2, d, wide), BF16),
        V((4, nb, r, wide), BF16),
        V((rows, d), BF16),
        V((d, rows), BF16),
        V((d, rows), BF16),
        V((rows, d), F32),
        V((rows, d), F32),
        V((rows, d), BF16),
        V((nb, r, d), BF16),
        D((4,)), D((2,)), D((8,)),
    ]
    scratch += Gather.scratch(nb, nz)
    scratch += Scatter.scratch(nb, nz, r, wide, sums=False, line=False)
    return pl.pallas_call(
        functools.partial(ffn_kernel, nb, nz),
        out_shape=[
            S((rows, d), BF16),
            S((rows, d), F32),
            S((rows, d), BF16),
            S((nb, r, d), BF16),
            S((r, wide), BF16),
            *[S((nb, r, wide), BF16)] * 3,
            S((2, 8, d), F32),
            S((d, wide), BF16),
        ],
        in_specs=[ANY] * 3 + [WHOLE] + [ANY] * 5,
        out_specs=[ANY] * 8 + [WHOLE, ANY],
        scratch_shapes=scratch,
        compiler_params=pltpu.CompilerParams(
            collective_id=3, has_side_effects=True, vmem_limit_bytes=VMEM_LIMIT
        ),
    )(mixed, attended, out_t, norms, cot, ff0, ff1, ff2, ff_w)


def attention_kernel(
    nb, nz, att_grad, qkv_in, probs, part0, grad1, grad2,
    dqkv_out, ff_share, part2,
    dqkv, qkv, dout, pbuf, dk, dv, q_t, do_t, load, psem, att_send, att_recv, *rest,
):
    place = Place(nb, nz)
    z, group, k = place.z, place.group, place.k
    pairs, keys = qkv.shape[1], qkv.shape[2]
    frames = keys // nz
    wide = pairs * 128
    pz = pairs // 2
    qkv_load = pltpu.make_async_copy(qkv_in, qkv, load.at[1])
    qkv_load.start()
    place.greet()

    def att_copy(r, pair):
        owner = lax.rem(z + r, nz)
        item, member = lax.div(owner, place.half), lax.rem(owner, place.half)
        slot = pair * (nz - 1) + r - 1
        return remote(
            att_grad.at[part(item, frames), part(member * pairs + pair, 128)],
            dout.at[part(z, frames), part(pair, 128)],
            att_send.at[slot], att_recv.at[slot], (place.b, owner),
        )

    def att_start(pair):
        for r in range(1, nz):
            att_copy(r, pair).start()

    for pair in range(min(2, pairs)):
        att_start(pair)
    own = pltpu.make_async_copy(att_grad.at[part(group, frames), part(k, wide)], dout.at[part(z, frames)], load.at[0])
    own.start()
    rest = list(rest)

    def job(full, share, **kind):
        count = 3 + sum(kind.get(key, True) and size for key, size in (("sums", 1), ("plane", 2), ("line", 1)))
        mine = [rest.pop(0) for _ in range(count)]
        return Scatter(place, full, share, mine, **kind)

    early = [job(None, ff_share.at[0], plane=False)]
    late = [job(grad1, ff_share.at[1]), job(grad2, None, line=False)]
    go = lambda job, *stages: [job.stage(t) for t in stages if t < job.stages]
    early_loads = [
        pltpu.make_async_copy(p, e.sums.at[0], load.at[2 + i]) for i, (p, e) in enumerate(zip((part0,), early))
    ]
    for one in early_loads:
        one.start()
    go(late[0], 0)
    go(late[1], 0)
    go(late[0], 1)
    own.wait()
    qkv_load.wait()

    blocks = keys // QUERIES
    total = pairs * blocks

    def probs_copy(it):
        slot = lax.rem(it, 2)
        pair, q = lax.div(it, blocks), lax.rem(it, blocks)
        return pltpu.make_async_copy(probs.at[pair, :, part(q, QUERIES)], pbuf.at[slot], psem.at[slot])

    probs_copy(0).start()
    hooks = {}

    placed = {}

    def hook(it, *steps):
        at = min(it, total - 1)
        for step in steps:
            if not callable(step):
                at = max(at, placed.get(id(step[0]), 0))
                placed[id(step[0])] = at
            hooks.setdefault(at, []).append(step)

    zs = place.nz - 1
    rest_of = lambda job, t: [(job, s) for s in range(t, job.stages)]
    hook(0, *[lambda one=one: one.wait() for one in early_loads], (early[0], 0))
    hook(total * 2 // 16, (early[0], 1))
    hook(total * 4 // 16, (late[0], 2), *[(early[0], t) for t in range(2, zs)])
    hook(total * 5 // 16, (late[1], 1))
    hook(total * 6 // 16, (early[0], zs))
    hook(total * 8 // 16, (late[0], 3))
    hook(total * 10 // 16, (late[0], 4))
    hook(total * 11 // 16, (late[1], 2))
    hook(total * 12 // 16, (late[0], 5))

    def body(it, carry):
        pair, q = lax.div(it, blocks), lax.rem(it, blocks)
        at, slot = part(q, QUERIES), lax.rem(it, 2)
        for when, steps in hooks.items():
            pl.when(it == when)(lambda steps=steps: perform(steps))

        @pl.when(it + 1 < total)
        def _():
            probs_copy(it + 1).start()

        probs_copy(it).wait()

        @pl.when(q == 0)
        def _():
            for r in range(1, nz):
                att_copy(r, pair).wait_recv()
            pl.when(pair + 2 < pairs)(lambda: att_start(pair + 2))
            dk[...] = jnp.zeros_like(dk)
            dv[...] = jnp.zeros_like(dv)

        do = dout[at, part(pair, 128)]
        q_t[...] = qkv[0, pair, at, :].T
        do_t[...] = do.T
        block = lax.div(pair, pz)
        column = lambda t: part((block * 3 + t) * pz + lax.rem(pair, pz), 128)
        dqkv[at, column(0)] = backward_tile(qkv, do, do_t, q_t, pair, lambda i: pbuf[slot, i], dk, dv)

        @pl.when(q == blocks - 1)
        def _():
            dqkv[:, column(1)] = dk[...].T.astype(BF16)
            dqkv[:, column(2)] = dv[...].T.astype(BF16)

        return carry

    lax.fori_loop(0, total, body, 0)
    dqkv_copy = pltpu.make_async_copy(dqkv, dqkv_out, load.at[1])
    dqkv_copy.start()
    go(late[0], *range(6, late[0].stages))
    go(late[1], *range(3, late[1].stages))
    part_copy = pltpu.make_async_copy(late[1].sums.at[0], part2, load.at[0])
    part_copy.start()
    for pair in range(pairs):
        for r in range(1, nz):
            att_copy(r, pair).wait_send()
    part_copy.wait()
    dqkv_copy.wait()
    place.drain()


def attention_back(nb, nz, att_grad, qkv, probs, part0, grad1, grad2):
    _, pairs, keys, _ = qkv.shape
    S, V, D = jax.ShapeDtypeStruct, pltpu.VMEM, pltpu.SemaphoreType.DMA
    _, r, wide = grad2.shape
    scratch = [
        V((keys, 3 * pairs * 128), BF16),
        V((3, pairs, keys, 128), BF16),
        V((keys, pairs * 128), BF16),
        V((2, 2, QUERIES, keys), BF16),
        V((128, keys), F32),
        V((128, keys), F32),
        V((128, QUERIES), BF16),
        V((128, QUERIES), BF16),
        D((4,)), D((2,)), D((pairs * (nz - 1),)), D((pairs * (nz - 1),)),
    ]
    scratch += Scatter.scratch(nb, nz, r, wide, plane=False)
    scratch += Scatter.scratch(nb, nz, r, wide)
    scratch += Scatter.scratch(nb, nz, r, wide, line=False)
    return pl.pallas_call(
        functools.partial(attention_kernel, nb, nz),
        out_shape=[
            S((keys, 3 * pairs * 128), BF16),
            S((2, r, wide // nz), F32),
            S((r, wide), BF16),
        ],
        in_specs=[ANY] * 6,
        out_specs=[ANY, WHOLE, ANY],
        scratch_shapes=scratch,
        compiler_params=pltpu.CompilerParams(
            collective_id=1, has_side_effects=True, vmem_limit_bytes=VMEM_LIMIT
        ),
    )(att_grad, qkv, probs, part0, grad1, grad2)


def first_kernel(
    nb, nz, dqkv_in, everything_in, qkvw_in, x, skip_x, skip_w, mixed_in, middle_in, norms, second_sums, ff_early, part2, grad3, out_grad,
    input_out, skip_out, query_out, key_out, value_out, skip_share, norm_share, up_out, down_out, out_out,
    input_grad, skip_grad, qkv_share, ff_share, out_share,
    dqkv, everything, qkvw, mixed, middle_grad,
    qkv_grad, skip_w_grad, spare, joined, joined_t, mixed_low, ahead, mine, from_mate, to_partner, from_partner,
    sums, packed, norm_in, norm_line, load, swap_send, swap_recv, norm_send, norm_recv, flush, *rest,
):
    place = Place(nb, nz)
    z, group, k, half = place.z, place.group, place.k, place.half
    frames = x.shape[0] // 2
    width = x.shape[1]
    loads = [
        pltpu.make_async_copy(src, dst, load.at[i])
        for i, (src, dst) in enumerate(
            (
                (dqkv_in, dqkv),
                (qkvw_in, qkvw),
                (everything_in, everything),
                (mixed_in, mixed),
                (middle_in, middle_grad),
                (x, joined.at[:, pl.ds(0, width)]),
                (skip_x, joined.at[:, pl.ds(width, width)]),
            )
        )
    ]
    rest = list(rest)

    def job(full, share, paired=False, **kind):
        count = 3 + sum(kind.get(key, True) and size for key, size in (("sums", 1), ("plane", 2), ("line", 1)))
        mine = [rest.pop(0) for _ in range(count)]
        return Scatter(place, full, share, mine, paired, **kind)

    for one in loads:
        one.start()
    place.greet()
    line_job = job(None, ff_share.at[0], plane=False)
    ff_job = job(grad3, ff_share.at[1])
    out_job = job(out_grad, out_share)
    qkv_job = job(qkv_grad, qkv_share, True, sums=False)
    rs = skip_w_grad.shape[2]
    skips = [job(skip_w_grad.at[h], skip_share.at[pl.ds(h * rs, rs)], sums=False) for h in (0, 1)]
    loads.append(pltpu.make_async_copy(part2, line_job.sums.at[0], load.at[7]))
    loads[7].start()

    def go(job, *stages):
        for t in stages:
            if t < job.stages:
                job.stage(t)

    go(ff_job, 0)
    go(out_job, 0)
    for one in loads[:2]:
        one.wait()

    def mate_copy(r, t):
        slot = (r - 1) * 2 + t
        return remote(
            ahead.at[slot], from_mate.at[slot], swap_send.at[slot], swap_recv.at[slot], (place.b, place.mate(r))
        )

    for r in range(1, half):
        for s in (0, 1):
            block = lax.rem(k + r, half) + (1 - group if s == 0 else group) * half
            ahead[(r - 1) * 2 + s] = nt(dqkv[part(block, frames), :], qkvw[...]).astype(BF16)
            if s == 0:
                place.start(mate_copy, r, 0)
    for s in (0, 1):
        block = k + (1 - group if s == 0 else group) * half
        mine[s] = nt(dqkv[part(block, frames), :], qkvw[...])
    loads[2].wait()
    turned = everything[...].T
    rq = qkv_grad.shape[1]
    for j in range(nb):
        qkv_grad[flip(place.b, j)] = nn(turned[j * rq : (j + 1) * rq, :], dqkv[...]).astype(BF16)
    weights = [everything.at[pl.ds(0, width)], qkvw.at[:, pl.ds(0, width)] if qkvw.shape[1] >= width else spare]
    for i, ref in enumerate(weights):
        loads.append(pltpu.make_async_copy(skip_w.at[pl.ds(i * width, width)], ref, load.at[8 + i]))
        loads[-1].start()
    go(ff_job, 1)
    go(qkv_job, 0)
    go(out_job, 1)

    def add_mates(s):
        for r in range(1, half):
            mate_copy(r, s).wait_recv()
            slot = (r - 1) * 2 + s

            def body(at):
                mine[s, at] = mine[s, at] + from_mate[slot, at].astype(F32)

            rowwise(frames, 16, body)

    add_mates(0)
    sem = 2 * (half - 1)
    across = lambda: remote(to_partner, from_partner, swap_send.at[sem], swap_recv.at[sem], (place.b, place.partner))

    def narrow(at):
        to_partner[at] = mine[0, at].astype(BF16)

    rowwise(frames, 16, narrow)
    place.start(across)
    for r in range(1, half):
        place.start(mate_copy, r, 1)
    for one in loads[3:8]:
        one.wait()
    joined_t[...] = joined[...].T
    go(qkv_job, 1)
    go(ff_job, 2)
    go(out_job, 2)

    sums[...] = jnp.zeros_like(sums)
    gain = norms[0:1, :]

    def back(item, grad):
        def body(i, carry):
            at = part(i, 32)
            to = pl.ds(pl.multiple_of(item * frames + i * 32, 32), 32)
            part_grad = norm_back(grad(at), mixed[to, :], gain, sums.at[0], sums.at[1])
            mixed_low[to, :] = (middle_grad[to, :] + part_grad).astype(BF16)
            return carry

        lax.fori_loop(0, frames // 32, body, 0)

    add_mates(1)
    back(group, lambda at: mine[1, at])
    go(qkv_job, 2)
    go(ff_job, 3)
    across().wait_recv()
    back(1 - group, lambda at: from_partner[at].astype(F32))
    for h in (0, 1):
        for j in range(nb):
            block = slice((2 * j + h) * rs, (2 * j + h + 1) * rs)
            skip_w_grad[h, flip(place.b, j)] = nn(joined_t[block, :], mixed_low[...]).astype(BF16)
        go(skips[h], 0)

    total = lambda a: jnp.sum(a, 0, keepdims=True)
    for i, v in enumerate((sums[0], sums[1], second_sums[0], second_sums[1])):
        packed[i : i + 1, :] = total(v)
    packed[4:8, :] = jnp.zeros_like(packed[4:8, :])
    bits = [0] + place.rest
    norm_copy = lambda i: remote(
        packed, norm_in.at[i], norm_send.at[i], norm_recv.at[i], place.at(1 << bits[i])
    )
    c = norm_share.shape[1]
    line_copy = lambda r: remote(
        packed.at[:, part(lax.rem(z + r, nz), c)], norm_line.at[r - 1],
        norm_send.at[len(bits) + r - 1], norm_recv.at[len(bits) + r - 1], (place.b, lax.rem(z + r, nz)),
    )

    def norm_step(i):
        if i > 0:
            norm_copy(i - 1).wait()
            packed[...] = packed[...] + norm_in[i - 1]
        if i < len(bits):
            norm_copy(i).start()
        else:
            for r in range(1, nz):
                line_copy(r).start()

    norm_step(0)
    go(out_job, 3)
    go(qkv_job, 3)
    go(line_job, 0)
    go(skips[0], 1)
    go(skips[1], 1)
    norm_step(1)
    go(ff_job, 4)
    go(out_job, 4)
    go(line_job, 1)
    for one in loads[8:]:
        one.wait()
    input_grad[...] = nt(mixed_low[...], weights[0][...])
    flushes = [pltpu.make_async_copy(input_grad, input_out, flush.at[0])]
    flushes[0].start()
    go(skips[0], 2)
    norm_step(2)
    go(ff_job, 5)
    go(out_job, 5)
    go(line_job, 2)
    go(qkv_job, *range(4, qkv_job.stages))
    skip_grad[...] = nt(mixed_low[...], weights[1][...])
    flushes.append(pltpu.make_async_copy(skip_grad, skip_out, flush.at[1]))
    flushes[1].start()
    go(skips[1], 2)
    go(skips[0], 3)
    norm_step(3)
    go(ff_job, *range(6, ff_job.stages))
    go(out_job, *range(6, out_job.stages))
    go(skips[1], 3)
    go(line_job, *range(3, line_job.stages))
    for i in range(4, len(bits) + 1):
        norm_step(i)
    go(skips[0], 4)
    go(skips[1], 4)
    for i, ref in enumerate((query_out, key_out, value_out)):
        ref[...] = qkv_share[:, i * c : (i + 1) * c]
    out_out[...] = out_share[...].T
    cw = ff_share.shape[2] // 2
    for i in range(4):
        source = ff_early.at[i] if i < 2 else ff_share.at[i - 2]
        up_out[:, i * cw : (i + 1) * cw] = source[:, :cw]
        down_out[i * cw : (i + 1) * cw, :] = source[:, cw:].T
    for t in range(5, skips[0].stages):
        go(skips[0], t)
        go(skips[1], t)
    for one in flushes:
        one.wait()
    value = packed[:, part(z, c)]
    for r in range(1, nz):
        line_copy(r).wait()
        value = value + norm_line[r - 1]
    norm_share[...] = value
    place.drain()


def first_back(nb, nz, dqkv, everything, qkvw, x, skip_x, skip_w, mixed, middle_grad, norms, second_sums, ff_early, part2, grad3, out_grad):
    rows, width = x.shape
    frames = rows // 2
    half = nz // 2
    c = width // nz
    S, V, D = jax.ShapeDtypeStruct, pltpu.VMEM, pltpu.SemaphoreType.DMA
    qkv_wide = qkvw.shape[1]
    bits = nb.bit_length() - 1
    swaps = 2 * (half - 1)
    r, wide = ff_early.shape[1:]
    scratch = [
        V((rows, width), F32),
        V((rows, width), F32),
        V((r, 3 * c), F32),
        V((2, r, wide), F32),
        V((r, c), F32),
        V(dqkv.shape, BF16),
        V(everything.shape, BF16),
        V(qkvw.shape, BF16),
        V((rows, width), F32),
        V((rows, width), F32),
        V((nb, qkvw.shape[0] // nb, qkv_wide), BF16),
        V((2, nb, skip_w.shape[0] // nb // 2, width), BF16),
        V((width, width) if qkv_wide < width else (16, 128), BF16),
        V((rows, 2 * width), BF16),
        V((2 * width, rows), BF16),
        V((rows, width), BF16),
        V((max(swaps, 1), frames, width), BF16),
        V((2, frames, width), F32),
        V((max(swaps, 1), frames, width), BF16),
        V((frames, width), BF16),
        V((frames, width), BF16),
        V((2, 8, width), F32),
        V((8, width), F32),
        V((bits, 8, width), F32),
        V((nz - 1, 8, c), F32),
        D((10,)), D((swaps + 1,)), D((swaps + 1,)), D((bits + nz - 1,)), D((bits + nz - 1,)), D((2,)),
    ]
    scratch += Scatter.scratch(nb, nz, grad3.shape[1], grad3.shape[2], plane=False)
    scratch += Scatter.scratch(nb, nz, grad3.shape[1], grad3.shape[2])
    scratch += Scatter.scratch(nb, nz, out_grad.shape[1], out_grad.shape[2])
    scratch += Scatter.scratch(nb, nz, qkvw.shape[0] // nb, qkv_wide, True, sums=False)
    for _ in (0, 1):
        scratch += Scatter.scratch(nb, nz, skip_w.shape[0] // nb // 2, width, sums=False)
    return pl.pallas_call(
        functools.partial(first_kernel, nb, nz),
        out_shape=[
            S((rows, width), F32),
            S((rows, width), F32),
            *[S((r, c), F32)] * 3,
            S((skip_w.shape[0] // nb, c), F32),
            S((8, c), F32),
            S((r, 2 * wide), F32),
            S((2 * wide, r), F32),
            S((c, r), F32),
        ],
        in_specs=[ANY] * 8 + [WHOLE] * 3 + [ANY] * 3,
        out_specs=[ANY] * 2 + [WHOLE] * 8,
        scratch_shapes=scratch,
        compiler_params=pltpu.CompilerParams(
            collective_id=2, has_side_effects=True, vmem_limit_bytes=VMEM_LIMIT
        ),
    )(dqkv, everything, qkvw, x, skip_x, skip_w, mixed, middle_grad, norms, second_sums, ff_early, part2, grad3, out_grad)


def shards(
    inputs,
    skip_input,
    lengths,
    skip_weight,
    query_weight,
    key_weight,
    value_weight,
    out_weight,
    up_weight,
    down_weight,
    first_gain,
    first_shift,
    second_gain,
    second_shift,
    cotangent,
):
    nb, nz = lax.axis_size("batch"), lax.axis_size("seq")
    shape = inputs.shape
    flat = lambda a: a.reshape(shape[0] * shape[1], shape[2])
    x, skip_x, cot = flat(inputs), flat(skip_input), flat(cotangent)
    norms = (first_gain, first_shift, second_gain, second_shift)
    qkv_w = (query_weight, key_weight, value_weight)
    (mixed, everything, gains, skip_w, qkvw, out_t, ff0, ff1, ff2, ff3_w, qkv, probs, attended) = forward(
        nb, nz, lengths, x, skip_x, norms, skip_weight, qkv_w, out_weight, up_weight, down_weight
    )
    output, middle_grad, att_grad, out_grad, part0, grad1, grad2, grad3, second_sums, _ = ffn(
        nb, nz, mixed, attended, out_t, gains, cot, ff0, ff1, ff2, ff3_w
    )
    dqkv, ff_early, part2 = attention_back(nb, nz, att_grad, qkv, probs, part0, grad1, grad2)
    input_grad, skip_grad, query_share, key_share, value_share, skip_share, norm_share, up_share, down_share, out_share = (
        first_back(
            nb, nz, dqkv, everything, qkvw, x, skip_x, skip_w, mixed, middle_grad, gains, second_sums, ff_early, part2,
            grad3, out_grad,
        )
    )
    return (
        output.reshape(shape),
        input_grad.reshape(shape),
        skip_grad.reshape(shape),
        skip_share,
        query_share,
        key_share,
        value_share,
        out_share,
        up_share,
        down_share,
        norm_share[0],
        norm_share[1],
        norm_share[2],
        norm_share[3],
    )


def solution(mesh):
    rows = P("batch", "seq", None)
    weight, turned, norm = P("batch", "seq"), P("seq", "batch"), P("seq")
    return jax.shard_map(
        shards,
        mesh=mesh,
        in_specs=(rows, rows, P("batch"), *[weight] * 4, turned, weight, turned, *[norm] * 4, rows),
        out_specs=(rows, rows, rows, *[weight] * 4, turned, weight, turned, *[norm] * 4),
        check_vma=False,
    )
```
